256 devices in a mesh: frame: 8 (over y, core), slab: 32 (over z, x).
Axes of the slice: x: 4, y: 4, z: 8, core: 2. Of those that a mesh axis runs over, the one named last changes fastest.
Arguments:
- positions: float32 [16, 3, 8192], P('frame', None, 'slab'), may hold values from 0 to 6
- species: int32 [16, 8192], P('frame', 'slab'), may hold values from 0 to 1
- atom_count: int32 [16, 32], P('frame', 'slab'), may hold values from 192 to 256, as said below
- halo_index: int32 [16, 2, 4096], P('frame', None, 'slab'), may hold values from 0 to 255, as said below
- neighbours: int32 [16, 48, 8192], P('frame', None, 'slab'), may hold values from -1 to 511, as said below
- embedding: bfloat16 [2, 128], replicated, may hold values from -6 to 6
- w_msg: bfloat16 [2, 128, 128], replicated, may hold values from -0.5 to 0.5
- w_rad1: bfloat16 [2, 8, 64], replicated, may hold values from -2 to 2
- w_rad2: bfloat16 [2, 64, 256], replicated, may hold values from -0.75 to 0.75
- w_up: bfloat16 [2, 256, 128], replicated, may hold values from -0.375 to 0.375
- w_out: float32 [128], replicated, may hold values from -0.5 to 0.5
- e_shift: float32 [2], replicated, may hold values from 0.2 to 0.6
- u_reference: float32 [16], P('frame'), may hold values from -201000 to 1000
- inverse_temp: float32 [1], replicated, may hold values from 0.002 to 0.006
- q_vectors: float32 [3, 16], replicated, may hold values from -1.5 to 1.5
- s_target: float32 [16], replicated, may hold values from 0.2 to 1
Outputs:
- atom_energy: float32 [16, 8192], P('frame', 'slab')
- mean_structure: float32 [16], replicated
- grad_up: float32 [256, 128], replicated
- grad_out: float32 [128], replicated
The draws below stay inside these ranges and needn't reach their ends.
Inputs may be any that keep to these rules, and one draw needn't show every extreme that they name: `atom_count`: in every frame some slab holds 256 live atoms; the live atoms of a slab are its first slots. `halo_index`: each slab's blocks hold 128 indices of its own live atoms; indices may repeat. `neighbours`: an entry below 256 is another live atom of the same slab, 256 + h the h-th atom passed up from the slab below, 384 + h the h-th atom passed down from the slab above, -1 an empty slot. Each live atom has 24 to 48 entries, empty atom slots have none; entries may repeat.
All inputs are finite; a program needn't handle non-finite values.
Results may differ from the reference program's by a relative error of at most 0.0065.
Values may be sent and summed in bfloat16 or wider, within the bound.
No kernel may reach another device: no remote copies, remote signals or barrier semaphores. Data moves between devices by JAX's collectives and lax.ppermute only.
A program may use at most 128 MiB of HBM per device.

```python
import math
import jax
import jax.numpy as jnp
from jax import lax

C = 128
RH = 64
NB = 8
SP = 2
LAYERS = 2
NBR = 48
Q = 16
ATOMS_DEV = 256
HALO = 128
ATOMS = 8192
FRAMES = 16
N_SLAB = 32


def live_counts(key):
    key = jax.random.fold_in(key, 101)
    base_key, full_key = jax.random.split(key)
    slab_total = ATOMS // ATOMS_DEV
    base = jax.random.randint(base_key, (FRAMES, slab_total), 3 * ATOMS_DEV // 4, ATOMS_DEV + 1)
    fullest = jax.random.randint(full_key, (FRAMES, 1), 0, slab_total)
    slab_ids = jnp.arange(slab_total, dtype=jnp.int32)[None, :]
    return jnp.where(slab_ids == fullest, ATOMS_DEV, base).astype(jnp.int32)


def draw_atom_count(key, part):
    counts = live_counts(key)
    return counts


def draw_halo_index(key, part):
    counts = live_counts(key)
    key = jax.random.fold_in(key, 3)
    slab_total = ATOMS // ATOMS_DEV
    raw = jax.random.randint(key, (FRAMES, 2, slab_total, HALO), 0, ATOMS_DEV)
    limit = counts[:, None, :, None]
    picked = raw % limit
    first = jnp.arange(HALO, dtype=jnp.int32)[None, None, None, :] == 0
    picked = jnp.where(first, limit - 1, picked)
    return picked.reshape(FRAMES, 2, slab_total * HALO).astype(jnp.int32)


def draw_neighbours(key, part):
    counts = live_counts(key)
    key = jax.random.fold_in(key, 7)
    degree_key, pick_key = jax.random.split(key)
    slab_total = ATOMS // ATOMS_DEV
    degree = jax.random.randint(degree_key, (FRAMES, slab_total, 1, ATOMS_DEV), NBR // 2, NBR + 1)
    raw = jax.random.randint(pick_key, (FRAMES, slab_total, NBR, ATOMS_DEV), 0, ATOMS_DEV + 2 * HALO)
    limit = counts[:, :, None, None]
    picked = raw % (limit + 2 * HALO)
    mapped = jnp.where(picked < limit, picked, picked - limit + ATOMS_DEV)
    atom_ids = jnp.arange(ATOMS_DEV, dtype=jnp.int32)[None, None, None, :]
    mapped = jnp.where(mapped == atom_ids, (atom_ids + 1) % limit, mapped)
    slot_ids = jnp.arange(NBR, dtype=jnp.int32)[None, None, :, None]
    keeping = (slot_ids < degree) & (atom_ids < limit)
    result = jnp.where(keeping, mapped, -1)
    result = jnp.where((slot_ids == 0) & (atom_ids == 0), ATOMS_DEV + 2 * HALO - 1, result)
    return jnp.transpose(result, (0, 2, 1, 3)).reshape(FRAMES, NBR, ATOMS).astype(jnp.int32)


def draw_u_reference(key, part):
    key = jax.random.fold_in(key, 11)
    spread_key = jax.random.fold_in(key, 0)
    spread = jnp.clip(100.0 * jax.random.normal(spread_key, (FRAMES,), jnp.float32), -800.0, 800.0)
    return spread


def place_ends(values, own_key, smallest, top_value):
    longest = values.shape.index(max(values.shape))
    spots = []
    for shift in (0, 1):
        where = [jax.random.randint(jax.random.fold_in(own_key, axis), (), 0, length) for axis, length in enumerate(values.shape)]
        where[longest] = (where[longest] + shift) % values.shape[longest]
        spots.append(tuple(where))
    return values.at[spots[0]].set(smallest).at[spots[1]].set(top_value)


def levels(rng, extent, cuts, least, top_value):
    factor_of = 1.0
    for axis_at, parts in cuts:
        draws = jax.random.uniform(jax.random.fold_in(jax.random.fold_in(rng, 6), axis_at), (parts,), jnp.float32, least / len(cuts), top_value / len(cuts))
        factor_of = factor_of * jnp.repeat(jnp.exp(draws), extent[axis_at] // parts).reshape((-1,) + (1,) * (len(extent) - 1 - axis_at))
    return factor_of


def normal_values(stream_key, shape, scale, most, kind=jnp.bfloat16):
    drawn = scale * jax.random.normal(stream_key, shape, jnp.float32)
    return jnp.clip(drawn, min=-most, max=most).astype(kind)


def setup_inputs(seed: int = 0) -> dict:
    seeds = jax.random.split(jax.random.key(seed), 17)
    return {
        "positions": jnp.clip(6.0 * jax.random.uniform(seeds[0], (FRAMES, 3, ATOMS), jnp.float32) ** levels(seeds[0], (FRAMES, 3, ATOMS), ((0, 8), (2, 32)), -0.2, 0.2), 0.0, 6.0),
        "species": place_ends(jax.random.randint(seeds[1], (FRAMES, ATOMS), 0, SP), jax.random.fold_in(seeds[1], 1), 0, SP - 1).astype(jnp.int32),
        "atom_count": draw_atom_count(jax.random.fold_in(seeds[16], 71), 0),
        "halo_index": draw_halo_index(jax.random.fold_in(seeds[16], 71), 0),
        "neighbours": draw_neighbours(jax.random.fold_in(seeds[16], 71), 0),
        "embedding": normal_values(seeds[5], (SP, C), 1.0, 6.0),
        "w_msg": normal_values(seeds[6], (LAYERS, C, C), C ** -0.5, 0.5),
        "w_rad1": normal_values(seeds[7], (LAYERS, NB, RH), NB ** -0.5, 2.0),
        "w_rad2": normal_values(seeds[8], (LAYERS, RH, 2 * C), RH ** -0.5, 0.75),
        "w_up": normal_values(seeds[9], (LAYERS, 2 * C, C), (2 * C) ** -0.5, 0.375),
        "w_out": normal_values(seeds[10], (C,), C ** -0.5, 0.5, jnp.float32),
        "e_shift": jnp.clip(jax.random.uniform(seeds[11], (SP,), jnp.float32, 0.2, 0.6), 0.2, 0.6),
        "u_reference": draw_u_reference(jax.random.fold_in(seeds[16], 71), 0),
        "inverse_temp": jnp.clip(jnp.exp(jax.random.uniform(seeds[13], (1,), jnp.float32, math.log(0.002), math.log(0.006))), 0.002, 0.006),
        "q_vectors": jnp.clip(jax.random.uniform(seeds[14], (3, Q), jnp.float32, -1.5, 1.5), -1.5, 1.5),
        "s_target": jnp.clip(jax.random.uniform(seeds[15], (Q,), jnp.float32, 0.2, 1.0), 0.2, 1.0),
    }


slab_depth = 6.0
vector_scale = 0.2
target_var = 0.01
hydrogen_length = -0.64

def radial_basis(distance, number):
    centers = jnp.arange(number, dtype=jnp.float32)
    return jnp.exp(-jnp.square(distance[..., None] - centers))

def silu_slope(values):
    sigmoid = jax.nn.sigmoid(values)
    return sigmoid * (1.0 + values * (1.0 - sigmoid))

def edge_terms(feature_all, coord_all, own_coords, slot_lists, rad_first, rad_second):
    present = slot_lists >= 0
    target_idx = jnp.maximum(slot_lists, 0)
    offsets = coord_all[:, target_idx] - own_coords[:, None, :]
    distance = jnp.sqrt(lax.optimization_barrier(jnp.sum(offsets * offsets, axis=0)))
    expanded = lax.optimization_barrier(radial_basis(distance, rad_first.shape[0]).astype(jnp.bfloat16))
    hidden = jax.nn.silu(jnp.einsum('kbn,nh->kbh', expanded.astype(jnp.float32), rad_first.astype(jnp.float32)))
    hidden = lax.optimization_barrier(hidden.astype(jnp.bfloat16))
    radial = jnp.einsum('kbh,hc->kbc', hidden.astype(jnp.float32), rad_second.astype(jnp.float32))
    radial = radial * present[..., None]
    channels = feature_all.shape[1]
    gathered = feature_all[target_idx].astype(jnp.float32)
    scaling = slot_lists.shape[0] ** (-0.5)
    scalar_part = scaling * lax.optimization_barrier(jnp.sum(radial[..., :channels] * gathered, axis=0))
    vector_term = radial[..., channels:] * gathered
    squared = jnp.zeros_like(scalar_part)
    for component in range(3):
        projected = scaling * lax.optimization_barrier(jnp.sum((vector_scale * offsets[component])[..., None] * vector_term, axis=0))
        squared = squared + projected * projected
    return jnp.concatenate([scalar_part, squared], axis=1)

def frame_terms(frame_coords, frame_species, live_count, frame_halo, frame_lists, embedding, w_msg, w_rad1, w_rad2, w_up, w_out, e_shift, q_vectors):
    slot_count = frame_lists.shape[0]
    slab_coords = frame_coords.reshape(3, N_SLAB, ATOMS_DEV).transpose(1, 0, 2)
    slab_species = frame_species.reshape(N_SLAB, ATOMS_DEV)
    slab_halo = frame_halo.reshape(2, N_SLAB, HALO)
    slab_lists = frame_lists.reshape(slot_count, N_SLAB, ATOMS_DEV).transpose(1, 0, 2)
    living = (jnp.arange(ATOMS_DEV)[None, :] < live_count[:, None]).astype(jnp.float32)
    pick_columns = jax.vmap(lambda source, chosen: source[:, chosen])
    pick_rows = jax.vmap(lambda source, chosen: source[chosen])
    slab_lift = jnp.array([0.0, 0.0, slab_depth], dtype=jnp.float32)[None, :, None]
    down_coords = pick_columns(slab_coords, slab_halo[0])
    up_coords = pick_columns(slab_coords, slab_halo[1])
    coord_all = jnp.concatenate([slab_coords, jnp.roll(up_coords, 1, axis=0) - slab_lift, jnp.roll(down_coords, -1, axis=0) + slab_lift], axis=2)
    features = embedding[slab_species].astype(jnp.float32)
    channels = features.shape[-1]
    mixed_in = None
    update = None
    for layer_idx in range(LAYERS):
        message = jnp.dot(features.reshape(-1, channels).astype(jnp.bfloat16), w_msg[layer_idx], preferred_element_type=jnp.float32)
        message = message.astype(jnp.bfloat16).reshape(features.shape)
        down_rows = pick_rows(message, slab_halo[0])
        up_rows = pick_rows(message, slab_halo[1])
        feature_all = jnp.concatenate([message, jnp.roll(up_rows, 1, axis=0), jnp.roll(down_rows, -1, axis=0)], axis=1)
        first_rad = w_rad1[layer_idx]
        second_rad = w_rad2[layer_idx]
        mixed = lax.map(lambda operands: edge_terms(operands[0], operands[1], operands[2], operands[3], first_rad, second_rad), (feature_all, coord_all, slab_coords, slab_lists))
        mixed_in = mixed.astype(jnp.bfloat16)
        update = jnp.dot(mixed_in.reshape(-1, 2 * channels), w_up[layer_idx], preferred_element_type=jnp.float32).reshape(features.shape)
        features = features + jax.nn.silu(update)
    readout = jnp.dot(features.reshape(-1, channels), w_out, precision=lax.Precision.HIGHEST).reshape(living.shape)
    atom_energy = living * (readout + e_shift[slab_species])
    frame_total = jnp.sum(atom_energy)
    global_z = slab_coords[:, 2, :] + jnp.arange(N_SLAB, dtype=jnp.float32)[:, None] * slab_depth
    phases = q_vectors[0][None, :, None] * slab_coords[:, 0, :][:, None, :] + q_vectors[1][None, :, None] * slab_coords[:, 1, :][:, None, :] + q_vectors[2][None, :, None] * global_z[:, None, :]
    lengths = living * jnp.where(slab_species == 1, 1.0, hydrogen_length)
    cos_sum = lax.optimization_barrier(jnp.sum(lengths[:, None, :] * jnp.cos(phases), axis=(0, 2)))
    sin_sum = lax.optimization_barrier(jnp.sum(lengths[:, None, :] * jnp.sin(phases), axis=(0, 2)))
    structure = (cos_sum * cos_sum + sin_sum * sin_sum) / ATOMS
    grad_out_f = lax.optimization_barrier(jnp.sum(living[..., None] * features, axis=(0, 1)))
    slope = (living[..., None] * w_out * silu_slope(update)).astype(jnp.bfloat16)
    grad_up_f = jnp.einsum('ak,ac->kc', mixed_in.reshape(-1, 2 * channels).astype(jnp.float32), slope.reshape(-1, channels).astype(jnp.float32), precision=lax.Precision.HIGHEST)
    return (atom_energy.reshape(-1), frame_total, structure, grad_up_f, grad_out_f)

def reference(positions, species, atom_count, halo_index, neighbours, embedding, w_msg, w_rad1, w_rad2, w_up, w_out, e_shift, u_reference, inverse_temp, q_vectors, s_target):
    energies, totals, structure, grad_ups, grad_outs = lax.map(lambda operands: frame_terms(operands[0], operands[1], operands[2], operands[3], operands[4], embedding, w_msg, w_rad1, w_rad2, w_up, w_out, e_shift, q_vectors), (positions, species, atom_count, halo_index, neighbours))
    log_weight = -inverse_temp[0] * (totals - u_reference)
    scaled = jnp.exp(log_weight - jnp.max(log_weight))
    weights = scaled / jnp.sum(scaled)
    mean_structure = lax.optimization_barrier(jnp.sum(weights[:, None] * structure, axis=0))
    slope_sq = (mean_structure - s_target) / target_var
    observed = lax.optimization_barrier(jnp.sum(structure * slope_sq, axis=1))
    average = jnp.sum(mean_structure * slope_sq)
    factor = -inverse_temp[0] * weights * (observed - average)
    grad_up = lax.optimization_barrier(jnp.sum(factor[:, None, None] * grad_ups, axis=0))
    grad_out = lax.optimization_barrier(jnp.sum(factor[:, None] * grad_outs, axis=0))
    return (energies, mean_structure, grad_up, grad_out)
```

```python
import functools

import jax
import jax.numpy as jnp
from jax import lax
from jax.experimental import pallas as pl
from jax.experimental.pallas import tpu as pltpu
from jax.sharding import PartitionSpec as P

slab_depth = 6.0
vector_scale = 0.2
target_var = 0.01
hydrogen_length = -0.64
LANES = 128
GROUP = 4
EXTRA = 8
VMEM_BYTES = 48 * 1024 * 1024

f32 = jnp.float32
bf16 = jnp.bfloat16


def lane_gather(table, index):
    numbers = lax.GatherDimensionNumbers(
        offset_dims=(),
        collapsed_slice_dims=(1,),
        start_index_map=(1,),
        operand_batching_dims=(0,),
        start_indices_batching_dims=(0,),
    )
    return lax.gather(
        table,
        index[..., None],
        numbers,
        slice_sizes=(1, 1),
        mode=lax.GatherScatterMode.PROMISE_IN_BOUNDS,
    )


def spread(row, rows):
    return jnp.broadcast_to(row, (rows, row.shape[1]))


def column(row):
    return spread(row, LANES).T


def as_row(col):
    wide = jnp.broadcast_to(col, (col.shape[0], LANES))
    if col.shape[0] < LANES:
        wide = jnp.concatenate([wide, jnp.zeros((LANES - col.shape[0], LANES), f32)], axis=0)
    return wide.T[0:1]


def sigmoid(values):
    return 0.5 * (1.0 + jnp.tanh(0.5 * values))


def silu(values):
    half = 0.5 * values
    return half + half * jnp.tanh(half)


def mm(a, b):
    return jnp.dot(a, b, preferred_element_type=f32)


def rad1_blocks(w_rad1):
    basis, hidden = w_rad1.shape
    w = w_rad1.astype(f32)
    wide = jnp.concatenate([w] * GROUP, axis=1)
    tall = jnp.concatenate([wide] * GROUP, axis=0)
    row = lax.broadcasted_iota(jnp.int32, tall.shape, 0) // basis
    col = lax.broadcasted_iota(jnp.int32, tall.shape, 1) // hidden
    tall = jnp.where(row == col, tall, 0.0)
    tall = jnp.concatenate([tall, jnp.zeros((LANES - GROUP * basis, GROUP * hidden), f32)], axis=0)
    return tall.T[:, : GROUP * basis].astype(bf16)


def transposed(w):
    return w.astype(f32).T.astype(bf16)


def pack_kernel(pos_ref, spec_ref, halo_ref, down_ref, up_ref):
    frames = pos_ref.shape[0]
    for f in range(frames):
        rows = [pos_ref[f, c : c + 1, :] for c in range(3)]
        rows.append(spec_ref[f : f + 1, :].astype(f32))
        for side, out in ((0, down_ref), (1, up_ref)):
            index = halo_ref[f, side : side + 1, :]
            lane = spread(index & (LANES - 1), 8)
            high = spread(index, 8) >= LANES
            for c, row in enumerate(rows):
                low_g = lane_gather(spread(row[:, :LANES], 8), lane)
                high_g = lane_gather(spread(row[:, LANES:], 8), lane)
                out[4 * f + c : 4 * f + c + 1, :] = jnp.where(high, high_g, low_g)[0:1]


def structure_kernel(slab_ref, count_ref, pos_ref, spec_ref, qt_ref, out_ref):
    frames, _, atoms = pos_ref.shape
    lift = slab_ref[0].astype(f32) * slab_depth
    number = lax.broadcasted_iota(jnp.int32, (1, atoms), 1)
    for f in range(frames):
        x, y, z = (pos_ref[f, c : c + 1, :] for c in range(3))
        phases = qt_ref[:, 0:1] * x + qt_ref[:, 1:2] * y + qt_ref[:, 2:3] * (z + lift)
        lengths = jnp.where(spec_ref[f : f + 1, :] == 1, 1.0, hydrogen_length)
        lengths = jnp.where(number < count_ref[f, 0], lengths, 0.0)
        cos_part = jnp.sum(lengths * jnp.cos(phases), axis=1, keepdims=True)
        sin_part = jnp.sum(lengths * jnp.sin(phases), axis=1, keepdims=True)
        out_ref[2 + f : 3 + f, :] = as_row(cos_part)
        out_ref[4 + f : 5 + f, :] = as_row(sin_part)
    out_ref[0:2, :] = jnp.zeros((2, LANES), f32)
    out_ref[6:8, :] = jnp.zeros((2, LANES), f32)


def basis_rows(dist_ref, f, i, first, atoms):
    center = lax.broadcasted_iota(jnp.int32, (8, atoms), 0).astype(f32)
    parts = []
    for j in range(first, first + GROUP):
        off = spread(dist_ref[f, 3, i, j : j + 1, :], 8) - center
        parts.append(jnp.exp(-(off * off)))
    return jnp.concatenate(parts, axis=0).astype(bf16)


def first_kernel(
    pos_ref,
    spec_ref,
    below_ref,
    above_ref,
    nb_ref,
    halo_ref,
    emb_ref,
    wmsg_ref,
    wr1_ref,
    wr2_ref,
    wup_ref,
    geo_ref,
    feat_ref,
    msg_ref,
    down_ref,
    up_ref,
    wgt_ref,
    acc_ref,
    w1_ref,
):
    frames, _, atoms = pos_ref.shape
    batches = nb_ref.shape[1]
    slots = batches * 8
    hidden = wr1_ref.shape[2]
    w1_ref[...] = rad1_blocks(wr1_ref[0])
    w2 = transposed(wr2_ref[0])
    w2s = jnp.concatenate([w2[:LANES]] * 2, axis=1)
    w2v = jnp.concatenate([w2[LANES:]] * 2, axis=1)
    wup = transposed(wup_ref[0])
    wmsg = transposed(wmsg_ref[1])
    emb = emb_ref[...]
    table = mm(emb, wmsg_ref[0]).astype(bf16).astype(f32)
    emb_cols = [column(emb[s : s + 1].astype(f32)) for s in range(2)]
    msg_cols = [column(table[s : s + 1]) for s in range(2)]
    scale = slots**-0.5
    for f in range(frames):
        for half in range(atoms // LANES):
            cols = slice(half * LANES, (half + 1) * LANES)
            for s in range(batches):
                index = nb_ref[f, s, :, cols]
                lane = index & (LANES - 1)
                block = index >> 7
                present = (index >= 0).astype(f32)

                def fetch(own_row, halo_row):
                    parts = [
                        own_row[:, :LANES],
                        own_row[:, LANES:],
                        below_ref[halo_row : halo_row + 1, :],
                        above_ref[halo_row : halo_row + 1, :],
                    ]
                    return parts

                squares = None
                offsets = []
                for c in range(3):
                    own_row = pos_ref[f, c : c + 1, :]
                    parts = fetch(own_row, 4 * f + c)
                    if c == 2:
                        parts[2] = parts[2] - slab_depth
                        parts[3] = parts[3] + slab_depth
                    got = [lane_gather(spread(p, 8), lane) for p in parts]
                    there = jnp.where(
                        block == 0,
                        got[0],
                        jnp.where(block == 1, got[1], jnp.where(block == 2, got[2], got[3])),
                    )
                    offset = there - own_row[:, cols]
                    offsets.append(offset)
                    geo_ref[f, c, s, :, cols] = offset
                    squares = offset * offset if squares is None else squares + offset * offset
                geo_ref[f, 3, s, :, cols] = jnp.sqrt(squares)
                parts = fetch(spec_ref[f : f + 1, :].astype(f32), 4 * f + 3)
                got = [lane_gather(spread(p, 8), lane) for p in parts]
                kind = jnp.where(
                    block == 0,
                    got[0],
                    jnp.where(block == 1, got[1], jnp.where(block == 2, got[2], got[3])),
                )
                kinds = (present * (1.0 - kind), present * kind)
                for k in range(2):
                    wgt_ref[k, s, :, cols] = kinds[k]
                    for c in range(3):
                        wgt_ref[2 * (c + 1) + k, s, :, cols] = offsets[c] * kinds[k]
        acc_ref[...] = jnp.zeros_like(acc_ref)

        def step(i, carry):
            acts = []
            for first in range(0, 8, GROUP):
                pre = mm(w1_ref[...], basis_rows(geo_ref, f, i, first, atoms))
                acts.append(silu(pre).astype(bf16).astype(f32))
            for half in range(atoms // LANES):
                cols = slice(half * LANES, (half + 1) * LANES)
                for part in range(0, hidden, 32):
                    hid = []
                    for j in range(8):
                        at = (j % GROUP) * hidden + part
                        hid.append(acts[j // GROUP][at : at + 32, cols])
                    for k in range(8):
                        total = acc_ref[k, part : part + 32, cols]
                        for j in range(8):
                            total = total + wgt_ref[k, i, j : j + 1, cols] * hid[j]
                        acc_ref[k, part : part + 32, cols] = total
            return carry

        lax.fori_loop(0, batches, step, 0)

        def project(k, w):
            total = acc_ref[k]
            high = total.astype(bf16)
            low = (total - high.astype(f32)).astype(bf16)
            return mm(w, jnp.concatenate([high, low], axis=0))

        cols0 = jnp.concatenate([msg_cols[0]] * 2, axis=1)
        cols1 = jnp.concatenate([msg_cols[1]] * 2, axis=1)
        scalar = scale * (cols0 * project(0, w2s) + cols1 * project(1, w2s))
        squared = None
        for c in range(3):
            vec = (scale * vector_scale) * (
                cols0 * project(2 * c + 2, w2v) + cols1 * project(2 * c + 3, w2v)
            )
            squared = vec * vec if squared is None else squared + vec * vec
        mixed = jnp.concatenate([scalar, squared], axis=0).astype(bf16)
        update = mm(wup, mixed)
        e0 = jnp.concatenate([emb_cols[0]] * 2, axis=1)
        e1 = jnp.concatenate([emb_cols[1]] * 2, axis=1)
        features = jnp.where(spec_ref[f : f + 1, :] == 1, e1, e0) + silu(update)
        feat_ref[f] = features
        message = mm(wmsg, features.astype(bf16)).astype(bf16)
        msg_ref[f] = message
        message = message.astype(f32)
        for side, out in ((0, down_ref), (1, up_ref)):
            index = halo_ref[f, side : side + 1, :]
            lane = spread(index & (LANES - 1), LANES)
            low_g = lane_gather(message[:, :LANES], lane)
            high_g = lane_gather(message[:, LANES:], lane)
            out[f] = jnp.where(index >= LANES, high_g, low_g).astype(bf16)


def hidden_kernel(geo_ref, nb_ref, wr1_ref, out_ref, w1_ref):
    frames, batches, _, atoms = nb_ref.shape
    hidden = wr1_ref.shape[2]
    w1_ref[...] = rad1_blocks(wr1_ref[1])
    for f in range(frames):

        def step(i, carry):
            for first in range(0, 8, GROUP):
                act = silu(mm(w1_ref[...], basis_rows(geo_ref, f, i, first, atoms)))
                for j in range(GROUP):
                    here = nb_ref[f, i, first + j : first + j + 1, :] >= 0
                    rows = slice(j * hidden, (j + 1) * hidden)
                    kept = jnp.where(here, act[rows], 0.0).astype(bf16)
                    out_ref[f, i, (first + j) * hidden : (first + j + 1) * hidden, :] = kept
            return carry

        lax.fori_loop(0, batches, step, 0)


def second_kernel(
    rows_each,
    count_ref,
    spec_ref,
    eshift_ref,
    nb_ref,
    geo_ref,
    hid_ref,
    feat_ref,
    msg_ref,
    below_ref,
    above_ref,
    wr2_ref,
    wup_ref,
    wout_ref,
    struct_ref,
    energy_ref,
    chunk_ref,
    acc_ref,
    src_ref,
    w2_ref,
):
    frames, batches, _, atoms = nb_ref.shape
    slots = batches * 8
    hidden = wr2_ref.shape[1]
    chunks = chunk_ref.shape[0]
    w2_ref[...] = transposed(wr2_ref[1])
    wup = transposed(wup_ref[1])
    wout = jnp.concatenate([column(wout_ref[...])] * 2, axis=1)
    scale = slots**-0.5
    number = lax.broadcasted_iota(jnp.int32, (1, atoms), 1)
    extra = [None] * EXTRA
    for f in range(frames):
        src_ref[0] = msg_ref[f, :, :LANES].astype(f32)
        src_ref[1] = msg_ref[f, :, LANES:].astype(f32)
        src_ref[2] = below_ref[f].astype(f32)
        src_ref[3] = above_ref[f].astype(f32)
        acc_ref[...] = jnp.zeros_like(acc_ref)

        def step(i, carry):
            filters = [
                mm(w2_ref[...], hid_ref[f, i, j * hidden : (j + 1) * hidden, :]) for j in range(8)
            ]
            width = 32
            for half in range(atoms // LANES):
                cols = slice(half * LANES, (half + 1) * LANES)
                index = [nb_ref[f, i, j : j + 1, cols] for j in range(8)]
                lane = [spread(v & (LANES - 1), width) for v in index]
                block = [spread(v >> 7, width) for v in index]
                offset = [[geo_ref[f, c, i, j : j + 1, cols] for c in range(3)] for j in range(8)]
                for part in range(0, LANES, width):
                    rows = slice(part, part + width)
                    total = [acc_ref[k, rows, cols] for k in range(4)]
                    for j in range(8):
                        got = [lane_gather(src_ref[b, rows, :], lane[j]) for b in range(4)]
                        there = jnp.where(
                            block[j] < 2,
                            jnp.where(block[j] == 1, got[1], got[0]),
                            jnp.where(block[j] == 2, got[2], got[3]),
                        )
                        total[0] = total[0] + filters[j][rows, cols] * there
                        vec = filters[j][LANES + part : LANES + part + width, cols] * there
                        for c in range(3):
                            total[c + 1] = total[c + 1] + offset[j][c] * vec
                    for k in range(4):
                        acc_ref[k, rows, cols] = total[k]
            return carry

        lax.fori_loop(0, batches, step, 0)

        scalar = scale * acc_ref[0]
        squared = None
        for c in range(3):
            vec = (scale * vector_scale) * acc_ref[c + 1]
            squared = vec * vec if squared is None else squared + vec * vec
        mixed = jnp.concatenate([scalar, squared], axis=0).astype(bf16)
        update = mm(wup, mixed)
        gate = sigmoid(update)
        features = feat_ref[f] + update * gate
        living = (number < count_ref[f, 0]).astype(f32)
        slope = (living * wout * (gate * (1.0 + update * (1.0 - gate)))).astype(bf16)
        kind = spec_ref[f : f + 1, :]
        readout = jnp.sum(features * wout, axis=0, keepdims=True)
        energy = living * (readout + jnp.where(kind == 1, eshift_ref[1], eshift_ref[0]))
        energy_ref[f : f + 1, :] = energy
        grad = lax.dot_general(mixed, slope, (((1,), (1,)), ((), ())), preferred_element_type=f32)
        chunk_ref[:, f * rows_each : (f + 1) * rows_each, :] = grad.reshape(
            chunks, rows_each, LANES
        )
        extra[f] = as_row(jnp.sum(living * features, axis=1, keepdims=True))
        extra[2 + f] = struct_ref[2 + f : 3 + f, :]
        extra[4 + f] = struct_ref[4 + f : 5 + f, :]
        extra[6 + f] = jnp.broadcast_to(jnp.sum(energy, axis=1, keepdims=True), (1, LANES))
    block = jnp.concatenate(extra, axis=0)
    chunk_ref[:, frames * rows_each :, :] = jnp.broadcast_to(block[None], (chunks, EXTRA, LANES))


def total_kernel(uref_ref, beta_ref, in_ref, out_ref):
    rows = in_ref.shape[1]
    total = in_ref[0]
    for s in range(1, in_ref.shape[0]):
        total = total + in_ref[s]
    for d in range(out_ref.shape[0]):
        out_ref[d] = total
    for f in range(2):
        row = total[rows - 2 + f : rows - 1 + f]
        log_weight = -beta_ref[0] * (row - uref_ref[f])
        for d in range(out_ref.shape[0]):
            out_ref[d, rows - 2 + f : rows - 1 + f, :] = log_weight


def final_kernel(rows_each, atoms_all, beta_ref, in_ref, target_ref, chunk_ref, mean_ref, out_ref):
    devices = in_ref.shape[0]
    q = target_ref.shape[1]
    base = 2 * rows_each

    def gather(at):
        return jnp.concatenate([in_ref[d, base + at : base + at + 2, :] for d in range(devices)], 0)

    cos_tot, sin_tot, log_weight = gather(2), gather(4), gather(6)
    structure = ((cos_tot * cos_tot + sin_tot * sin_tot) / atoms_all)[:, :q]
    scaled = jnp.exp(log_weight - jnp.max(log_weight, axis=0, keepdims=True))
    weights = scaled / jnp.sum(scaled, axis=0, keepdims=True)
    mean = jnp.sum(weights[:, :q] * structure, axis=0, keepdims=True)
    slope_sq = (mean - target_ref[...]) / target_var
    observed = jnp.sum(structure * slope_sq, axis=1, keepdims=True)
    average = jnp.sum(mean * slope_sq, axis=1, keepdims=True)
    factor = (-beta_ref[0]) * weights * (observed - average)
    grad = jnp.zeros((rows_each, LANES), f32)
    for d in range(devices):
        for f in range(2):
            k = 2 * d + f
            grad = grad + factor[k : k + 1] * in_ref[d, f * rows_each : (f + 1) * rows_each, :]
    mean_ref[...] = mean
    out_ref[...] = jnp.sum(factor * gather(0), axis=0, keepdims=True)
    for s in range(chunk_ref.shape[0]):
        chunk_ref[s] = grad


VM = pl.BlockSpec(memory_space=pltpu.VMEM)
SM = pl.BlockSpec(memory_space=pltpu.SMEM)


def call(kernel, name, ins, outs, scratch, *operands):
    return pl.pallas_call(
        kernel,
        name=name,
        out_shape=outs,
        in_specs=ins,
        out_specs=jax.tree.map(lambda _: VM, outs),
        scratch_shapes=scratch,
        compiler_params=pltpu.CompilerParams(vmem_limit_bytes=VMEM_BYTES),
    )(*operands)


def array(shape, dtype=f32):
    return jax.ShapeDtypeStruct(shape, dtype)


def per_device(
    positions,
    species,
    atom_count,
    halo_index,
    neighbours,
    embedding,
    w_msg,
    w_rad1,
    w_rad2,
    w_up,
    w_out,
    e_shift,
    u_reference,
    inverse_temp,
    q_vectors,
    s_target,
):
    frames, _, atoms = positions.shape
    slots = neighbours.shape[1]
    halo = halo_index.shape[2]
    hidden = w_rad1.shape[2]
    channels = w_msg.shape[1]
    neighbours = neighbours.reshape(frames, slots // 8, 8, atoms)
    slab_devs = lax.axis_size("slab")
    frame_devs = lax.axis_size("frame")
    rows_each = 2 * channels // slab_devs
    chunk_rows = frames * rows_each + EXTRA
    up = [(i, (i + 1) % slab_devs) for i in range(slab_devs)]
    down = [(j, i) for i, j in up]

    rows = array((4 * frames, halo))
    leave_down, leave_up = call(
        pack_kernel, "halo_rows", [VM] * 3, (rows, rows), [], positions, species, halo_index
    )
    below = lax.ppermute(leave_up, "slab", up)
    above = lax.ppermute(leave_down, "slab", down)
    slab_pos = lax.axis_index("slab").reshape(1)
    structure = call(
        structure_kernel,
        "structure_sums",
        [SM, SM, VM, VM, VM],
        array((EXTRA, LANES)),
        [],
        slab_pos,
        atom_count,
        positions,
        species,
        q_vectors.T,
    )
    halo_rows = array((frames, channels, halo), bf16)
    geometry, features, message, msg_down, msg_up = call(
        first_kernel,
        "first_layer",
        [VM] * 11,
        (
            array((frames, 4, slots // 8, 8, atoms)),
            array((frames, channels, atoms)),
            array((frames, channels, atoms), bf16),
            halo_rows,
            halo_rows,
        ),
        [
            pltpu.VMEM((8, slots // 8, 8, atoms), f32),
            pltpu.VMEM((8, hidden, atoms), f32),
            pltpu.VMEM((GROUP * hidden, GROUP * w_rad1.shape[1]), bf16),
        ],
        positions,
        species,
        below,
        above,
        neighbours,
        halo_index,
        embedding,
        w_msg,
        w_rad1,
        w_rad2,
        w_up,
    )
    msg_below = lax.ppermute(msg_up, "slab", up)
    msg_above = lax.ppermute(msg_down, "slab", down)
    radial_hidden = call(
        hidden_kernel,
        "radial_hidden",
        [VM] * 3,
        array((frames, slots // 8, 8 * hidden, atoms), bf16),
        [pltpu.VMEM((GROUP * hidden, GROUP * w_rad1.shape[1]), bf16)],
        geometry,
        neighbours,
        w_rad1,
    )
    atom_energy, chunks = call(
        functools.partial(second_kernel, rows_each),
        "second_layer",
        [SM, VM, SM] + [VM] * 11,
        (array((frames, atoms)), array((slab_devs, chunk_rows, LANES))),
        [
            pltpu.VMEM((4, channels, atoms), f32),
            pltpu.VMEM((4, channels, LANES), f32),
            pltpu.VMEM((2 * channels, hidden), bf16),
        ],
        atom_count,
        species,
        e_shift,
        neighbours,
        geometry,
        radial_hidden,
        features,
        message,
        msg_below,
        msg_above,
        w_rad2,
        w_up,
        w_out.reshape(1, channels),
        structure,
    )
    chunks = lax.all_to_all(chunks, "slab", 0, 0, tiled=True)
    totals = call(
        total_kernel,
        "slab_totals",
        [SM, SM, VM],
        array((frame_devs, chunk_rows, LANES)),
        [],
        u_reference,
        inverse_temp,
        chunks,
    )
    totals = lax.all_to_all(totals, "frame", 0, 0, tiled=True)
    q = s_target.shape[0]
    grad_rows, mean_structure, grad_out = call(
        functools.partial(final_kernel, rows_each, atoms * slab_devs),
        "reweighted",
        [SM, VM, VM],
        (array((slab_devs, rows_each, LANES)), array((1, q)), array((1, channels))),
        [],
        inverse_temp,
        totals,
        s_target.reshape(1, q),
    )
    grad_up = lax.all_to_all(grad_rows, "slab", 0, 0, tiled=True)
    return (
        atom_energy,
        mean_structure.reshape(q),
        grad_up.reshape(2 * channels, channels),
        grad_out.reshape(channels),
    )


def solution(mesh):
    in_specs = (
        P("frame", None, "slab"),
        P("frame", "slab"),
        P("frame", "slab"),
        P("frame", None, "slab"),
        P("frame", None, "slab"),
        P(),
        P(),
        P(),
        P(),
        P(),
        P(),
        P(),
        P("frame"),
        P(),
        P(),
        P(),
    )
    out_specs = (P("frame", "slab"), P(), P(), P())
    return jax.shard_map(
        per_device, mesh=mesh, in_specs=in_specs, out_specs=out_specs, check_vma=False
    )
```

```python
import functools

import jax
import jax.numpy as jnp
from jax import lax
from jax.experimental import pallas as pl
from jax.experimental.pallas import tpu as pltpu
from jax.sharding import PartitionSpec as P

slab_depth = 6.0
vector_scale = 0.2
target_var = 0.01
hydrogen_length = -0.64
LANES = 128
GROUP = 4
EXTRA = 8
XLU = 32
UN1 = 6
UNH = 3
UN2 = 2
WIDTH = 32
VMEM_BYTES = 48 * 1024 * 1024

f32 = jnp.float32
bf16 = jnp.bfloat16


def lane_gather(table, index):
    numbers = lax.GatherDimensionNumbers(
        offset_dims=(),
        collapsed_slice_dims=(1,),
        start_index_map=(1,),
        operand_batching_dims=(0,),
        start_indices_batching_dims=(0,),
    )
    return lax.gather(
        table,
        index[..., None],
        numbers,
        slice_sizes=(1, 1),
        mode=lax.GatherScatterMode.PROMISE_IN_BOUNDS,
    )


def spread(row, rows):
    return jnp.broadcast_to(row, (rows, row.shape[1]))


def column(row):
    return spread(row, LANES).T


def as_row(col):
    wide = jnp.broadcast_to(col, (col.shape[0], LANES))
    if col.shape[0] < LANES:
        wide = jnp.concatenate([wide, jnp.zeros((LANES - col.shape[0], LANES), f32)], axis=0)
    return wide.T[0:1]


def sigmoid(values):
    return 0.5 * (1.0 + jnp.tanh(0.5 * values))


def silu(values):
    half = 0.5 * values
    return half + half * jnp.tanh(half)


def mm(a, b):
    return jnp.dot(a, b, preferred_element_type=f32)


def rad1_blocks(w_rad1):
    basis, hidden = w_rad1.shape
    w = w_rad1.astype(f32)
    wide = jnp.concatenate([w] * GROUP, axis=1)
    tall = jnp.concatenate([wide] * GROUP, axis=0)
    row = lax.broadcasted_iota(jnp.int32, tall.shape, 0) // basis
    col = lax.broadcasted_iota(jnp.int32, tall.shape, 1) // hidden
    tall = jnp.where(row == col, tall, 0.0)
    tall = jnp.concatenate([tall, jnp.zeros((LANES - GROUP * basis, GROUP * hidden), f32)], axis=0)
    return tall.T[:, : GROUP * basis].astype(bf16)


def transposed(w):
    return w.astype(f32).T.astype(bf16)


def fetch_all(sems, pairs):
    copies = [pltpu.make_async_copy(src, dst, sems.at[i]) for i, (src, dst) in enumerate(pairs)]
    for copy in copies:
        copy.start()
    return copies


def pack_kernel(pos_hbm, spec_hbm, halo_hbm, down_ref, up_ref, pos_ref, spec_ref, halo_ref, sems):
    pairs = ((pos_hbm, pos_ref), (spec_hbm, spec_ref), (halo_hbm, halo_ref))
    for copy in fetch_all(sems, pairs):
        copy.wait()
    frames = spec_ref.shape[0]
    for f in range(frames):
        rows = [pos_ref[c, f : f + 1, :] for c in range(3)]
        rows.append(spec_ref[f : f + 1, :].astype(f32))
        for side, out in ((0, down_ref), (1, up_ref)):
            index = halo_ref[f, side : side + 1, :]
            lane = spread(index & (LANES - 1), 8)
            high = spread(index, 8) >= LANES
            for c, row in enumerate(rows):
                low_g = lane_gather(spread(row[:, :LANES], 8), lane)
                high_g = lane_gather(spread(row[:, LANES:], 8), lane)
                out[4 * f + c : 4 * f + c + 1, :] = jnp.where(high, high_g, low_g)[0:1]


def stage_kernel(
    slab_ref,
    pos_ref,
    spec_ref,
    nb_hbm,
    count_hbm,
    q_hbm,
    emb_hbm,
    wmsg_hbm,
    wr1_hbm,
    wr2_hbm,
    wup_hbm,
    wout_hbm,
    nb_ref,
    w1_ref,
    w2_ref,
    wup_ref,
    wmsg_ref,
    kind_ref,
    wout_ref,
    struct_ref,
    live_ref,
    count_in,
    q_in,
    emb_in,
    wmsg_in,
    wr1_in,
    wr2_in,
    wup_in,
    wout_in,
    sems,
):
    pairs = (
        (count_hbm, count_in),
        (q_hbm, q_in),
        (wr1_hbm, wr1_in),
        (wr2_hbm, wr2_in),
        (wup_hbm, wup_in),
        (wmsg_hbm, wmsg_in),
        (emb_hbm, emb_in),
        (wout_hbm, wout_in),
        (nb_hbm, nb_ref),
    )
    copies = fetch_all(sems, pairs)
    for copy in copies[:-1]:
        copy.wait()
    _, frames, atoms = pos_ref.shape
    number_q = q_in.shape[1]
    same = lax.broadcasted_iota(jnp.int32, (number_q, number_q), 0) == lax.broadcasted_iota(
        jnp.int32, (number_q, number_q), 1
    )
    q = [
        jnp.sum(jnp.where(same, spread(q_in[c : c + 1, :], number_q), 0.0), axis=1, keepdims=True)
        for c in range(3)
    ]
    lift = slab_ref[0].astype(f32) * slab_depth
    number = lax.broadcasted_iota(jnp.int32, (1, atoms), 1)
    struct_ref[...] = jnp.zeros_like(struct_ref)
    for f in range(frames):
        x, y, z = (pos_ref[c, f : f + 1, :] for c in range(3))
        phases = q[0] * x + q[1] * y + q[2] * (z + lift)
        lengths = jnp.where(spec_ref[f : f + 1, :] == 1, 1.0, hydrogen_length)
        living = (number < count_in[:, f : f + 1]).astype(f32)
        live_ref[f : f + 1, :] = living
        lengths = living * lengths
        cos_part = jnp.sum(lengths * jnp.cos(phases), axis=1, keepdims=True)
        sin_part = jnp.sum(lengths * jnp.sin(phases), axis=1, keepdims=True)
        struct_ref[2 + f : 3 + f, :] = as_row(cos_part)
        struct_ref[4 + f : 5 + f, :] = as_row(sin_part)
    for layer in range(2):
        w1_ref[layer] = rad1_blocks(wr1_in[layer])
        w2_ref[layer] = transposed(wr2_in[layer])
        wup_ref[layer] = transposed(wup_in[layer])
    wmsg_ref[...] = transposed(wmsg_in[1])
    emb = emb_in[...]
    table = mm(emb, wmsg_in[0]).astype(bf16).astype(f32)
    for k in range(2):
        kind_ref[k] = column(emb[k : k + 1].astype(f32))
        kind_ref[2 + k] = column(table[k : k + 1])
    wout_ref[...] = column(wout_in[...])
    copies[-1].wait()


def basis_rows(dist_ref, f, i, first, atoms):
    center = lax.broadcasted_iota(jnp.int32, (8, atoms), 0).astype(f32)
    parts = []
    for j in range(first, first + GROUP):
        off = spread(dist_ref[f, 3, i, j : j + 1, :], 8) - center
        parts.append(jnp.exp(-(off * off)))
    return jnp.concatenate(parts, axis=0).astype(bf16)


def first_kernel(
    pos_ref,
    spec_ref,
    below_ref,
    above_ref,
    nb_ref,
    halo_ref,
    w1_ref,
    w2_ref,
    wup_ref,
    wmsg_ref,
    kind_ref,
    geo_ref,
    feat_ref,
    msg_ref,
    down_ref,
    up_ref,
    wgt_ref,
    acc_ref,
):
    _, frames, atoms = pos_ref.shape
    batches = nb_ref.shape[1]
    slots = batches * 8
    hidden = w2_ref.shape[2]
    w2s = jnp.concatenate([w2_ref[0, :LANES, :]] * 2, axis=1)
    w2v = jnp.concatenate([w2_ref[0, LANES:, :]] * 2, axis=1)
    scale = slots**-0.5
    for f in range(frames):
        for half in range(atoms // LANES):
            cols = slice(half * LANES, (half + 1) * LANES)
            for s in range(batches):
                index = nb_ref[f, s, :, cols]
                lane = index & (LANES - 1)
                block = index >> 7
                present = (index >= 0).astype(f32)

                def fetch(own_row, halo_row):
                    parts = [
                        own_row[:, :LANES],
                        own_row[:, LANES:],
                        below_ref[halo_row : halo_row + 1, :],
                        above_ref[halo_row : halo_row + 1, :],
                    ]
                    return parts

                squares = None
                offsets = []
                for c in range(3):
                    own_row = pos_ref[c, f : f + 1, :]
                    parts = fetch(own_row, 4 * f + c)
                    if c == 2:
                        parts[2] = parts[2] - slab_depth
                        parts[3] = parts[3] + slab_depth
                    got = [lane_gather(spread(p, 8), lane) for p in parts]
                    there = jnp.where(
                        block == 0,
                        got[0],
                        jnp.where(block == 1, got[1], jnp.where(block == 2, got[2], got[3])),
                    )
                    offset = there - own_row[:, cols]
                    offsets.append(offset)
                    geo_ref[f, c, s, :, cols] = offset
                    squares = offset * offset if squares is None else squares + offset * offset
                geo_ref[f, 3, s, :, cols] = jnp.sqrt(squares)
                parts = fetch(spec_ref[f : f + 1, :].astype(f32), 4 * f + 3)
                got = [lane_gather(spread(p, 8), lane) for p in parts]
                kind = jnp.where(
                    block == 0,
                    got[0],
                    jnp.where(block == 1, got[1], jnp.where(block == 2, got[2], got[3])),
                )
                kinds = (present * (1.0 - kind), present * kind)
                for k in range(2):
                    wgt_ref[k, s, :, cols] = kinds[k]
                    for c in range(3):
                        wgt_ref[2 * (c + 1) + k, s, :, cols] = offsets[c] * kinds[k]
        acc_ref[...] = jnp.zeros_like(acc_ref)

        def step(i, carry):
            acts = []
            for first in range(0, 8, GROUP):
                pre = mm(w1_ref[0], basis_rows(geo_ref, f, i, first, atoms))
                acts.append(silu(pre).astype(bf16).astype(f32))
            for half in range(atoms // LANES):
                cols = slice(half * LANES, (half + 1) * LANES)
                for part in range(0, hidden, 32):
                    hid = []
                    for j in range(8):
                        at = (j % GROUP) * hidden + part
                        hid.append(acts[j // GROUP][at : at + 32, cols])
                    for k in range(8):
                        total = acc_ref[k, part : part + 32, cols]
                        for j in range(8):
                            total = total + wgt_ref[k, i, j : j + 1, cols] * hid[j]
                        acc_ref[k, part : part + 32, cols] = total
            return carry

        lax.fori_loop(0, batches, step, 0, unroll=UN1)

        def project(k, w):
            total = acc_ref[k]
            high = total.astype(bf16)
            low = (total - high.astype(f32)).astype(bf16)
            return mm(w, jnp.concatenate([high, low], axis=0))

        cols0 = jnp.concatenate([kind_ref[2]] * 2, axis=1)
        cols1 = jnp.concatenate([kind_ref[3]] * 2, axis=1)
        scalar = scale * (cols0 * project(0, w2s) + cols1 * project(1, w2s))
        squared = None
        for c in range(3):
            vec = (scale * vector_scale) * (
                cols0 * project(2 * c + 2, w2v) + cols1 * project(2 * c + 3, w2v)
            )
            squared = vec * vec if squared is None else squared + vec * vec
        mixed = jnp.concatenate([scalar, squared], axis=0).astype(bf16)
        update = mm(wup_ref[0], mixed)
        e0 = jnp.concatenate([kind_ref[0]] * 2, axis=1)
        e1 = jnp.concatenate([kind_ref[1]] * 2, axis=1)
        features = jnp.where(spec_ref[f : f + 1, :] == 1, e1, e0) + silu(update)
        feat_ref[f] = features
        message = mm(wmsg_ref[...], features.astype(bf16)).astype(bf16)
        msg_ref[f] = message
        message = message.astype(f32)
        for side, out in ((0, down_ref), (1, up_ref)):
            index = halo_ref[f, side : side + 1, :]
            lane = spread(index & (LANES - 1), LANES)
            low_g = lane_gather(message[:, :LANES], lane)
            high_g = lane_gather(message[:, LANES:], lane)
            out[f] = jnp.where(index >= LANES, high_g, low_g).astype(bf16)


def hidden_kernel(geo_ref, nb_ref, w1_ref, w2_ref, out_ref):
    frames, batches, _, atoms = nb_ref.shape
    hidden = w2_ref.shape[2]
    for f in range(frames):

        def step(i, carry):
            for first in range(0, 8, GROUP):
                act = silu(mm(w1_ref[1], basis_rows(geo_ref, f, i, first, atoms)))
                for j in range(GROUP):
                    here = nb_ref[f, i, first + j : first + j + 1, :] >= 0
                    rows = slice(j * hidden, (j + 1) * hidden)
                    kept = jnp.where(here, act[rows], 0.0).astype(bf16)
                    out_ref[f, i, (first + j) * hidden : (first + j + 1) * hidden, :] = kept
            return carry

        lax.fori_loop(0, batches, step, 0, unroll=UNH)


def second_kernel(
    rows_each,
    live_ref,
    spec_ref,
    eshift_ref,
    nb_ref,
    geo_ref,
    hid_ref,
    feat_ref,
    msg_ref,
    below_ref,
    above_ref,
    w2_ref,
    wup_ref,
    wout_ref,
    struct_ref,
    energy_ref,
    chunk_ref,
    acc_ref,
    src_ref,
    pair_ref,
):
    frames, batches, _, atoms = nb_ref.shape
    slots = batches * 8
    hidden = w2_ref.shape[2]
    chunks = chunk_ref.shape[0]
    wout = jnp.concatenate([wout_ref[...]] * 2, axis=1)
    scale = slots**-0.5
    extra = [None] * EXTRA
    for f in range(frames):
        src_ref[0] = msg_ref[f, :, :LANES]
        src_ref[1] = msg_ref[f, :, LANES:]
        src_ref[2] = below_ref[f]
        src_ref[3] = above_ref[f]
        halo = jnp.concatenate([below_ref[f, XLU:, :], above_ref[f, XLU:, :]], axis=1)
        pair_ref[...] = jnp.concatenate([msg_ref[f, XLU:, :], halo], axis=0)
        acc_ref[...] = jnp.zeros_like(acc_ref)

        def step(i, carry):
            filters = [
                mm(w2_ref[1], hid_ref[f, i, j * hidden : (j + 1) * hidden, :]) for j in range(8)
            ]
            width = WIDTH
            if XLU < LANES:
                target = lax.broadcasted_iota(jnp.int32, (2 * LANES, atoms), 0).astype(bf16)
                found = []
                for j in range(8):
                    want = (nb_ref[f, i, j : j + 1, :] & (2 * LANES - 1)).astype(f32).astype(bf16)
                    hot = jnp.where(target == want, jnp.asarray(1, bf16), jnp.asarray(0, bf16))
                    found.append(mm(pair_ref[...], hot))
            for half in range(atoms // LANES):
                cols = slice(half * LANES, (half + 1) * LANES)
                index = [nb_ref[f, i, j : j + 1, cols] for j in range(8)]
                lane = [spread(v & (LANES - 1), width).astype(jnp.int16) for v in index]
                block = [spread(v >> 7, width) for v in index]
                block16 = [v.astype(jnp.int16) for v in block]
                offset = [[geo_ref[f, c, i, j : j + 1, cols] for c in range(3)] for j in range(8)]
                for part in range(0, LANES, width):
                    rows = slice(part, part + width)
                    total = [acc_ref[k, rows, cols] for k in range(4)]
                    for j in range(8):
                        if part < XLU:
                            got = [lane_gather(src_ref[b, rows, :], lane[j]) for b in range(4)]
                            there = jnp.where(
                                block16[j] < 2,
                                jnp.where(block16[j] == 1, got[1], got[0]),
                                jnp.where(block16[j] == 2, got[2], got[3]),
                            ).astype(f32)
                        else:
                            at = part - XLU
                            there = jnp.where(
                                block[j] < 2,
                                found[j][at : at + width, cols],
                                found[j][LANES - XLU + at : LANES - XLU + at + width, cols],
                            )
                        total[0] = total[0] + filters[j][rows, cols] * there
                        vec = filters[j][LANES + part : LANES + part + width, cols] * there
                        for c in range(3):
                            total[c + 1] = total[c + 1] + offset[j][c] * vec
                    for k in range(4):
                        acc_ref[k, rows, cols] = total[k]
            return carry

        lax.fori_loop(0, batches, step, 0, unroll=UN2)

        scalar = scale * acc_ref[0]
        squared = None
        for c in range(3):
            vec = (scale * vector_scale) * acc_ref[c + 1]
            squared = vec * vec if squared is None else squared + vec * vec
        mixed = jnp.concatenate([scalar, squared], axis=0).astype(bf16)
        update = mm(wup_ref[1], mixed)
        gate = sigmoid(update)
        features = feat_ref[f] + update * gate
        living = live_ref[f : f + 1, :]
        slope = (living * wout * (gate * (1.0 + update * (1.0 - gate)))).astype(bf16)
        kind = spec_ref[f : f + 1, :]
        readout = jnp.sum(features * wout, axis=0, keepdims=True)
        energy = living * (readout + jnp.where(kind == 1, eshift_ref[1], eshift_ref[0]))
        energy_ref[f : f + 1, :] = energy
        grad = lax.dot_general(mixed, slope, (((1,), (1,)), ((), ())), preferred_element_type=f32)
        chunk_ref[:, f * rows_each : (f + 1) * rows_each, :] = grad.reshape(
            chunks, rows_each, LANES
        )
        extra[f] = as_row(jnp.sum(living * features, axis=1, keepdims=True))
        extra[2 + f] = struct_ref[2 + f : 3 + f, :]
        extra[4 + f] = struct_ref[4 + f : 5 + f, :]
        extra[6 + f] = jnp.broadcast_to(jnp.sum(energy, axis=1, keepdims=True), (1, LANES))
    block = jnp.concatenate(extra, axis=0)
    chunk_ref[:, frames * rows_each :, :] = jnp.broadcast_to(block[None], (chunks, EXTRA, LANES))


def total_kernel(uref_ref, beta_ref, in_ref, out_ref):
    rows = in_ref.shape[1]
    total = in_ref[0]
    for s in range(1, in_ref.shape[0]):
        total = total + in_ref[s]
    for d in range(out_ref.shape[0]):
        out_ref[d] = total
    for f in range(2):
        row = total[rows - 2 + f : rows - 1 + f]
        log_weight = -beta_ref[0] * (row - uref_ref[f])
        for d in range(out_ref.shape[0]):
            out_ref[d, rows - 2 + f : rows - 1 + f, :] = log_weight


def final_kernel(rows_each, atoms_all, beta_ref, in_ref, target_ref, chunk_ref, mean_ref, out_ref):
    devices = in_ref.shape[0]
    q = target_ref.shape[1]
    base = 2 * rows_each

    def gather(at):
        return jnp.concatenate([in_ref[d, base + at : base + at + 2, :] for d in range(devices)], 0)

    cos_tot, sin_tot, log_weight = gather(2), gather(4), gather(6)
    structure = ((cos_tot * cos_tot + sin_tot * sin_tot) / atoms_all)[:, :q]
    scaled = jnp.exp(log_weight - jnp.max(log_weight, axis=0, keepdims=True))
    weights = scaled / jnp.sum(scaled, axis=0, keepdims=True)
    mean = jnp.sum(weights[:, :q] * structure, axis=0, keepdims=True)
    slope_sq = (mean - target_ref[...]) / target_var
    observed = jnp.sum(structure * slope_sq, axis=1, keepdims=True)
    average = jnp.sum(mean * slope_sq, axis=1, keepdims=True)
    factor = (-beta_ref[0]) * weights * (observed - average)
    grad = jnp.zeros((rows_each, LANES), f32)
    for d in range(devices):
        for f in range(2):
            k = 2 * d + f
            grad = grad + factor[k : k + 1] * in_ref[d, f * rows_each : (f + 1) * rows_each, :]
    mean_ref[...] = mean
    out_ref[...] = jnp.sum(factor * gather(0), axis=0, keepdims=True)
    for s in range(chunk_ref.shape[0]):
        chunk_ref[s] = grad


VM = pl.BlockSpec(memory_space=pltpu.VMEM)
SM = pl.BlockSpec(memory_space=pltpu.SMEM)
HB = pl.BlockSpec(memory_space=pltpu.HBM)


def call(kernel, name, ins, outs, scratch, *operands):
    return pl.pallas_call(
        kernel,
        name=name,
        out_shape=outs,
        in_specs=ins,
        out_specs=jax.tree.map(lambda _: VM, outs),
        scratch_shapes=scratch,
        compiler_params=pltpu.CompilerParams(vmem_limit_bytes=VMEM_BYTES),
    )(*operands)


def in_hbm(value):
    return pltpu.with_memory_space_constraint(value, pltpu.HBM)


def array(shape, dtype=f32):
    return jax.ShapeDtypeStruct(shape, dtype)


def per_device(
    positions,
    species,
    atom_count,
    halo_index,
    neighbours,
    embedding,
    w_msg,
    w_rad1,
    w_rad2,
    w_up,
    w_out,
    e_shift,
    u_reference,
    inverse_temp,
    q_vectors,
    s_target,
):
    frames, _, atoms = positions.shape
    slots = neighbours.shape[1]
    halo = halo_index.shape[2]
    hidden = w_rad1.shape[2]
    channels = w_msg.shape[1]
    neighbours = neighbours.reshape(frames, slots // 8, 8, atoms)
    positions = positions.transpose(1, 0, 2)
    slab_devs = lax.axis_size("slab")
    frame_devs = lax.axis_size("frame")
    rows_each = 2 * channels // slab_devs
    chunk_rows = frames * rows_each + EXTRA
    up = [(i, (i + 1) % slab_devs) for i in range(slab_devs)]
    down = [(j, i) for i, j in up]

    basis = w_rad1.shape[1]
    rows = array((4 * frames, halo))
    leave_down, leave_up, positions, species, halo_index = call(
        pack_kernel,
        "halo_rows",
        [HB] * 3,
        (
            rows,
            rows,
            array(positions.shape),
            array(species.shape, jnp.int32),
            array(halo_index.shape, jnp.int32),
        ),
        [pltpu.SemaphoreType.DMA((3,))],
        *map(in_hbm, (positions, species, halo_index)),
    )
    below = lax.ppermute(leave_up, "slab", up)
    above = lax.ppermute(leave_down, "slab", down)
    small = (
        atom_count.reshape(1, frames),
        q_vectors,
        embedding,
        w_msg,
        w_rad1,
        w_rad2,
        w_up,
        w_out.reshape(1, channels),
    )
    neighbours, w1, w2, wup, wmsg, kinds, wout, structure, living = call(
        stage_kernel,
        "staged_inputs",
        [SM, VM, VM] + [HB] * 9,
        (
            array(neighbours.shape, jnp.int32),
            array((2, GROUP * hidden, GROUP * basis), bf16),
            array((2, 2 * channels, hidden), bf16),
            array((2, channels, 2 * channels), bf16),
            array((channels, channels), bf16),
            array((4, channels, LANES)),
            array((channels, LANES)),
            array((EXTRA, LANES)),
            array((frames, atoms)),
        ),
        [pltpu.VMEM(w.shape, w.dtype) for w in small] + [pltpu.SemaphoreType.DMA((9,))],
        lax.axis_index("slab").reshape(1),
        positions,
        species,
        in_hbm(neighbours),
        *map(in_hbm, small),
    )
    halo_rows = array((frames, channels, halo), bf16)
    geometry, features, message, msg_down, msg_up = call(
        first_kernel,
        "first_layer",
        [VM] * 11,
        (
            array((frames, 4, slots // 8, 8, atoms)),
            array((frames, channels, atoms)),
            array((frames, channels, atoms), bf16),
            halo_rows,
            halo_rows,
        ),
        [pltpu.VMEM((8, slots // 8, 8, atoms), f32), pltpu.VMEM((8, hidden, atoms), f32)],
        positions,
        species,
        below,
        above,
        neighbours,
        halo_index,
        w1,
        w2,
        wup,
        wmsg,
        kinds,
    )
    msg_below = lax.ppermute(msg_up, "slab", up)
    msg_above = lax.ppermute(msg_down, "slab", down)
    radial_hidden = call(
        hidden_kernel,
        "radial_hidden",
        [VM] * 4,
        array((frames, slots // 8, 8 * hidden, atoms), bf16),
        [],
        geometry,
        neighbours,
        w1,
        w2,
    )
    atom_energy, chunks = call(
        functools.partial(second_kernel, rows_each),
        "second_layer",
        [VM, VM, SM] + [VM] * 11,
        (array((frames, atoms)), array((slab_devs, chunk_rows, LANES))),
        [
            pltpu.VMEM((4, channels, atoms), f32),
            pltpu.VMEM((4, channels, LANES), bf16),
            pltpu.VMEM((2 * (LANES - XLU), 2 * LANES), bf16),
        ],
        living,
        species,
        e_shift,
        neighbours,
        geometry,
        radial_hidden,
        features,
        message,
        msg_below,
        msg_above,
        w2,
        wup,
        wout,
        structure,
    )
    chunks = lax.all_to_all(chunks, "slab", 0, 0, tiled=True)
    totals = call(
        total_kernel,
        "slab_totals",
        [SM, SM, VM],
        array((frame_devs, chunk_rows, LANES)),
        [],
        u_reference,
        inverse_temp,
        chunks,
    )
    totals = lax.all_to_all(totals, "frame", 0, 0, tiled=True)
    q = s_target.shape[0]
    grad_rows, mean_structure, grad_out = call(
        functools.partial(final_kernel, rows_each, atoms * slab_devs),
        "reweighted",
        [SM, VM, VM],
        (array((slab_devs, rows_each, LANES)), array((1, q)), array((1, channels))),
        [],
        inverse_temp,
        totals,
        s_target.reshape(1, q),
    )
    grad_up = lax.all_to_all(grad_rows, "slab", 0, 0, tiled=True)
    return (
        atom_energy,
        mean_structure.reshape(q),
        grad_up.reshape(2 * channels, channels),
        grad_out.reshape(channels),
    )


def solution(mesh):
    in_specs = (
        P("frame", None, "slab"),
        P("frame", "slab"),
        P("frame", "slab"),
        P("frame", None, "slab"),
        P("frame", None, "slab"),
        P(),
        P(),
        P(),
        P(),
        P(),
        P(),
        P(),
        P("frame"),
        P(),
        P(),
        P(),
    )
    out_specs = (P("frame", "slab"), P(), P(), P())
    return jax.shard_map(
        per_device, mesh=mesh, in_specs=in_specs, out_specs=out_specs, check_vma=False
    )
```

```python
import functools

import jax
import jax.numpy as jnp
from jax import lax
from jax.experimental import pallas as pl
from jax.experimental.pallas import tpu as pltpu
from jax.sharding import PartitionSpec as P

slab_depth = 6.0
vector_scale = 0.2
target_var = 0.01
hydrogen_length = -0.64
LANES = 128
GROUP = 4
EXTRA = 8
XLU = 32
UN1 = 6
UNH = 3
UN2 = 2
WIDTH = 32
VMEM_BYTES = 48 * 1024 * 1024

f32 = jnp.float32
bf16 = jnp.bfloat16


def lane_gather(table, index):
    numbers = lax.GatherDimensionNumbers(
        offset_dims=(),
        collapsed_slice_dims=(1,),
        start_index_map=(1,),
        operand_batching_dims=(0,),
        start_indices_batching_dims=(0,),
    )
    return lax.gather(
        table,
        index[..., None],
        numbers,
        slice_sizes=(1, 1),
        mode=lax.GatherScatterMode.PROMISE_IN_BOUNDS,
    )


def spread(row, rows):
    return jnp.broadcast_to(row, (rows, row.shape[1]))


def column(row):
    return spread(row, LANES).T


def as_row(col):
    wide = jnp.broadcast_to(col, (col.shape[0], LANES))
    if col.shape[0] < LANES:
        wide = jnp.concatenate([wide, jnp.zeros((LANES - col.shape[0], LANES), f32)], axis=0)
    return wide.T[0:1]


def sigmoid(values):
    return 0.5 * (1.0 + jnp.tanh(0.5 * values))


def silu(values):
    half = 0.5 * values
    return half + half * jnp.tanh(half)


def mm(a, b):
    return jnp.dot(a, b, preferred_element_type=f32)


def rad1_blocks(w_rad1):
    basis, hidden = w_rad1.shape
    w = w_rad1.astype(f32)
    wide = jnp.concatenate([w] * GROUP, axis=1)
    tall = jnp.concatenate([wide] * GROUP, axis=0)
    row = lax.broadcasted_iota(jnp.int32, tall.shape, 0) // basis
    col = lax.broadcasted_iota(jnp.int32, tall.shape, 1) // hidden
    tall = jnp.where(row == col, tall, 0.0)
    tall = jnp.concatenate([tall, jnp.zeros((LANES - GROUP * basis, GROUP * hidden), f32)], axis=0)
    return tall.T[:, : GROUP * basis].astype(bf16)


def transposed(w):
    return w.astype(f32).T.astype(bf16)


def fetch_all(sems, pairs):
    copies = [pltpu.make_async_copy(src, dst, sems.at[i]) for i, (src, dst) in enumerate(pairs)]
    for copy in copies:
        copy.start()
    return copies


def pack_kernel(pos_hbm, spec_hbm, halo_hbm, down_ref, up_ref, pos_ref, spec_ref, halo_ref, sems):
    pairs = ((pos_hbm, pos_ref), (spec_hbm, spec_ref), (halo_hbm, halo_ref))
    for copy in fetch_all(sems, pairs):
        copy.wait()
    frames = spec_ref.shape[0]
    for f in range(frames):
        rows = [pos_ref[c, f : f + 1, :] for c in range(3)]
        rows.append(spec_ref[f : f + 1, :].astype(f32))
        for side, out in ((0, down_ref), (1, up_ref)):
            index = halo_ref[f, side : side + 1, :]
            lane = spread(index & (LANES - 1), 8)
            high = spread(index, 8) >= LANES
            for c, row in enumerate(rows):
                low_g = lane_gather(spread(row[:, :LANES], 8), lane)
                high_g = lane_gather(spread(row[:, LANES:], 8), lane)
                out[4 * f + c : 4 * f + c + 1, :] = jnp.where(high, high_g, low_g)[0:1]


def stage_kernel(
    slab_ref,
    beta_ref,
    pos_ref,
    spec_ref,
    nb_hbm,
    target_hbm,
    uref_hbm,
    eshift_hbm,
    count_hbm,
    q_hbm,
    emb_hbm,
    wmsg_hbm,
    wr1_hbm,
    wr2_hbm,
    wup_hbm,
    wout_hbm,
    nb_ref,
    w1_ref,
    w2_ref,
    wup_ref,
    wmsg_ref,
    kind_ref,
    wout_ref,
    struct_ref,
    live_ref,
    scalar_ref,
    target_ref,
    uref_in,
    eshift_in,
    count_in,
    q_in,
    emb_in,
    wmsg_in,
    wr1_in,
    wr2_in,
    wup_in,
    wout_in,
    sems,
):
    pairs = (
        (count_hbm, count_in),
        (uref_hbm, uref_in),
        (eshift_hbm, eshift_in),
        (target_hbm, target_ref),
        (q_hbm, q_in),
        (wr1_hbm, wr1_in),
        (wr2_hbm, wr2_in),
        (wup_hbm, wup_in),
        (wmsg_hbm, wmsg_in),
        (emb_hbm, emb_in),
        (wout_hbm, wout_in),
        (nb_hbm, nb_ref),
    )
    copies = fetch_all(sems, pairs)
    for copy in copies[:-1]:
        copy.wait()
    _, frames, atoms = pos_ref.shape
    number_q = q_in.shape[1]
    same = lax.broadcasted_iota(jnp.int32, (number_q, number_q), 0) == lax.broadcasted_iota(
        jnp.int32, (number_q, number_q), 1
    )
    q = [
        jnp.sum(jnp.where(same, spread(q_in[c : c + 1, :], number_q), 0.0), axis=1, keepdims=True)
        for c in range(3)
    ]
    lift = slab_ref[0].astype(f32) * slab_depth
    number = lax.broadcasted_iota(jnp.int32, (1, atoms), 1)
    struct_ref[...] = jnp.zeros_like(struct_ref)
    for f in range(frames):
        x, y, z = (pos_ref[c, f : f + 1, :] for c in range(3))
        phases = q[0] * x + q[1] * y + q[2] * (z + lift)
        lengths = jnp.where(spec_ref[f : f + 1, :] == 1, 1.0, hydrogen_length)
        living = (number < count_in[:, f : f + 1]).astype(f32)
        live_ref[f : f + 1, :] = living
        lengths = living * lengths
        cos_part = jnp.sum(lengths * jnp.cos(phases), axis=1, keepdims=True)
        sin_part = jnp.sum(lengths * jnp.sin(phases), axis=1, keepdims=True)
        struct_ref[2 + f : 3 + f, :] = as_row(cos_part)
        struct_ref[4 + f : 5 + f, :] = as_row(sin_part)
    for layer in range(2):
        w1_ref[layer] = rad1_blocks(wr1_in[layer])
        w2_ref[layer] = transposed(wr2_in[layer])
        wup_ref[layer] = transposed(wup_in[layer])
    wmsg_ref[...] = transposed(wmsg_in[1])
    emb = emb_in[...]
    table = mm(emb, wmsg_in[0]).astype(bf16).astype(f32)
    for k in range(2):
        kind_ref[k] = column(emb[k : k + 1].astype(f32))
        kind_ref[2 + k] = column(table[k : k + 1])
    wout_ref[...] = column(wout_in[...])
    for k in range(2):
        scalar_ref[k : k + 1, :] = jnp.broadcast_to(uref_in[:, k : k + 1], (1, LANES))
        scalar_ref[2 + k : 3 + k, :] = jnp.full((1, LANES), beta_ref[0], f32)
        scalar_ref[4 + k : 5 + k, :] = jnp.broadcast_to(eshift_in[:, k : k + 1], (1, LANES))
    scalar_ref[6:8, :] = jnp.zeros((2, LANES), f32)
    copies[-1].wait()


def basis_rows(dist_ref, f, i, first, atoms):
    center = lax.broadcasted_iota(jnp.int32, (8, atoms), 0).astype(f32)
    parts = []
    for j in range(first, first + GROUP):
        off = spread(dist_ref[f, 3, i, j : j + 1, :], 8) - center
        parts.append(jnp.exp(-(off * off)))
    return jnp.concatenate(parts, axis=0).astype(bf16)


def first_kernel(
    pos_ref,
    spec_ref,
    below_ref,
    above_ref,
    nb_ref,
    halo_ref,
    w1_ref,
    w2_ref,
    wup_ref,
    wmsg_ref,
    kind_ref,
    geo_ref,
    feat_ref,
    msg_ref,
    down_ref,
    up_ref,
    wgt_ref,
    acc_ref,
):
    _, frames, atoms = pos_ref.shape
    batches = nb_ref.shape[1]
    slots = batches * 8
    hidden = w2_ref.shape[2]
    w2s = jnp.concatenate([w2_ref[0, :LANES, :]] * 2, axis=1)
    w2v = jnp.concatenate([w2_ref[0, LANES:, :]] * 2, axis=1)
    scale = slots**-0.5
    for f in range(frames):
        for half in range(atoms // LANES):
            cols = slice(half * LANES, (half + 1) * LANES)
            for s in range(batches):
                index = nb_ref[f, s, :, cols]
                lane = index & (LANES - 1)
                block = index >> 7
                present = (index >= 0).astype(f32)

                def fetch(own_row, halo_row):
                    parts = [
                        own_row[:, :LANES],
                        own_row[:, LANES:],
                        below_ref[halo_row : halo_row + 1, :],
                        above_ref[halo_row : halo_row + 1, :],
                    ]
                    return parts

                squares = None
                offsets = []
                for c in range(3):
                    own_row = pos_ref[c, f : f + 1, :]
                    parts = fetch(own_row, 4 * f + c)
                    if c == 2:
                        parts[2] = parts[2] - slab_depth
                        parts[3] = parts[3] + slab_depth
                    got = [lane_gather(spread(p, 8), lane) for p in parts]
                    there = jnp.where(
                        block == 0,
                        got[0],
                        jnp.where(block == 1, got[1], jnp.where(block == 2, got[2], got[3])),
                    )
                    offset = there - own_row[:, cols]
                    offsets.append(offset)
                    geo_ref[f, c, s, :, cols] = offset
                    squares = offset * offset if squares is None else squares + offset * offset
                geo_ref[f, 3, s, :, cols] = jnp.sqrt(squares)
                parts = fetch(spec_ref[f : f + 1, :].astype(f32), 4 * f + 3)
                got = [lane_gather(spread(p, 8), lane) for p in parts]
                kind = jnp.where(
                    block == 0,
                    got[0],
                    jnp.where(block == 1, got[1], jnp.where(block == 2, got[2], got[3])),
                )
                kinds = (present * (1.0 - kind), present * kind)
                for k in range(2):
                    wgt_ref[k, s, :, cols] = kinds[k]
                    for c in range(3):
                        wgt_ref[2 * (c + 1) + k, s, :, cols] = offsets[c] * kinds[k]
        acc_ref[...] = jnp.zeros_like(acc_ref)

        def step(i, carry):
            acts = []
            for first in range(0, 8, GROUP):
                pre = mm(w1_ref[0], basis_rows(geo_ref, f, i, first, atoms))
                acts.append(silu(pre).astype(bf16).astype(f32))
            for half in range(atoms // LANES):
                cols = slice(half * LANES, (half + 1) * LANES)
                for part in range(0, hidden, 32):
                    hid = []
                    for j in range(8):
                        at = (j % GROUP) * hidden + part
                        hid.append(acts[j // GROUP][at : at + 32, cols])
                    for k in range(8):
                        total = acc_ref[k, part : part + 32, cols]
                        for j in range(8):
                            total = total + wgt_ref[k, i, j : j + 1, cols] * hid[j]
                        acc_ref[k, part : part + 32, cols] = total
            return carry

        lax.fori_loop(0, batches, step, 0, unroll=UN1)

        def project(k, w):
            total = acc_ref[k]
            high = total.astype(bf16)
            low = (total - high.astype(f32)).astype(bf16)
            return mm(w, jnp.concatenate([high, low], axis=0))

        cols0 = jnp.concatenate([kind_ref[2]] * 2, axis=1)
        cols1 = jnp.concatenate([kind_ref[3]] * 2, axis=1)
        scalar = scale * (cols0 * project(0, w2s) + cols1 * project(1, w2s))
        squared = None
        for c in range(3):
            vec = (scale * vector_scale) * (
                cols0 * project(2 * c + 2, w2v) + cols1 * project(2 * c + 3, w2v)
            )
            squared = vec * vec if squared is None else squared + vec * vec
        mixed = jnp.concatenate([scalar, squared], axis=0).astype(bf16)
        update = mm(wup_ref[0], mixed)
        e0 = jnp.concatenate([kind_ref[0]] * 2, axis=1)
        e1 = jnp.concatenate([kind_ref[1]] * 2, axis=1)
        features = jnp.where(spec_ref[f : f + 1, :] == 1, e1, e0) + silu(update)
        feat_ref[f] = features
        message = mm(wmsg_ref[...], features.astype(bf16)).astype(bf16)
        msg_ref[f] = message
        message = message.astype(f32)
        for side, out in ((0, down_ref), (1, up_ref)):
            index = halo_ref[f, side : side + 1, :]
            lane = spread(index & (LANES - 1), LANES)
            low_g = lane_gather(message[:, :LANES], lane)
            high_g = lane_gather(message[:, LANES:], lane)
            out[f] = jnp.where(index >= LANES, high_g, low_g).astype(bf16)


def hidden_kernel(geo_ref, nb_ref, w1_ref, w2_ref, out_ref):
    frames, batches, _, atoms = nb_ref.shape
    hidden = w2_ref.shape[2]
    for f in range(frames):

        def step(i, carry):
            for first in range(0, 8, GROUP):
                act = silu(mm(w1_ref[1], basis_rows(geo_ref, f, i, first, atoms)))
                for j in range(GROUP):
                    here = nb_ref[f, i, first + j : first + j + 1, :] >= 0
                    rows = slice(j * hidden, (j + 1) * hidden)
                    kept = jnp.where(here, act[rows], 0.0).astype(bf16)
                    out_ref[f, i, (first + j) * hidden : (first + j + 1) * hidden, :] = kept
            return carry

        lax.fori_loop(0, batches, step, 0, unroll=UNH)


def second_kernel(
    rows_each,
    live_ref,
    spec_ref,
    scalar_ref,
    nb_ref,
    geo_ref,
    hid_ref,
    feat_ref,
    msg_ref,
    below_ref,
    above_ref,
    w2_ref,
    wup_ref,
    wout_ref,
    struct_ref,
    energy_ref,
    chunk_ref,
    acc_ref,
    src_ref,
    pair_ref,
):
    frames, batches, _, atoms = nb_ref.shape
    slots = batches * 8
    hidden = w2_ref.shape[2]
    chunks = chunk_ref.shape[0]
    wout = jnp.concatenate([wout_ref[...]] * 2, axis=1)
    shift = [jnp.concatenate([scalar_ref[4 + k : 5 + k, :]] * 2, axis=1) for k in range(2)]
    scale = slots**-0.5
    extra = [None] * EXTRA
    for f in range(frames):
        src_ref[0] = msg_ref[f, :, :LANES]
        src_ref[1] = msg_ref[f, :, LANES:]
        src_ref[2] = below_ref[f]
        src_ref[3] = above_ref[f]
        halo = jnp.concatenate([below_ref[f, XLU:, :], above_ref[f, XLU:, :]], axis=1)
        pair_ref[...] = jnp.concatenate([msg_ref[f, XLU:, :], halo], axis=0)
        acc_ref[...] = jnp.zeros_like(acc_ref)

        def step(i, carry):
            filters = [
                mm(w2_ref[1], hid_ref[f, i, j * hidden : (j + 1) * hidden, :]) for j in range(8)
            ]
            width = WIDTH
            if XLU < LANES:
                target = lax.broadcasted_iota(jnp.int32, (2 * LANES, atoms), 0).astype(bf16)
                found = []
                for j in range(8):
                    want = (nb_ref[f, i, j : j + 1, :] & (2 * LANES - 1)).astype(f32).astype(bf16)
                    hot = jnp.where(target == want, jnp.asarray(1, bf16), jnp.asarray(0, bf16))
                    found.append(mm(pair_ref[...], hot))
            for half in range(atoms // LANES):
                cols = slice(half * LANES, (half + 1) * LANES)
                index = [nb_ref[f, i, j : j + 1, cols] for j in range(8)]
                lane = [spread(v & (LANES - 1), width).astype(jnp.int16) for v in index]
                block = [spread(v >> 7, width) for v in index]
                block16 = [v.astype(jnp.int16) for v in block]
                offset = [[geo_ref[f, c, i, j : j + 1, cols] for c in range(3)] for j in range(8)]
                for part in range(0, LANES, width):
                    rows = slice(part, part + width)
                    total = [acc_ref[k, rows, cols] for k in range(4)]
                    for j in range(8):
                        if part < XLU:
                            got = [lane_gather(src_ref[b, rows, :], lane[j]) for b in range(4)]
                            there = jnp.where(
                                block16[j] < 2,
                                jnp.where(block16[j] == 1, got[1], got[0]),
                                jnp.where(block16[j] == 2, got[2], got[3]),
                            ).astype(f32)
                        else:
                            at = part - XLU
                            there = jnp.where(
                                block[j] < 2,
                                found[j][at : at + width, cols],
                                found[j][LANES - XLU + at : LANES - XLU + at + width, cols],
                            )
                        total[0] = total[0] + filters[j][rows, cols] * there
                        vec = filters[j][LANES + part : LANES + part + width, cols] * there
                        for c in range(3):
                            total[c + 1] = total[c + 1] + offset[j][c] * vec
                    for k in range(4):
                        acc_ref[k, rows, cols] = total[k]
            return carry

        lax.fori_loop(0, batches, step, 0, unroll=UN2)

        scalar = scale * acc_ref[0]
        squared = None
        for c in range(3):
            vec = (scale * vector_scale) * acc_ref[c + 1]
            squared = vec * vec if squared is None else squared + vec * vec
        mixed = jnp.concatenate([scalar, squared], axis=0).astype(bf16)
        update = mm(wup_ref[1], mixed)
        gate = sigmoid(update)
        features = feat_ref[f] + update * gate
        living = live_ref[f : f + 1, :]
        slope = (living * wout * (gate * (1.0 + update * (1.0 - gate)))).astype(bf16)
        kind = spec_ref[f : f + 1, :]
        readout = jnp.sum(features * wout, axis=0, keepdims=True)
        energy = living * (readout + jnp.where(kind == 1, shift[1], shift[0]))
        energy_ref[f : f + 1, :] = energy
        grad = lax.dot_general(mixed, slope, (((1,), (1,)), ((), ())), preferred_element_type=f32)
        chunk_ref[:, f * rows_each : (f + 1) * rows_each, :] = grad.reshape(
            chunks, rows_each, LANES
        )
        extra[f] = as_row(jnp.sum(living * features, axis=1, keepdims=True))
        extra[2 + f] = struct_ref[2 + f : 3 + f, :]
        extra[4 + f] = struct_ref[4 + f : 5 + f, :]
        extra[6 + f] = jnp.broadcast_to(jnp.sum(energy, axis=1, keepdims=True), (1, LANES))
    block = jnp.concatenate(extra, axis=0)
    chunk_ref[:, frames * rows_each :, :] = jnp.broadcast_to(block[None], (chunks, EXTRA, LANES))


def total_kernel(scalar_ref, in_ref, out_ref):
    rows = in_ref.shape[1]
    total = in_ref[0]
    for s in range(1, in_ref.shape[0]):
        total = total + in_ref[s]
    for d in range(out_ref.shape[0]):
        out_ref[d] = total
    for f in range(2):
        row = total[rows - 2 + f : rows - 1 + f]
        log_weight = -scalar_ref[2 + f : 3 + f, :] * (row - scalar_ref[f : f + 1, :])
        for d in range(out_ref.shape[0]):
            out_ref[d, rows - 2 + f : rows - 1 + f, :] = log_weight


def final_kernel(
    rows_each, atoms_all, scalar_ref, in_ref, target_ref, chunk_ref, mean_ref, out_ref
):
    devices = in_ref.shape[0]
    q = target_ref.shape[1]
    base = 2 * rows_each

    def gather(at):
        return jnp.concatenate([in_ref[d, base + at : base + at + 2, :] for d in range(devices)], 0)

    cos_tot, sin_tot, log_weight = gather(2), gather(4), gather(6)
    structure = ((cos_tot * cos_tot + sin_tot * sin_tot) / atoms_all)[:, :q]
    scaled = jnp.exp(log_weight - jnp.max(log_weight, axis=0, keepdims=True))
    weights = scaled / jnp.sum(scaled, axis=0, keepdims=True)
    mean = jnp.sum(weights[:, :q] * structure, axis=0, keepdims=True)
    slope_sq = (mean - target_ref[...]) / target_var
    observed = jnp.sum(structure * slope_sq, axis=1, keepdims=True)
    average = jnp.sum(mean * slope_sq, axis=1, keepdims=True)
    factor = -scalar_ref[2:3, :] * weights * (observed - average)
    grad = jnp.zeros((rows_each, LANES), f32)
    for d in range(devices):
        for f in range(2):
            k = 2 * d + f
            grad = grad + factor[k : k + 1] * in_ref[d, f * rows_each : (f + 1) * rows_each, :]
    mean_ref[...] = mean
    out_ref[...] = jnp.sum(factor * gather(0), axis=0, keepdims=True)
    for s in range(chunk_ref.shape[0]):
        chunk_ref[s] = grad


VM = pl.BlockSpec(memory_space=pltpu.VMEM)
SM = pl.BlockSpec(memory_space=pltpu.SMEM)
HB = pl.BlockSpec(memory_space=pltpu.HBM)


def call(kernel, name, ins, outs, scratch, *operands):
    return pl.pallas_call(
        kernel,
        name=name,
        out_shape=outs,
        in_specs=ins,
        out_specs=jax.tree.map(lambda _: VM, outs),
        scratch_shapes=scratch,
        compiler_params=pltpu.CompilerParams(vmem_limit_bytes=VMEM_BYTES),
    )(*operands)


def in_hbm(value):
    return pltpu.with_memory_space_constraint(value, pltpu.HBM)


def array(shape, dtype=f32):
    return jax.ShapeDtypeStruct(shape, dtype)


def per_device(
    positions,
    species,
    atom_count,
    halo_index,
    neighbours,
    embedding,
    w_msg,
    w_rad1,
    w_rad2,
    w_up,
    w_out,
    e_shift,
    u_reference,
    inverse_temp,
    q_vectors,
    s_target,
):
    frames, _, atoms = positions.shape
    slots = neighbours.shape[1]
    halo = halo_index.shape[2]
    hidden = w_rad1.shape[2]
    channels = w_msg.shape[1]
    neighbours = neighbours.reshape(frames, slots // 8, 8, atoms)
    positions = positions.transpose(1, 0, 2)
    slab_devs = lax.axis_size("slab")
    frame_devs = lax.axis_size("frame")
    rows_each = 2 * channels // slab_devs
    chunk_rows = frames * rows_each + EXTRA
    up = [(i, (i + 1) % slab_devs) for i in range(slab_devs)]
    down = [(j, i) for i, j in up]

    basis = w_rad1.shape[1]
    rows = array((4 * frames, halo))
    leave_down, leave_up, positions, species, halo_index = call(
        pack_kernel,
        "halo_rows",
        [HB] * 3,
        (
            rows,
            rows,
            array(positions.shape),
            array(species.shape, jnp.int32),
            array(halo_index.shape, jnp.int32),
        ),
        [pltpu.SemaphoreType.DMA((3,))],
        *map(in_hbm, (positions, species, halo_index)),
    )
    below = lax.ppermute(leave_up, "slab", up)
    above = lax.ppermute(leave_down, "slab", down)
    q = s_target.shape[0]
    small = (
        u_reference.reshape(1, frames),
        e_shift.reshape(1, 2),
        atom_count.reshape(1, frames),
        q_vectors,
        embedding,
        w_msg,
        w_rad1,
        w_rad2,
        w_up,
        w_out.reshape(1, channels),
    )
    neighbours, w1, w2, wup, wmsg, kinds, wout, structure, living, scalars, target = call(
        stage_kernel,
        "staged_inputs",
        [SM, SM, VM, VM] + [HB] * 12,
        (
            array(neighbours.shape, jnp.int32),
            array((2, GROUP * hidden, GROUP * basis), bf16),
            array((2, 2 * channels, hidden), bf16),
            array((2, channels, 2 * channels), bf16),
            array((channels, channels), bf16),
            array((4, channels, LANES)),
            array((channels, LANES)),
            array((EXTRA, LANES)),
            array((frames, atoms)),
            array((8, LANES)),
            array((1, q)),
        ),
        [pltpu.VMEM(w.shape, w.dtype) for w in small] + [pltpu.SemaphoreType.DMA((12,))],
        lax.axis_index("slab").reshape(1),
        inverse_temp,
        positions,
        species,
        in_hbm(neighbours),
        in_hbm(s_target.reshape(1, q)),
        *map(in_hbm, small),
    )
    halo_rows = array((frames, channels, halo), bf16)
    geometry, features, message, msg_down, msg_up = call(
        first_kernel,
        "first_layer",
        [VM] * 11,
        (
            array((frames, 4, slots // 8, 8, atoms)),
            array((frames, channels, atoms)),
            array((frames, channels, atoms), bf16),
            halo_rows,
            halo_rows,
        ),
        [pltpu.VMEM((8, slots // 8, 8, atoms), f32), pltpu.VMEM((8, hidden, atoms), f32)],
        positions,
        species,
        below,
        above,
        neighbours,
        halo_index,
        w1,
        w2,
        wup,
        wmsg,
        kinds,
    )
    msg_below = lax.ppermute(msg_up, "slab", up)
    msg_above = lax.ppermute(msg_down, "slab", down)
    radial_hidden = call(
        hidden_kernel,
        "radial_hidden",
        [VM] * 4,
        array((frames, slots // 8, 8 * hidden, atoms), bf16),
        [],
        geometry,
        neighbours,
        w1,
        w2,
    )
    atom_energy, chunks = call(
        functools.partial(second_kernel, rows_each),
        "second_layer",
        [VM] * 14,
        (array((frames, atoms)), array((slab_devs, chunk_rows, LANES))),
        [
            pltpu.VMEM((4, channels, atoms), f32),
            pltpu.VMEM((4, channels, LANES), bf16),
            pltpu.VMEM((2 * (LANES - XLU), 2 * LANES), bf16),
        ],
        living,
        species,
        scalars,
        neighbours,
        geometry,
        radial_hidden,
        features,
        message,
        msg_below,
        msg_above,
        w2,
        wup,
        wout,
        structure,
    )
    chunks = lax.all_to_all(chunks, "slab", 0, 0, tiled=True)
    totals = call(
        total_kernel,
        "slab_totals",
        [VM, VM],
        array((frame_devs, chunk_rows, LANES)),
        [],
        scalars,
        chunks,
    )
    totals = lax.all_to_all(totals, "frame", 0, 0, tiled=True)
    grad_rows, mean_structure, grad_out = call(
        functools.partial(final_kernel, rows_each, atoms * slab_devs),
        "reweighted",
        [VM] * 3,
        (array((slab_devs, rows_each, LANES)), array((1, q)), array((1, channels))),
        [],
        scalars,
        totals,
        target,
    )
    grad_up = lax.all_to_all(grad_rows, "slab", 0, 0, tiled=True)
    return (
        atom_energy,
        mean_structure.reshape(q),
        grad_up.reshape(2 * channels, channels),
        grad_out.reshape(channels),
    )


def solution(mesh):
    in_specs = (
        P("frame", None, "slab"),
        P("frame", "slab"),
        P("frame", "slab"),
        P("frame", None, "slab"),
        P("frame", None, "slab"),
        P(),
        P(),
        P(),
        P(),
        P(),
        P(),
        P(),
        P("frame"),
        P(),
        P(),
        P(),
    )
    out_specs = (P("frame", "slab"), P(), P(), P())
    return jax.shard_map(
        per_device, mesh=mesh, in_specs=in_specs, out_specs=out_specs, check_vma=False
    )
```

```python
import functools

import jax
import jax.numpy as jnp
from jax import lax
from jax.experimental import pallas as pl
from jax.experimental.pallas import tpu as pltpu
from jax.sharding import PartitionSpec as P

slab_depth = 6.0
vector_scale = 0.2
target_var = 0.01
hydrogen_length = -0.64
LANES = 128
GROUP = 4
EXTRA = 8
EMPTY = 1.0e4
XLU = 32
UN1 = 6
UNH = 3
UN2 = 2
WIDTH = 32
VMEM_BYTES = 48 * 1024 * 1024

f32 = jnp.float32
bf16 = jnp.bfloat16


def lane_gather(table, index):
    numbers = lax.GatherDimensionNumbers(
        offset_dims=(),
        collapsed_slice_dims=(1,),
        start_index_map=(1,),
        operand_batching_dims=(0,),
        start_indices_batching_dims=(0,),
    )
    return lax.gather(
        table,
        index[..., None],
        numbers,
        slice_sizes=(1, 1),
        mode=lax.GatherScatterMode.PROMISE_IN_BOUNDS,
    )


def spread(row, rows):
    return jnp.broadcast_to(row, (rows, row.shape[1]))


def column(row):
    return spread(row, LANES).T


def as_row(col):
    wide = jnp.broadcast_to(col, (col.shape[0], LANES))
    if col.shape[0] < LANES:
        wide = jnp.concatenate([wide, jnp.zeros((LANES - col.shape[0], LANES), f32)], axis=0)
    return wide.T[0:1]


def sigmoid(values):
    return 0.5 * (1.0 + jnp.tanh(0.5 * values))


def silu(values):
    half = 0.5 * values
    return half + half * jnp.tanh(half)


def mm(a, b):
    return jnp.dot(a, b, preferred_element_type=f32)


def rad1_blocks(w_rad1):
    basis, hidden = w_rad1.shape
    w = w_rad1.astype(f32)
    wide = jnp.concatenate([w] * GROUP, axis=1)
    tall = jnp.concatenate([wide] * GROUP, axis=0)
    row = lax.broadcasted_iota(jnp.int32, tall.shape, 0) // basis
    col = lax.broadcasted_iota(jnp.int32, tall.shape, 1) // hidden
    tall = jnp.where(row == col, tall, 0.0)
    tall = jnp.concatenate([tall, jnp.zeros((LANES - GROUP * basis, GROUP * hidden), f32)], axis=0)
    return tall.T[:, : GROUP * basis].astype(bf16)


def transposed(w):
    return w.astype(f32).T.astype(bf16)


def fetch_all(sems, pairs):
    copies = [pltpu.make_async_copy(src, dst, sems.at[i]) for i, (src, dst) in enumerate(pairs)]
    for copy in copies:
        copy.start()
    return copies


def pack_kernel(pos_hbm, spec_hbm, halo_hbm, down_ref, up_ref, pos_ref, spec_ref, halo_ref, sems):
    pairs = ((pos_hbm, pos_ref), (spec_hbm, spec_ref), (halo_hbm, halo_ref))
    for copy in fetch_all(sems, pairs):
        copy.wait()
    frames = spec_ref.shape[0]
    for f in range(frames):
        rows = [pos_ref[c, f : f + 1, :] for c in range(3)]
        rows.append(spec_ref[f : f + 1, :].astype(f32))
        for side, out in ((0, down_ref), (1, up_ref)):
            index = halo_ref[f, side : side + 1, :]
            lane = spread(index & (LANES - 1), 8)
            high = spread(index, 8) >= LANES
            for c, row in enumerate(rows):
                low_g = lane_gather(spread(row[:, :LANES], 8), lane)
                high_g = lane_gather(spread(row[:, LANES:], 8), lane)
                out[4 * f + c : 4 * f + c + 1, :] = jnp.where(high, high_g, low_g)[0:1]


def stage_kernel(
    beta_ref,
    nb_hbm,
    emb_hbm,
    wmsg_hbm,
    wr1_hbm,
    wr2_hbm,
    wup_hbm,
    nb_ref,
    w1_ref,
    w2_ref,
    wup_ref,
    wmsg_ref,
    kind_ref,
    temp_ref,
    emb_in,
    wmsg_in,
    wr1_in,
    wr2_in,
    wup_in,
    sems,
):
    pairs = (
        (nb_hbm, nb_ref),
        (wr1_hbm, wr1_in),
        (wr2_hbm.at[0], wr2_in),
        (wup_hbm.at[0], wup_in),
        (wmsg_hbm, wmsg_in),
        (emb_hbm, emb_in),
    )
    copies = fetch_all(sems, pairs)
    temp_ref[...] = jnp.full((1, LANES), beta_ref[0], f32)
    for copy in copies:
        copy.wait()
    for layer in range(2):
        w1_ref[layer] = rad1_blocks(wr1_in[layer])
    w2_ref[...] = transposed(wr2_in[...])
    wup_ref[...] = transposed(wup_in[...])
    wmsg_ref[...] = transposed(wmsg_in[1])
    emb = emb_in[...]
    table = mm(emb, wmsg_in[0]).astype(bf16).astype(f32)
    for k in range(2):
        kind_ref[k] = column(emb[k : k + 1].astype(f32))
        kind_ref[2 + k] = column(table[k : k + 1])


def basis_rows(dist_ref, f, i, first, atoms):
    center = lax.broadcasted_iota(jnp.int32, (8, atoms), 0).astype(f32)
    parts = []
    for j in range(first, first + GROUP):
        off = spread(dist_ref[f, 3, i, j : j + 1, :], 8) - center
        parts.append(jnp.exp(-(off * off)))
    return jnp.concatenate(parts, axis=0).astype(bf16)


def first_kernel(
    pos_ref,
    spec_ref,
    below_ref,
    above_ref,
    nb_ref,
    halo_ref,
    w1_ref,
    w2_ref,
    wup_ref,
    wmsg_ref,
    kind_ref,
    geo_ref,
    feat_ref,
    msg_ref,
    down_ref,
    up_ref,
    wgt_ref,
    acc_ref,
):
    _, frames, atoms = pos_ref.shape
    batches = nb_ref.shape[1]
    slots = batches * 8
    hidden = w2_ref.shape[1]
    w2s = jnp.concatenate([w2_ref[:LANES, :]] * 2, axis=1)
    w2v = jnp.concatenate([w2_ref[LANES:, :]] * 2, axis=1)
    scale = slots**-0.5
    for f in range(frames):
        for half in range(atoms // LANES):
            cols = slice(half * LANES, (half + 1) * LANES)
            for s in range(batches):
                index = nb_ref[f, s, :, cols]
                lane = index & (LANES - 1)
                block = index >> 7

                def fetch(own_row, halo_row):
                    parts = [
                        own_row[:, :LANES],
                        own_row[:, LANES:],
                        below_ref[halo_row : halo_row + 1, :],
                        above_ref[halo_row : halo_row + 1, :],
                    ]
                    return parts

                squares = None
                offsets = []
                for c in range(3):
                    own_row = pos_ref[c, f : f + 1, :]
                    parts = fetch(own_row, 4 * f + c)
                    if c == 2:
                        parts[2] = parts[2] - slab_depth
                        parts[3] = parts[3] + slab_depth
                    got = [lane_gather(spread(p, 8), lane) for p in parts]
                    there = jnp.where(
                        block == 0,
                        got[0],
                        jnp.where(block == 1, got[1], jnp.where(block == 2, got[2], got[3])),
                    )
                    offset = there - own_row[:, cols]
                    offsets.append(offset)
                    geo_ref[f, c, s, :, cols] = offset
                    squares = offset * offset if squares is None else squares + offset * offset
                geo_ref[f, 3, s, :, cols] = jnp.where(index >= 0, jnp.sqrt(squares), EMPTY)
                parts = fetch(spec_ref[f : f + 1, :].astype(f32), 4 * f + 3)
                got = [lane_gather(spread(p, 8), lane) for p in parts]
                kind = jnp.where(
                    block == 0,
                    got[0],
                    jnp.where(block == 1, got[1], jnp.where(block == 2, got[2], got[3])),
                )
                wgt_ref[0, s, :, cols] = kind
                for c in range(3):
                    wgt_ref[2 * c + 1, s, :, cols] = offsets[c] * (1.0 - kind)
                    wgt_ref[2 * c + 2, s, :, cols] = offsets[c] * kind
        acc_ref[...] = jnp.zeros_like(acc_ref)

        def step(i, carry):
            acts = []
            for first in range(0, 8, GROUP):
                pre = mm(w1_ref[0], basis_rows(geo_ref, f, i, first, atoms))
                acts.append(silu(pre).astype(bf16).astype(f32))
            for half in range(atoms // LANES):
                cols = slice(half * LANES, (half + 1) * LANES)
                for part in range(0, hidden, 32):
                    hid = []
                    for j in range(8):
                        at = (j % GROUP) * hidden + part
                        hid.append(acts[j // GROUP][at : at + 32, cols])
                    total = hid[0]
                    for j in range(1, 8):
                        total = total + hid[j]
                    acc_ref[0, part : part + 32, cols] += total
                    for k in range(7):
                        total = acc_ref[k + 1, part : part + 32, cols]
                        for j in range(8):
                            total = total + wgt_ref[k, i, j : j + 1, cols] * hid[j]
                        acc_ref[k + 1, part : part + 32, cols] = total
            return carry

        lax.fori_loop(0, batches, step, 0, unroll=UN1)

        acc_ref[0] = acc_ref[0] - acc_ref[1]

        def project(k, w):
            total = acc_ref[k]
            high = total.astype(bf16)
            low = (total - high.astype(f32)).astype(bf16)
            return mm(w, jnp.concatenate([high, low], axis=0))

        cols0 = jnp.concatenate([kind_ref[2]] * 2, axis=1)
        cols1 = jnp.concatenate([kind_ref[3]] * 2, axis=1)
        scalar = scale * (cols0 * project(0, w2s) + cols1 * project(1, w2s))
        squared = None
        for c in range(3):
            vec = (scale * vector_scale) * (
                cols0 * project(2 * c + 2, w2v) + cols1 * project(2 * c + 3, w2v)
            )
            squared = vec * vec if squared is None else squared + vec * vec
        mixed = jnp.concatenate([scalar, squared], axis=0).astype(bf16)
        update = mm(wup_ref[...], mixed)
        e0 = jnp.concatenate([kind_ref[0]] * 2, axis=1)
        e1 = jnp.concatenate([kind_ref[1]] * 2, axis=1)
        features = jnp.where(spec_ref[f : f + 1, :] == 1, e1, e0) + silu(update)
        feat_ref[f] = features
        message = mm(wmsg_ref[...], features.astype(bf16)).astype(bf16)
        msg_ref[f] = message
        message = message.astype(f32)
        for side, out in ((0, down_ref), (1, up_ref)):
            index = halo_ref[f, side : side + 1, :]
            lane = spread(index & (LANES - 1), LANES)
            low_g = lane_gather(message[:, :LANES], lane)
            high_g = lane_gather(message[:, LANES:], lane)
            out[f] = jnp.where(index >= LANES, high_g, low_g).astype(bf16)


def hidden_kernel(
    slab_ref,
    geo_ref,
    w1_ref,
    temp_ref,
    pos_ref,
    spec_ref,
    target_hbm,
    uref_hbm,
    eshift_hbm,
    count_hbm,
    q_hbm,
    wr2_hbm,
    wup_hbm,
    wout_hbm,
    out_ref,
    w2_ref,
    wup_ref,
    wout_ref,
    struct_ref,
    live_ref,
    scalar_ref,
    target_ref,
    uref_in,
    eshift_in,
    count_in,
    q_in,
    wr2_in,
    wup_in,
    wout_in,
    sems,
):
    pairs = (
        (target_hbm, target_ref),
        (uref_hbm, uref_in),
        (eshift_hbm, eshift_in),
        (count_hbm, count_in),
        (q_hbm, q_in),
        (wr2_hbm.at[1], wr2_in),
        (wup_hbm.at[1], wup_in),
        (wout_hbm, wout_in),
    )
    copies = fetch_all(sems, pairs)
    _, frames, atoms = pos_ref.shape
    batches = geo_ref.shape[2]
    hidden = wr2_in.shape[0]
    for f in range(frames):

        def step(i, carry):
            for first in range(0, 8, GROUP):
                act = silu(mm(w1_ref[1], basis_rows(geo_ref, f, i, first, atoms)))
                out_ref[f, i, first * hidden : (first + GROUP) * hidden, :] = act.astype(bf16)
            return carry

        lax.fori_loop(0, batches, step, 0, unroll=UNH)
    for copy in copies:
        copy.wait()
    number_q = q_in.shape[1]
    same = lax.broadcasted_iota(jnp.int32, (number_q, number_q), 0) == lax.broadcasted_iota(
        jnp.int32, (number_q, number_q), 1
    )
    q = [
        jnp.sum(jnp.where(same, spread(q_in[c : c + 1, :], number_q), 0.0), axis=1, keepdims=True)
        for c in range(3)
    ]
    lift = slab_ref[0].astype(f32) * slab_depth
    number = lax.broadcasted_iota(jnp.int32, (1, atoms), 1)
    struct_ref[...] = jnp.zeros_like(struct_ref)
    for f in range(frames):
        x, y, z = (pos_ref[c, f : f + 1, :] for c in range(3))
        phases = q[0] * x + q[1] * y + q[2] * (z + lift)
        lengths = jnp.where(spec_ref[f : f + 1, :] == 1, 1.0, hydrogen_length)
        living = (number < count_in[:, f : f + 1]).astype(f32)
        live_ref[f : f + 1, :] = living
        lengths = living * lengths
        cos_part = jnp.sum(lengths * jnp.cos(phases), axis=1, keepdims=True)
        sin_part = jnp.sum(lengths * jnp.sin(phases), axis=1, keepdims=True)
        struct_ref[2 + f : 3 + f, :] = as_row(cos_part)
        struct_ref[4 + f : 5 + f, :] = as_row(sin_part)
    w2_ref[...] = transposed(wr2_in[...])
    wup_ref[...] = transposed(wup_in[...])
    wout_ref[...] = column(wout_in[...])
    for k in range(2):
        scalar_ref[k : k + 1, :] = jnp.broadcast_to(uref_in[:, k : k + 1], (1, LANES))
        scalar_ref[2 + k : 3 + k, :] = temp_ref[...]
        scalar_ref[4 + k : 5 + k, :] = jnp.broadcast_to(eshift_in[:, k : k + 1], (1, LANES))
    scalar_ref[6:8, :] = jnp.zeros((2, LANES), f32)


def second_kernel(
    rows_each,
    live_ref,
    spec_ref,
    scalar_ref,
    nb_ref,
    geo_ref,
    hid_ref,
    feat_ref,
    msg_ref,
    below_ref,
    above_ref,
    w2_ref,
    wup_ref,
    wout_ref,
    struct_ref,
    energy_hbm,
    chunk_ref,
    acc_ref,
    src_ref,
    pair_ref,
    energy_ref,
    sem,
):
    frames, batches, _, atoms = nb_ref.shape
    slots = batches * 8
    hidden = w2_ref.shape[1]
    chunks = chunk_ref.shape[0]
    wout = jnp.concatenate([wout_ref[...]] * 2, axis=1)
    shift = [jnp.concatenate([scalar_ref[4 + k : 5 + k, :]] * 2, axis=1) for k in range(2)]
    scale = slots**-0.5
    extra = [None] * EXTRA
    for f in range(frames):
        src_ref[0] = msg_ref[f, :, :LANES]
        src_ref[1] = msg_ref[f, :, LANES:]
        src_ref[2] = below_ref[f]
        src_ref[3] = above_ref[f]
        halo = jnp.concatenate([below_ref[f, XLU:, :], above_ref[f, XLU:, :]], axis=1)
        pair_ref[...] = jnp.concatenate([msg_ref[f, XLU:, :], halo], axis=0)
        acc_ref[...] = jnp.zeros_like(acc_ref)

        def step(i, carry):
            filters = [
                mm(w2_ref[...], hid_ref[f, i, j * hidden : (j + 1) * hidden, :]) for j in range(8)
            ]
            width = WIDTH
            if XLU < LANES:
                target = lax.broadcasted_iota(jnp.int32, (2 * LANES, atoms), 0).astype(bf16)
                found = []
                for j in range(8):
                    want = (nb_ref[f, i, j : j + 1, :] & (2 * LANES - 1)).astype(f32).astype(bf16)
                    hot = jnp.where(target == want, jnp.asarray(1, bf16), jnp.asarray(0, bf16))
                    found.append(mm(pair_ref[...], hot))
            for half in range(atoms // LANES):
                cols = slice(half * LANES, (half + 1) * LANES)
                index = [nb_ref[f, i, j : j + 1, cols] for j in range(8)]
                lane = [spread(v & (LANES - 1), width).astype(jnp.int16) for v in index]
                block = [spread(v >> 7, width) for v in index]
                block16 = [v.astype(jnp.int16) for v in block]
                offset = [[geo_ref[f, c, i, j : j + 1, cols] for c in range(3)] for j in range(8)]
                for part in range(0, LANES, width):
                    rows = slice(part, part + width)
                    total = [acc_ref[k, rows, cols] for k in range(4)]
                    for j in range(8):
                        if part < XLU:
                            got = [lane_gather(src_ref[b, rows, :], lane[j]) for b in range(4)]
                            there = jnp.where(
                                block16[j] < 2,
                                jnp.where(block16[j] == 1, got[1], got[0]),
                                jnp.where(block16[j] == 2, got[2], got[3]),
                            ).astype(f32)
                        else:
                            at = part - XLU
                            there = jnp.where(
                                block[j] < 2,
                                found[j][at : at + width, cols],
                                found[j][LANES - XLU + at : LANES - XLU + at + width, cols],
                            )
                        total[0] = total[0] + filters[j][rows, cols] * there
                        vec = filters[j][LANES + part : LANES + part + width, cols] * there
                        for c in range(3):
                            total[c + 1] = total[c + 1] + offset[j][c] * vec
                    for k in range(4):
                        acc_ref[k, rows, cols] = total[k]
            return carry

        lax.fori_loop(0, batches, step, 0, unroll=UN2)

        scalar = scale * acc_ref[0]
        squared = None
        for c in range(3):
            vec = (scale * vector_scale) * acc_ref[c + 1]
            squared = vec * vec if squared is None else squared + vec * vec
        mixed = jnp.concatenate([scalar, squared], axis=0).astype(bf16)
        update = mm(wup_ref[...], mixed)
        gate = sigmoid(update)
        features = feat_ref[f] + update * gate
        living = live_ref[f : f + 1, :]
        slope = (living * wout * (gate * (1.0 + update * (1.0 - gate)))).astype(bf16)
        kind = spec_ref[f : f + 1, :]
        readout = jnp.sum(features * wout, axis=0, keepdims=True)
        energy = living * (readout + jnp.where(kind == 1, shift[1], shift[0]))
        energy_ref[f : f + 1, :] = energy
        if f == frames - 1:
            leaving = pltpu.make_async_copy(energy_ref, energy_hbm, sem)
            leaving.start()
        grad = lax.dot_general(mixed, slope, (((1,), (1,)), ((), ())), preferred_element_type=f32)
        chunk_ref[:, f * rows_each : (f + 1) * rows_each, :] = grad.reshape(
            chunks, rows_each, LANES
        )
        extra[f] = as_row(jnp.sum(living * features, axis=1, keepdims=True))
        extra[2 + f] = struct_ref[2 + f : 3 + f, :]
        extra[4 + f] = struct_ref[4 + f : 5 + f, :]
        extra[6 + f] = jnp.broadcast_to(jnp.sum(energy, axis=1, keepdims=True), (1, LANES))
    block = jnp.concatenate(extra, axis=0)
    chunk_ref[:, frames * rows_each :, :] = jnp.broadcast_to(block[None], (chunks, EXTRA, LANES))
    leaving.wait()


def total_kernel(scalar_ref, in_ref, out_ref):
    rows = in_ref.shape[1]
    total = in_ref[0]
    for s in range(1, in_ref.shape[0]):
        total = total + in_ref[s]
    for d in range(out_ref.shape[0]):
        out_ref[d] = total
    for f in range(2):
        row = total[rows - 2 + f : rows - 1 + f]
        log_weight = -scalar_ref[2 + f : 3 + f, :] * (row - scalar_ref[f : f + 1, :])
        for d in range(out_ref.shape[0]):
            out_ref[d, rows - 2 + f : rows - 1 + f, :] = log_weight


def final_kernel(
    rows_each, atoms_all, scalar_ref, in_ref, target_ref, chunk_ref, mean_ref, out_ref
):
    devices = in_ref.shape[0]
    q = target_ref.shape[1]
    base = 2 * rows_each

    def gather(at):
        return jnp.concatenate([in_ref[d, base + at : base + at + 2, :] for d in range(devices)], 0)

    cos_tot, sin_tot, log_weight = gather(2), gather(4), gather(6)
    structure = ((cos_tot * cos_tot + sin_tot * sin_tot) / atoms_all)[:, :q]
    scaled = jnp.exp(log_weight - jnp.max(log_weight, axis=0, keepdims=True))
    weights = scaled / jnp.sum(scaled, axis=0, keepdims=True)
    mean = jnp.sum(weights[:, :q] * structure, axis=0, keepdims=True)
    slope_sq = (mean - target_ref[...]) / target_var
    observed = jnp.sum(structure * slope_sq, axis=1, keepdims=True)
    average = jnp.sum(mean * slope_sq, axis=1, keepdims=True)
    factor = -scalar_ref[2:3, :] * weights * (observed - average)
    grad = jnp.zeros((rows_each, LANES), f32)
    for d in range(devices):
        for f in range(2):
            k = 2 * d + f
            grad = grad + factor[k : k + 1] * in_ref[d, f * rows_each : (f + 1) * rows_each, :]
    mean_ref[...] = mean
    out_ref[...] = jnp.sum(factor * gather(0), axis=0, keepdims=True)
    for s in range(chunk_ref.shape[0]):
        chunk_ref[s] = grad


VM = pl.BlockSpec(memory_space=pltpu.VMEM)
SM = pl.BlockSpec(memory_space=pltpu.SMEM)
HB = pl.BlockSpec(memory_space=pltpu.HBM)


def call(kernel, name, ins, outs, scratch, *operands, specs=None):
    return pl.pallas_call(
        kernel,
        name=name,
        out_shape=outs,
        in_specs=ins,
        out_specs=specs or jax.tree.map(lambda _: VM, outs),
        scratch_shapes=scratch,
        compiler_params=pltpu.CompilerParams(vmem_limit_bytes=VMEM_BYTES),
    )(*operands)


def in_hbm(value):
    return pltpu.with_memory_space_constraint(value, pltpu.HBM)


def array(shape, dtype=f32):
    return jax.ShapeDtypeStruct(shape, dtype)


def per_device(
    positions,
    species,
    atom_count,
    halo_index,
    neighbours,
    embedding,
    w_msg,
    w_rad1,
    w_rad2,
    w_up,
    w_out,
    e_shift,
    u_reference,
    inverse_temp,
    q_vectors,
    s_target,
):
    frames, _, atoms = positions.shape
    slots = neighbours.shape[1]
    halo = halo_index.shape[2]
    hidden = w_rad1.shape[2]
    channels = w_msg.shape[1]
    neighbours = neighbours.reshape(frames, slots // 8, 8, atoms)
    positions = positions.transpose(1, 0, 2)
    slab_devs = lax.axis_size("slab")
    frame_devs = lax.axis_size("frame")
    rows_each = 2 * channels // slab_devs
    chunk_rows = frames * rows_each + EXTRA
    up = [(i, (i + 1) % slab_devs) for i in range(slab_devs)]
    down = [(j, i) for i, j in up]

    basis = w_rad1.shape[1]
    rows = array((4 * frames, halo))
    leave_down, leave_up, positions, species, halo_index = call(
        pack_kernel,
        "halo_rows",
        [HB] * 3,
        (
            rows,
            rows,
            array(positions.shape),
            array(species.shape, jnp.int32),
            array(halo_index.shape, jnp.int32),
        ),
        [pltpu.SemaphoreType.DMA((3,))],
        *map(in_hbm, (positions, species, halo_index)),
    )
    below = lax.ppermute(leave_up, "slab", up)
    above = lax.ppermute(leave_down, "slab", down)
    q = s_target.shape[0]
    staged = (embedding, w_msg, w_rad1)
    halves = (array(w_rad2.shape[1:], bf16), array(w_up.shape[1:], bf16))
    neighbours, w1, w2, wup, wmsg, kinds, temp = call(
        stage_kernel,
        "staged_inputs",
        [SM] + [HB] * 6,
        (
            array(neighbours.shape, jnp.int32),
            array((2, GROUP * hidden, GROUP * basis), bf16),
            array((2 * channels, hidden), bf16),
            array((channels, 2 * channels), bf16),
            array((channels, channels), bf16),
            array((4, channels, LANES)),
            array((1, LANES)),
        ),
        [pltpu.VMEM(w.shape, w.dtype) for w in (*staged, *halves)]
        + [pltpu.SemaphoreType.DMA((6,))],
        inverse_temp,
        *map(in_hbm, (neighbours, *staged, w_rad2, w_up)),
    )
    halo_rows = array((frames, channels, halo), bf16)
    geometry, features, message, msg_down, msg_up = call(
        first_kernel,
        "first_layer",
        [VM] * 11,
        (
            array((frames, 4, slots // 8, 8, atoms)),
            array((frames, channels, atoms)),
            array((frames, channels, atoms), bf16),
            halo_rows,
            halo_rows,
        ),
        [pltpu.VMEM((7, slots // 8, 8, atoms), f32), pltpu.VMEM((8, hidden, atoms), f32)],
        positions,
        species,
        below,
        above,
        neighbours,
        halo_index,
        w1,
        w2,
        wup,
        wmsg,
        kinds,
    )
    msg_below = lax.ppermute(msg_up, "slab", up)
    msg_above = lax.ppermute(msg_down, "slab", down)
    small = (
        u_reference.reshape(1, frames),
        e_shift.reshape(1, 2),
        atom_count.reshape(1, frames),
        q_vectors,
    )
    wout_row = w_out.reshape(1, channels)
    radial_hidden, w2, wup, wout, structure, living, scalars, target = call(
        hidden_kernel,
        "radial_hidden",
        [SM] + [VM] * 5 + [HB] * 8,
        (
            array((frames, slots // 8, 8 * hidden, atoms), bf16),
            array((2 * channels, hidden), bf16),
            array((channels, 2 * channels), bf16),
            array((channels, LANES)),
            array((EXTRA, LANES)),
            array((frames, atoms)),
            array((8, LANES)),
            array((1, q)),
        ),
        [pltpu.VMEM(w.shape, w.dtype) for w in (*small, *halves, wout_row)]
        + [pltpu.SemaphoreType.DMA((8,))],
        lax.axis_index("slab").reshape(1),
        geometry,
        w1,
        temp,
        positions,
        species,
        *map(in_hbm, (s_target.reshape(1, q), *small, w_rad2, w_up, wout_row)),
    )
    atom_energy, chunks = call(
        functools.partial(second_kernel, rows_each),
        "second_layer",
        [VM] * 14,
        (array((frames, atoms)), array((slab_devs, chunk_rows, LANES))),
        [
            pltpu.VMEM((4, channels, atoms), f32),
            pltpu.VMEM((4, channels, LANES), bf16),
            pltpu.VMEM((2 * (LANES - XLU), 2 * LANES), bf16),
            pltpu.VMEM((frames, atoms), f32),
            pltpu.SemaphoreType.DMA,
        ],
        living,
        species,
        scalars,
        neighbours,
        geometry,
        radial_hidden,
        features,
        message,
        msg_below,
        msg_above,
        w2,
        wup,
        wout,
        structure,
        specs=(HB, VM),
    )
    chunks = lax.all_to_all(chunks, "slab", 0, 0, tiled=True)
    totals = call(
        total_kernel,
        "slab_totals",
        [VM, VM],
        array((frame_devs, chunk_rows, LANES)),
        [],
        scalars,
        chunks,
    )
    totals = lax.all_to_all(totals, "frame", 0, 0, tiled=True)
    grad_rows, mean_structure, grad_out = call(
        functools.partial(final_kernel, rows_each, atoms * slab_devs),
        "reweighted",
        [VM] * 3,
        (array((slab_devs, rows_each, LANES)), array((1, q)), array((1, channels))),
        [],
        scalars,
        totals,
        target,
    )
    grad_up = lax.all_to_all(grad_rows, "slab", 0, 0, tiled=True)
    return (
        atom_energy,
        mean_structure.reshape(q),
        grad_up.reshape(2 * channels, channels),
        grad_out.reshape(channels),
    )


def solution(mesh):
    in_specs = (
        P("frame", None, "slab"),
        P("frame", "slab"),
        P("frame", "slab"),
        P("frame", None, "slab"),
        P("frame", None, "slab"),
        P(),
        P(),
        P(),
        P(),
        P(),
        P(),
        P(),
        P("frame"),
        P(),
        P(),
        P(),
    )
    out_specs = (P("frame", "slab"), P(), P(), P())
    return jax.shard_map(
        per_device, mesh=mesh, in_specs=in_specs, out_specs=out_specs, check_vma=False
    )
```

```python
import functools

import jax
import jax.numpy as jnp
from jax import lax
from jax.experimental import pallas as pl
from jax.experimental.pallas import tpu as pltpu
from jax.sharding import PartitionSpec as P

slab_depth = 6.0
vector_scale = 0.2
target_var = 0.01
hydrogen_length = -0.64
LANES = 128
GROUP = 4
EXTRA = 8
EMPTY = 1.0e4
UN1 = 6
UNH = 3
UN2 = 3
WIDTH = 32
VMEM_BYTES = 48 * 1024 * 1024

f32 = jnp.float32
bf16 = jnp.bfloat16


def lane_gather(table, index):
    numbers = lax.GatherDimensionNumbers(
        offset_dims=(),
        collapsed_slice_dims=(1,),
        start_index_map=(1,),
        operand_batching_dims=(0,),
        start_indices_batching_dims=(0,),
    )
    return lax.gather(
        table,
        index[..., None],
        numbers,
        slice_sizes=(1, 1),
        mode=lax.GatherScatterMode.PROMISE_IN_BOUNDS,
    )


def spread(row, rows):
    return jnp.broadcast_to(row, (rows, row.shape[1]))


def column(row):
    return spread(row, LANES).T


def as_row(col):
    wide = jnp.broadcast_to(col, (col.shape[0], LANES))
    if col.shape[0] < LANES:
        wide = jnp.concatenate([wide, jnp.zeros((LANES - col.shape[0], LANES), f32)], axis=0)
    return wide.T[0:1]


def sigmoid(values):
    return 0.5 * (1.0 + jnp.tanh(0.5 * values))


def silu(values):
    half = 0.5 * values
    return half + half * jnp.tanh(half)


def mm(a, b):
    return jnp.dot(a, b, preferred_element_type=f32)


def rad1_blocks(w_rad1):
    basis, hidden = w_rad1.shape
    w = w_rad1.astype(f32)
    wide = jnp.concatenate([w] * GROUP, axis=1)
    tall = jnp.concatenate([wide] * GROUP, axis=0)
    row = lax.broadcasted_iota(jnp.int32, tall.shape, 0) // basis
    col = lax.broadcasted_iota(jnp.int32, tall.shape, 1) // hidden
    tall = jnp.where(row == col, tall, 0.0)
    tall = jnp.concatenate([tall, jnp.zeros((LANES - GROUP * basis, GROUP * hidden), f32)], axis=0)
    return tall.T[:, : GROUP * basis].astype(bf16)


def transposed(w):
    return w.astype(f32).T.astype(bf16)


def fetch_all(sems, pairs):
    copies = [pltpu.make_async_copy(src, dst, sems.at[i]) for i, (src, dst) in enumerate(pairs)]
    for copy in copies:
        copy.start()
    return copies


def pack_kernel(pos_hbm, spec_hbm, halo_hbm, down_ref, up_ref, pos_ref, spec_ref, halo_ref, sems):
    pairs = ((pos_hbm, pos_ref), (spec_hbm, spec_ref), (halo_hbm, halo_ref))
    for copy in fetch_all(sems, pairs):
        copy.wait()
    frames = spec_ref.shape[0]
    for f in range(frames):
        rows = [pos_ref[c, f : f + 1, :] for c in range(3)]
        rows.append(spec_ref[f : f + 1, :].astype(f32))
        for side, out in ((0, down_ref), (1, up_ref)):
            index = halo_ref[f, side : side + 1, :]
            lane = spread(index & (LANES - 1), 8)
            high = spread(index, 8) >= LANES
            for c, row in enumerate(rows):
                low_g = lane_gather(spread(row[:, :LANES], 8), lane)
                high_g = lane_gather(spread(row[:, LANES:], 8), lane)
                out[4 * f + c : 4 * f + c + 1, :] = jnp.where(high, high_g, low_g)[0:1]


def stage_kernel(
    beta_ref,
    nb_hbm,
    emb_hbm,
    wmsg_hbm,
    wr1_hbm,
    wr2_hbm,
    wup_hbm,
    nb_ref,
    w1_ref,
    w2_ref,
    wup_ref,
    wmsg_ref,
    kind_ref,
    temp_ref,
    emb_in,
    wmsg_in,
    wr1_in,
    wr2_in,
    wup_in,
    sems,
):
    pairs = (
        (nb_hbm, nb_ref),
        (wr1_hbm, wr1_in),
        (wr2_hbm.at[0], wr2_in),
        (wup_hbm.at[0], wup_in),
        (wmsg_hbm, wmsg_in),
        (emb_hbm, emb_in),
    )
    copies = fetch_all(sems, pairs)
    temp_ref[...] = jnp.full((1, LANES), beta_ref[0], f32)
    for copy in copies:
        copy.wait()
    for layer in range(2):
        w1_ref[layer] = rad1_blocks(wr1_in[layer])
    w2_ref[...] = transposed(wr2_in[...])
    wup_ref[...] = transposed(wup_in[...])
    wmsg_ref[...] = transposed(wmsg_in[1])
    emb = emb_in[...]
    table = mm(emb, wmsg_in[0]).astype(bf16).astype(f32)
    for k in range(2):
        kind_ref[k] = column(emb[k : k + 1].astype(f32))
        kind_ref[2 + k] = column(table[k : k + 1])


def basis_rows(dist_ref, f, i, first, atoms):
    center = lax.broadcasted_iota(jnp.int32, (8, atoms), 0).astype(f32)
    parts = []
    for j in range(first, first + GROUP):
        off = spread(dist_ref[f, 3, i, j : j + 1, :], 8) - center
        parts.append(jnp.exp(-(off * off)))
    return jnp.concatenate(parts, axis=0).astype(bf16)


def first_kernel(
    pos_ref,
    spec_ref,
    below_ref,
    above_ref,
    nb_ref,
    halo_ref,
    w1_ref,
    w2_ref,
    wup_ref,
    wmsg_ref,
    kind_ref,
    geo_ref,
    feat_ref,
    msg_ref,
    down_ref,
    up_ref,
    wgt_ref,
    acc_ref,
):
    _, frames, atoms = pos_ref.shape
    batches = nb_ref.shape[1]
    slots = batches * 8
    hidden = w2_ref.shape[1]
    w2s = jnp.concatenate([w2_ref[:LANES, :]] * 2, axis=1)
    w2v = jnp.concatenate([w2_ref[LANES:, :]] * 2, axis=1)
    scale = slots**-0.5
    for f in range(frames):
        for half in range(atoms // LANES):
            cols = slice(half * LANES, (half + 1) * LANES)
            for s in range(batches):
                index = nb_ref[f, s, :, cols]
                lane = index & (LANES - 1)
                block = index >> 7

                def fetch(own_row, halo_row):
                    parts = [
                        own_row[:, :LANES],
                        own_row[:, LANES:],
                        below_ref[halo_row : halo_row + 1, :],
                        above_ref[halo_row : halo_row + 1, :],
                    ]
                    return parts

                squares = None
                offsets = []
                for c in range(3):
                    own_row = pos_ref[c, f : f + 1, :]
                    parts = fetch(own_row, 4 * f + c)
                    if c == 2:
                        parts[2] = parts[2] - slab_depth
                        parts[3] = parts[3] + slab_depth
                    got = [lane_gather(spread(p, 8), lane) for p in parts]
                    there = jnp.where(
                        block == 0,
                        got[0],
                        jnp.where(block == 1, got[1], jnp.where(block == 2, got[2], got[3])),
                    )
                    offset = there - own_row[:, cols]
                    offsets.append(offset)
                    geo_ref[f, c, s, :, cols] = offset
                    squares = offset * offset if squares is None else squares + offset * offset
                geo_ref[f, 3, s, :, cols] = jnp.where(index >= 0, jnp.sqrt(squares), EMPTY)
                parts = fetch(spec_ref[f : f + 1, :].astype(f32), 4 * f + 3)
                got = [lane_gather(spread(p, 8), lane) for p in parts]
                kind = jnp.where(
                    block == 0,
                    got[0],
                    jnp.where(block == 1, got[1], jnp.where(block == 2, got[2], got[3])),
                )
                wgt_ref[0, s, :, cols] = kind
                for c in range(3):
                    wgt_ref[2 * c + 1, s, :, cols] = offsets[c] * (1.0 - kind)
                    wgt_ref[2 * c + 2, s, :, cols] = offsets[c] * kind
        acc_ref[...] = jnp.zeros_like(acc_ref)

        def step(i, carry):
            acts = []
            for first in range(0, 8, GROUP):
                pre = mm(w1_ref[0], basis_rows(geo_ref, f, i, first, atoms))
                acts.append(silu(pre).astype(bf16).astype(f32))
            for half in range(atoms // LANES):
                cols = slice(half * LANES, (half + 1) * LANES)
                for part in range(0, hidden, 32):
                    hid = []
                    for j in range(8):
                        at = (j % GROUP) * hidden + part
                        hid.append(acts[j // GROUP][at : at + 32, cols])
                    total = hid[0]
                    for j in range(1, 8):
                        total = total + hid[j]
                    acc_ref[0, part : part + 32, cols] += total
                    for k in range(7):
                        total = acc_ref[k + 1, part : part + 32, cols]
                        for j in range(8):
                            total = total + wgt_ref[k, i, j : j + 1, cols] * hid[j]
                        acc_ref[k + 1, part : part + 32, cols] = total
            return carry

        lax.fori_loop(0, batches, step, 0, unroll=UN1)

        acc_ref[0] = acc_ref[0] - acc_ref[1]

        def project(k, w):
            total = acc_ref[k]
            high = total.astype(bf16)
            low = (total - high.astype(f32)).astype(bf16)
            return mm(w, jnp.concatenate([high, low], axis=0))

        cols0 = jnp.concatenate([kind_ref[2]] * 2, axis=1)
        cols1 = jnp.concatenate([kind_ref[3]] * 2, axis=1)
        scalar = scale * (cols0 * project(0, w2s) + cols1 * project(1, w2s))
        squared = None
        for c in range(3):
            vec = (scale * vector_scale) * (
                cols0 * project(2 * c + 2, w2v) + cols1 * project(2 * c + 3, w2v)
            )
            squared = vec * vec if squared is None else squared + vec * vec
        mixed = jnp.concatenate([scalar, squared], axis=0).astype(bf16)
        update = mm(wup_ref[...], mixed)
        e0 = jnp.concatenate([kind_ref[0]] * 2, axis=1)
        e1 = jnp.concatenate([kind_ref[1]] * 2, axis=1)
        features = jnp.where(spec_ref[f : f + 1, :] == 1, e1, e0) + silu(update)
        feat_ref[f] = features
        message = mm(wmsg_ref[...], features.astype(bf16)).astype(bf16)
        msg_ref[f] = message
        for side, out in ((0, down_ref), (1, up_ref)):
            index = spread(halo_ref[f, side : side + 1, :], LANES)
            lane = (index & (LANES - 1)).astype(jnp.int16)
            high = (index >> 7).astype(jnp.int16) > 0
            low_g = lane_gather(message[:, :LANES], lane)
            high_g = lane_gather(message[:, LANES:], lane)
            out[f] = jnp.where(high, high_g, low_g)


def hidden_kernel(
    slab_ref,
    geo_ref,
    w1_ref,
    temp_ref,
    pos_ref,
    spec_ref,
    target_hbm,
    uref_hbm,
    eshift_hbm,
    count_hbm,
    q_hbm,
    wr2_hbm,
    wup_hbm,
    wout_hbm,
    out_ref,
    w2_ref,
    wup_ref,
    wout_ref,
    struct_ref,
    live_ref,
    scalar_ref,
    target_ref,
    uref_in,
    eshift_in,
    count_in,
    q_in,
    wr2_in,
    wup_in,
    wout_in,
    sems,
):
    pairs = (
        (target_hbm, target_ref),
        (uref_hbm, uref_in),
        (eshift_hbm, eshift_in),
        (count_hbm, count_in),
        (q_hbm, q_in),
        (wr2_hbm.at[1], wr2_in),
        (wup_hbm.at[1], wup_in),
        (wout_hbm, wout_in),
    )
    copies = fetch_all(sems, pairs)
    _, frames, atoms = pos_ref.shape
    batches = geo_ref.shape[2]
    hidden = wr2_in.shape[0]
    for f in range(frames):

        def step(i, carry):
            for first in range(0, 8, GROUP):
                act = silu(mm(w1_ref[1], basis_rows(geo_ref, f, i, first, atoms)))
                out_ref[f, i, first * hidden : (first + GROUP) * hidden, :] = act.astype(bf16)
            return carry

        lax.fori_loop(0, batches, step, 0, unroll=UNH)
    for copy in copies:
        copy.wait()
    number_q = q_in.shape[1]
    same = lax.broadcasted_iota(jnp.int32, (number_q, number_q), 0) == lax.broadcasted_iota(
        jnp.int32, (number_q, number_q), 1
    )
    q = [
        jnp.sum(jnp.where(same, spread(q_in[c : c + 1, :], number_q), 0.0), axis=1, keepdims=True)
        for c in range(3)
    ]
    lift = slab_ref[0].astype(f32) * slab_depth
    number = lax.broadcasted_iota(jnp.int32, (1, atoms), 1)
    struct_ref[...] = jnp.zeros_like(struct_ref)
    for f in range(frames):
        x, y, z = (pos_ref[c, f : f + 1, :] for c in range(3))
        phases = q[0] * x + q[1] * y + q[2] * (z + lift)
        lengths = jnp.where(spec_ref[f : f + 1, :] == 1, 1.0, hydrogen_length)
        living = (number < count_in[:, f : f + 1]).astype(f32)
        live_ref[f : f + 1, :] = living
        lengths = living * lengths
        cos_part = jnp.sum(lengths * jnp.cos(phases), axis=1, keepdims=True)
        sin_part = jnp.sum(lengths * jnp.sin(phases), axis=1, keepdims=True)
        struct_ref[2 + f : 3 + f, :] = as_row(cos_part)
        struct_ref[4 + f : 5 + f, :] = as_row(sin_part)
    w2_ref[...] = transposed(wr2_in[...])
    wup_ref[...] = transposed(wup_in[...])
    wout_ref[...] = column(wout_in[...])
    for k in range(2):
        scalar_ref[k : k + 1, :] = jnp.broadcast_to(uref_in[:, k : k + 1], (1, LANES))
        scalar_ref[2 + k : 3 + k, :] = temp_ref[...]
        scalar_ref[4 + k : 5 + k, :] = jnp.broadcast_to(eshift_in[:, k : k + 1], (1, LANES))
    scalar_ref[6:8, :] = jnp.zeros((2, LANES), f32)


def second_kernel(
    rows_each,
    live_ref,
    spec_ref,
    scalar_ref,
    nb_ref,
    geo_ref,
    hid_ref,
    feat_ref,
    msg_ref,
    below_ref,
    above_ref,
    w2_ref,
    wup_ref,
    wout_ref,
    struct_ref,
    energy_ref,
    chunk_ref,
    acc_ref,
    pair_ref,
):
    frames, batches, _, atoms = nb_ref.shape
    slots = batches * 8
    hidden = w2_ref.shape[1]
    chunks = chunk_ref.shape[0]
    wout = jnp.concatenate([wout_ref[...]] * 2, axis=1)
    shift = [jnp.concatenate([scalar_ref[4 + k : 5 + k, :]] * 2, axis=1) for k in range(2)]
    scale = slots**-0.5
    extra = [None] * EXTRA
    for f in range(frames):
        halo = jnp.concatenate([below_ref[f], above_ref[f]], axis=1)
        pair_ref[...] = jnp.concatenate([msg_ref[f], halo], axis=0)
        acc_ref[...] = jnp.zeros_like(acc_ref)

        def step(i, carry):
            target = lax.broadcasted_iota(jnp.int32, (2 * LANES, atoms), 0).astype(bf16)
            filters, found = [], []
            for j in range(8):
                want = (nb_ref[f, i, j : j + 1, :] & (2 * LANES - 1)).astype(f32).astype(bf16)
                hot = jnp.where(target == want, jnp.asarray(1, bf16), jnp.asarray(0, bf16))
                found.append(mm(pair_ref[...], hot))
                filters.append(mm(w2_ref[...], hid_ref[f, i, j * hidden : (j + 1) * hidden, :]))
            for half in range(atoms // LANES):
                cols = slice(half * LANES, (half + 1) * LANES)
                own = [spread(nb_ref[f, i, j : j + 1, cols], WIDTH) < 2 * LANES for j in range(8)]
                offset = [[geo_ref[f, c, i, j : j + 1, cols] for c in range(3)] for j in range(8)]
                for part in range(0, LANES, WIDTH):
                    rows = slice(part, part + WIDTH)
                    lower = slice(LANES + part, LANES + part + WIDTH)
                    total = [acc_ref[k, rows, cols] for k in range(4)]
                    for j in range(8):
                        there = jnp.where(own[j], found[j][rows, cols], found[j][lower, cols])
                        total[0] = total[0] + filters[j][rows, cols] * there
                        vec = filters[j][lower, cols] * there
                        for c in range(3):
                            total[c + 1] = total[c + 1] + offset[j][c] * vec
                    for k in range(4):
                        acc_ref[k, rows, cols] = total[k]
            return carry

        lax.fori_loop(0, batches, step, 0, unroll=UN2)

        scalar = scale * acc_ref[0]
        squared = None
        for c in range(3):
            vec = (scale * vector_scale) * acc_ref[c + 1]
            squared = vec * vec if squared is None else squared + vec * vec
        mixed = jnp.concatenate([scalar, squared], axis=0).astype(bf16)
        update = mm(wup_ref[...], mixed)
        gate = sigmoid(update)
        features = feat_ref[f] + update * gate
        living = live_ref[f : f + 1, :]
        slope = (living * wout * (gate * (1.0 + update * (1.0 - gate)))).astype(bf16)
        kind = spec_ref[f : f + 1, :]
        readout = jnp.sum(features * wout, axis=0, keepdims=True)
        energy = living * (readout + jnp.where(kind == 1, shift[1], shift[0]))
        energy_ref[f : f + 1, :] = energy
        grad = lax.dot_general(mixed, slope, (((1,), (1,)), ((), ())), preferred_element_type=f32)
        chunk_ref[:, f * rows_each : (f + 1) * rows_each, :] = grad.reshape(
            chunks, rows_each, LANES
        )
        extra[f] = as_row(jnp.sum(living * features, axis=1, keepdims=True))
        extra[2 + f] = struct_ref[2 + f : 3 + f, :]
        extra[4 + f] = struct_ref[4 + f : 5 + f, :]
        extra[6 + f] = jnp.broadcast_to(jnp.sum(energy, axis=1, keepdims=True), (1, LANES))
    block = jnp.concatenate(extra, axis=0)
    chunk_ref[:, frames * rows_each :, :] = jnp.broadcast_to(block[None], (chunks, EXTRA, LANES))


def total_kernel(scalar_ref, in_ref, out_ref):
    rows = in_ref.shape[1]
    total = in_ref[0]
    for s in range(1, in_ref.shape[0]):
        total = total + in_ref[s]
    for d in range(out_ref.shape[0]):
        out_ref[d] = total
    for f in range(2):
        row = total[rows - 2 + f : rows - 1 + f]
        log_weight = -scalar_ref[2 + f : 3 + f, :] * (row - scalar_ref[f : f + 1, :])
        for d in range(out_ref.shape[0]):
            out_ref[d, rows - 2 + f : rows - 1 + f, :] = log_weight


def final_kernel(
    rows_each,
    atoms_all,
    scalar_ref,
    in_ref,
    target_ref,
    chunk_ref,
    mean_ref,
    out_ref,
):
    devices = in_ref.shape[0]
    q = target_ref.shape[1]
    base = 2 * rows_each

    def gather(at):
        return jnp.concatenate([in_ref[d, base + at : base + at + 2, :] for d in range(devices)], 0)

    cos_tot, sin_tot, log_weight = gather(2), gather(4), gather(6)
    structure = ((cos_tot * cos_tot + sin_tot * sin_tot) / atoms_all)[:, :q]
    scaled = jnp.exp(log_weight - jnp.max(log_weight, axis=0, keepdims=True))
    weights = scaled / jnp.sum(scaled, axis=0, keepdims=True)
    mean = jnp.sum(weights[:, :q] * structure, axis=0, keepdims=True)
    slope_sq = (mean - target_ref[...]) / target_var
    observed = jnp.sum(structure * slope_sq, axis=1, keepdims=True)
    average = jnp.sum(mean * slope_sq, axis=1, keepdims=True)
    factor = -scalar_ref[2:3, :] * weights * (observed - average)
    mean_ref[...] = mean
    out_ref[...] = jnp.sum(factor * gather(0), axis=0, keepdims=True)
    grad = jnp.zeros((rows_each, LANES), f32)
    for d in range(devices):
        for f in range(2):
            k = 2 * d + f
            grad = grad + factor[k : k + 1] * in_ref[d, f * rows_each : (f + 1) * rows_each, :]
    for s in range(chunk_ref.shape[0]):
        chunk_ref[s] = grad


VM = pl.BlockSpec(memory_space=pltpu.VMEM)
SM = pl.BlockSpec(memory_space=pltpu.SMEM)
HB = pl.BlockSpec(memory_space=pltpu.HBM)


def call(kernel, name, ins, outs, scratch, *operands):
    return pl.pallas_call(
        kernel,
        name=name,
        out_shape=outs,
        in_specs=ins,
        out_specs=jax.tree.map(lambda _: VM, outs),
        scratch_shapes=scratch,
        compiler_params=pltpu.CompilerParams(vmem_limit_bytes=VMEM_BYTES),
    )(*operands)


def in_hbm(value):
    return pltpu.with_memory_space_constraint(value, pltpu.HBM)


def array(shape, dtype=f32):
    return jax.ShapeDtypeStruct(shape, dtype)


def per_device(
    positions,
    species,
    atom_count,
    halo_index,
    neighbours,
    embedding,
    w_msg,
    w_rad1,
    w_rad2,
    w_up,
    w_out,
    e_shift,
    u_reference,
    inverse_temp,
    q_vectors,
    s_target,
):
    frames, _, atoms = positions.shape
    slots = neighbours.shape[1]
    halo = halo_index.shape[2]
    hidden = w_rad1.shape[2]
    channels = w_msg.shape[1]
    neighbours = neighbours.reshape(frames, slots // 8, 8, atoms)
    positions = positions.transpose(1, 0, 2)
    slab_devs = lax.axis_size("slab")
    frame_devs = lax.axis_size("frame")
    rows_each = 2 * channels // slab_devs
    chunk_rows = frames * rows_each + EXTRA
    up = [(i, (i + 1) % slab_devs) for i in range(slab_devs)]
    down = [(j, i) for i, j in up]

    basis = w_rad1.shape[1]
    rows = array((4 * frames, halo))
    leave_down, leave_up, positions, species, halo_index = call(
        pack_kernel,
        "halo_rows",
        [HB] * 3,
        (
            rows,
            rows,
            array(positions.shape),
            array(species.shape, jnp.int32),
            array(halo_index.shape, jnp.int32),
        ),
        [pltpu.SemaphoreType.DMA((3,))],
        *map(in_hbm, (positions, species, halo_index)),
    )
    below = lax.ppermute(leave_up, "slab", up)
    above = lax.ppermute(leave_down, "slab", down)
    q = s_target.shape[0]
    staged = (embedding, w_msg, w_rad1)
    halves = (array(w_rad2.shape[1:], bf16), array(w_up.shape[1:], bf16))
    neighbours, w1, w2, wup, wmsg, kinds, temp = call(
        stage_kernel,
        "staged_inputs",
        [SM] + [HB] * 6,
        (
            array(neighbours.shape, jnp.int32),
            array((2, GROUP * hidden, GROUP * basis), bf16),
            array((2 * channels, hidden), bf16),
            array((channels, 2 * channels), bf16),
            array((channels, channels), bf16),
            array((4, channels, LANES)),
            array((1, LANES)),
        ),
        [pltpu.VMEM(w.shape, w.dtype) for w in (*staged, *halves)]
        + [pltpu.SemaphoreType.DMA((6,))],
        inverse_temp,
        *map(in_hbm, (neighbours, *staged, w_rad2, w_up)),
    )
    halo_rows = array((frames, channels, halo), bf16)
    geometry, features, message, msg_down, msg_up = call(
        first_kernel,
        "first_layer",
        [VM] * 11,
        (
            array((frames, 4, slots // 8, 8, atoms)),
            array((frames, channels, atoms)),
            array((frames, channels, atoms), bf16),
            halo_rows,
            halo_rows,
        ),
        [pltpu.VMEM((7, slots // 8, 8, atoms), f32), pltpu.VMEM((8, hidden, atoms), f32)],
        positions,
        species,
        below,
        above,
        neighbours,
        halo_index,
        w1,
        w2,
        wup,
        wmsg,
        kinds,
    )
    msg_below = lax.ppermute(msg_up, "slab", up)
    msg_above = lax.ppermute(msg_down, "slab", down)
    small = (
        u_reference.reshape(1, frames),
        e_shift.reshape(1, 2),
        atom_count.reshape(1, frames),
        q_vectors,
    )
    wout_row = w_out.reshape(1, channels)
    radial_hidden, w2, wup, wout, structure, living, scalars, target = call(
        hidden_kernel,
        "radial_hidden",
        [SM] + [VM] * 5 + [HB] * 8,
        (
            array((frames, slots // 8, 8 * hidden, atoms), bf16),
            array((2 * channels, hidden), bf16),
            array((channels, 2 * channels), bf16),
            array((channels, LANES)),
            array((EXTRA, LANES)),
            array((frames, atoms)),
            array((8, LANES)),
            array((1, q)),
        ),
        [pltpu.VMEM(w.shape, w.dtype) for w in (*small, *halves, wout_row)]
        + [pltpu.SemaphoreType.DMA((8,))],
        lax.axis_index("slab").reshape(1),
        geometry,
        w1,
        temp,
        positions,
        species,
        *map(in_hbm, (s_target.reshape(1, q), *small, w_rad2, w_up, wout_row)),
    )
    atom_energy, chunks = call(
        functools.partial(second_kernel, rows_each),
        "second_layer",
        [VM] * 14,
        (array((frames, atoms)), array((slab_devs, chunk_rows, LANES))),
        [
            pltpu.VMEM((4, channels, atoms), f32),
            pltpu.VMEM((2 * channels, 2 * LANES), bf16),
        ],
        living,
        species,
        scalars,
        neighbours,
        geometry,
        radial_hidden,
        features,
        message,
        msg_below,
        msg_above,
        w2,
        wup,
        wout,
        structure,
    )
    chunks = lax.all_to_all(chunks, "slab", 0, 0, tiled=True)
    totals = call(
        total_kernel,
        "slab_totals",
        [VM, VM],
        array((frame_devs, chunk_rows, LANES)),
        [],
        scalars,
        chunks,
    )
    totals = lax.all_to_all(totals, "frame", 0, 0, tiled=True)
    grad_rows, mean_structure, grad_out = call(
        functools.partial(final_kernel, rows_each, atoms * slab_devs),
        "reweighted",
        [VM] * 3,
        (array((slab_devs, rows_each, LANES)), array((1, q)), array((1, channels))),
        [],
        scalars,
        totals,
        target,
    )
    grad_up = lax.all_to_all(grad_rows, "slab", 0, 0, tiled=True)
    return (
        atom_energy,
        mean_structure.reshape(q),
        grad_up.reshape(2 * channels, channels),
        grad_out.reshape(channels),
    )


def solution(mesh):
    in_specs = (
        P("frame", None, "slab"),
        P("frame", "slab"),
        P("frame", "slab"),
        P("frame", None, "slab"),
        P("frame", None, "slab"),
        P(),
        P(),
        P(),
        P(),
        P(),
        P(),
        P(),
        P("frame"),
        P(),
        P(),
        P(),
    )
    out_specs = (P("frame", "slab"), P(), P(), P())
    return jax.shard_map(
        per_device, mesh=mesh, in_specs=in_specs, out_specs=out_specs, check_vma=False
    )
```

```python
import functools

import jax
import jax.numpy as jnp
from jax import lax
from jax.experimental import pallas as pl
from jax.experimental.pallas import tpu as pltpu
from jax.sharding import PartitionSpec as P

slab_depth = 6.0
vector_scale = 0.2
target_var = 0.01
hydrogen_length = -0.64
LANES = 128
GROUP = 4
EXTRA = 8
EMPTY = 1.0e4
UN1 = 6
UNH = 3
UN2 = 3
WIDTH = 32
VMEM_BYTES = 48 * 1024 * 1024

f32 = jnp.float32
bf16 = jnp.bfloat16


def lane_gather(table, index):
    numbers = lax.GatherDimensionNumbers(
        offset_dims=(),
        collapsed_slice_dims=(1,),
        start_index_map=(1,),
        operand_batching_dims=(0,),
        start_indices_batching_dims=(0,),
    )
    return lax.gather(
        table,
        index[..., None],
        numbers,
        slice_sizes=(1, 1),
        mode=lax.GatherScatterMode.PROMISE_IN_BOUNDS,
    )


def spread(row, rows):
    return jnp.broadcast_to(row, (rows, row.shape[1]))


def column(row):
    return spread(row, LANES).T


def as_row(col):
    wide = jnp.broadcast_to(col, (col.shape[0], LANES))
    if col.shape[0] < LANES:
        wide = jnp.concatenate([wide, jnp.zeros((LANES - col.shape[0], LANES), f32)], axis=0)
    return wide.T[0:1]


def sigmoid(values):
    return 0.5 * (1.0 + jnp.tanh(0.5 * values))


def silu(values):
    half = 0.5 * values
    return half + half * jnp.tanh(half)


def silu_of_twice(half):
    return half + half * jnp.tanh(half)


def mm(a, b):
    return jnp.dot(a, b, preferred_element_type=f32)


def rad1_blocks(w_rad1):
    basis, hidden = w_rad1.shape
    w = 0.5 * w_rad1.astype(f32)
    wide = jnp.concatenate([w] * GROUP, axis=1)
    tall = jnp.concatenate([wide] * GROUP, axis=0)
    row = lax.broadcasted_iota(jnp.int32, tall.shape, 0) // basis
    col = lax.broadcasted_iota(jnp.int32, tall.shape, 1) // hidden
    tall = jnp.where(row == col, tall, 0.0)
    tall = jnp.concatenate([tall, jnp.zeros((LANES - GROUP * basis, GROUP * hidden), f32)], axis=0)
    return tall.T[:, : GROUP * basis].astype(bf16)


def transposed(w):
    return w.astype(f32).T.astype(bf16)


def fetch_all(sems, pairs):
    copies = [pltpu.make_async_copy(src, dst, sems.at[i]) for i, (src, dst) in enumerate(pairs)]
    for copy in copies:
        copy.start()
    return copies


def pack_kernel(pos_hbm, spec_hbm, halo_hbm, down_ref, up_ref, pos_ref, spec_ref, halo_ref, sems):
    pairs = ((pos_hbm, pos_ref), (spec_hbm, spec_ref), (halo_hbm, halo_ref))
    for copy in fetch_all(sems, pairs):
        copy.wait()
    frames = spec_ref.shape[0]
    for f in range(frames):
        rows = [pos_ref[c, f : f + 1, :] for c in range(3)]
        rows.append(spec_ref[f : f + 1, :].astype(f32))
        for side, out in ((0, down_ref), (1, up_ref)):
            index = halo_ref[f, side : side + 1, :]
            lane = spread(index & (LANES - 1), 8)
            high = spread(index, 8) >= LANES
            for c, row in enumerate(rows):
                low_g = lane_gather(spread(row[:, :LANES], 8), lane)
                high_g = lane_gather(spread(row[:, LANES:], 8), lane)
                out[4 * f + c : 4 * f + c + 1, :] = jnp.where(high, high_g, low_g)[0:1]


def stage_kernel(
    beta_ref,
    nb_hbm,
    emb_hbm,
    wmsg_hbm,
    wr1_hbm,
    wr2_hbm,
    wup_hbm,
    nb_ref,
    w1_ref,
    w2_ref,
    wup_ref,
    wmsg_ref,
    kind_ref,
    temp_ref,
    emb_in,
    wmsg_in,
    wr1_in,
    wr2_in,
    wup_in,
    sems,
):
    pairs = (
        (nb_hbm, nb_ref),
        (wr1_hbm, wr1_in),
        (wr2_hbm.at[0], wr2_in),
        (wup_hbm.at[0], wup_in),
        (wmsg_hbm, wmsg_in),
        (emb_hbm, emb_in),
    )
    copies = fetch_all(sems, pairs)
    temp_ref[...] = jnp.full((1, LANES), beta_ref[0], f32)
    for copy in copies:
        copy.wait()
    for layer in range(2):
        w1_ref[layer] = rad1_blocks(wr1_in[layer])
    w2_ref[...] = transposed(wr2_in[...])
    wup_ref[...] = transposed(wup_in[...])
    wmsg_ref[...] = transposed(wmsg_in[1])
    emb = emb_in[...]
    table = mm(emb, wmsg_in[0]).astype(bf16).astype(f32)
    for k in range(2):
        kind_ref[k] = column(emb[k : k + 1].astype(f32))
        kind_ref[2 + k] = column(table[k : k + 1])


def basis_rows(dist_ref, f, i, first, atoms):
    center = lax.broadcasted_iota(jnp.int32, (8, atoms), 0).astype(f32)
    parts = []
    for j in range(first, first + GROUP):
        off = spread(dist_ref[f, 3, i, j : j + 1, :], 8) - center
        parts.append(jnp.exp(-(off * off)))
    return jnp.concatenate(parts, axis=0).astype(bf16)


def first_kernel(
    pos_ref,
    spec_ref,
    below_ref,
    above_ref,
    nb_ref,
    halo_ref,
    w1_ref,
    w2_ref,
    wup_ref,
    wmsg_ref,
    kind_ref,
    geo_ref,
    feat_ref,
    msg_ref,
    down_ref,
    up_ref,
    wgt_ref,
    acc_ref,
):
    _, frames, atoms = pos_ref.shape
    batches = nb_ref.shape[1]
    slots = batches * 8
    hidden = w2_ref.shape[1]
    w2s = jnp.concatenate([w2_ref[:LANES, :]] * 2, axis=1)
    w2v = jnp.concatenate([w2_ref[LANES:, :]] * 2, axis=1)
    scale = slots**-0.5
    for f in range(frames):
        for half in range(atoms // LANES):
            cols = slice(half * LANES, (half + 1) * LANES)
            for s in range(batches):
                index = nb_ref[f, s, :, cols]
                lane = index & (LANES - 1)
                block = index >> 7

                def fetch(own_row, halo_row):
                    parts = [
                        own_row[:, :LANES],
                        own_row[:, LANES:],
                        below_ref[halo_row : halo_row + 1, :],
                        above_ref[halo_row : halo_row + 1, :],
                    ]
                    return parts

                squares = None
                offsets = []
                for c in range(3):
                    own_row = pos_ref[c, f : f + 1, :]
                    parts = fetch(own_row, 4 * f + c)
                    if c == 2:
                        parts[2] = parts[2] - slab_depth
                        parts[3] = parts[3] + slab_depth
                    got = [lane_gather(spread(p, 8), lane) for p in parts]
                    there = jnp.where(
                        block == 0,
                        got[0],
                        jnp.where(block == 1, got[1], jnp.where(block == 2, got[2], got[3])),
                    )
                    offset = there - own_row[:, cols]
                    offsets.append(offset)
                    geo_ref[f, c, s, :, cols] = offset
                    squares = offset * offset if squares is None else squares + offset * offset
                geo_ref[f, 3, s, :, cols] = jnp.where(index >= 0, jnp.sqrt(squares), EMPTY)
                parts = fetch(spec_ref[f : f + 1, :].astype(f32), 4 * f + 3)
                got = [lane_gather(spread(p, 8), lane) for p in parts]
                kind = jnp.where(
                    block == 0,
                    got[0],
                    jnp.where(block == 1, got[1], jnp.where(block == 2, got[2], got[3])),
                )
                wgt_ref[0, s, :, cols] = kind
                for c in range(3):
                    wgt_ref[2 * c + 1, s, :, cols] = offsets[c] * (1.0 - kind)
                    wgt_ref[2 * c + 2, s, :, cols] = offsets[c] * kind
        acc_ref[...] = jnp.zeros_like(acc_ref)

        def step(i, carry):
            acts = []
            for first in range(0, 8, GROUP):
                pre = mm(w1_ref[0], basis_rows(geo_ref, f, i, first, atoms))
                acts.append(silu_of_twice(pre).astype(bf16).astype(f32))
            for half in range(atoms // LANES):
                cols = slice(half * LANES, (half + 1) * LANES)
                for part in range(0, hidden, 32):
                    hid = []
                    for j in range(8):
                        at = (j % GROUP) * hidden + part
                        hid.append(acts[j // GROUP][at : at + 32, cols])
                    total = hid[0]
                    for j in range(1, 8):
                        total = total + hid[j]
                    acc_ref[0, part : part + 32, cols] += total
                    for k in range(7):
                        total = acc_ref[k + 1, part : part + 32, cols]
                        for j in range(8):
                            total = total + wgt_ref[k, i, j : j + 1, cols] * hid[j]
                        acc_ref[k + 1, part : part + 32, cols] = total
            return carry

        lax.fori_loop(0, batches, step, 0, unroll=UN1)

        acc_ref[0] = acc_ref[0] - acc_ref[1]

        def project(k, w):
            total = acc_ref[k]
            high = total.astype(bf16)
            low = (total - high.astype(f32)).astype(bf16)
            return mm(w, jnp.concatenate([high, low], axis=0))

        cols0 = jnp.concatenate([kind_ref[2]] * 2, axis=1)
        cols1 = jnp.concatenate([kind_ref[3]] * 2, axis=1)
        scalar = scale * (cols0 * project(0, w2s) + cols1 * project(1, w2s))
        squared = None
        for c in range(3):
            vec = (scale * vector_scale) * (
                cols0 * project(2 * c + 2, w2v) + cols1 * project(2 * c + 3, w2v)
            )
            squared = vec * vec if squared is None else squared + vec * vec
        mixed = jnp.concatenate([scalar, squared], axis=0).astype(bf16)
        update = mm(wup_ref[...], mixed)
        e0 = jnp.concatenate([kind_ref[0]] * 2, axis=1)
        e1 = jnp.concatenate([kind_ref[1]] * 2, axis=1)
        features = jnp.where(spec_ref[f : f + 1, :] == 1, e1, e0) + silu(update)
        feat_ref[f] = features
        message = mm(wmsg_ref[...], features.astype(bf16)).astype(bf16)
        msg_ref[f] = message
        for side, out in ((0, down_ref), (1, up_ref)):
            index = spread(halo_ref[f, side : side + 1, :], LANES)
            lane = (index & (LANES - 1)).astype(jnp.int16)
            high = (index >> 7).astype(jnp.int16) > 0
            low_g = lane_gather(message[:, :LANES], lane)
            high_g = lane_gather(message[:, LANES:], lane)
            out[f] = jnp.where(high, high_g, low_g)


def hidden_kernel(
    slab_ref,
    geo_ref,
    w1_ref,
    temp_ref,
    pos_ref,
    spec_ref,
    target_hbm,
    uref_hbm,
    eshift_hbm,
    count_hbm,
    q_hbm,
    wr2_hbm,
    wup_hbm,
    wout_hbm,
    out_ref,
    w2_ref,
    wup_ref,
    wout_ref,
    struct_ref,
    live_ref,
    scalar_ref,
    target_ref,
    uref_in,
    eshift_in,
    count_in,
    q_in,
    wr2_in,
    wup_in,
    wout_in,
    sems,
):
    pairs = (
        (target_hbm, target_ref),
        (uref_hbm, uref_in),
        (eshift_hbm, eshift_in),
        (count_hbm, count_in),
        (q_hbm, q_in),
        (wr2_hbm.at[1], wr2_in),
        (wup_hbm.at[1], wup_in),
        (wout_hbm, wout_in),
    )
    copies = fetch_all(sems, pairs)
    _, frames, atoms = pos_ref.shape
    batches = geo_ref.shape[2]
    hidden = wr2_in.shape[0]
    for f in range(frames):

        def step(i, carry):
            for first in range(0, 8, GROUP):
                act = silu_of_twice(mm(w1_ref[1], basis_rows(geo_ref, f, i, first, atoms)))
                out_ref[f, i, first * hidden : (first + GROUP) * hidden, :] = act.astype(bf16)
            return carry

        lax.fori_loop(0, batches, step, 0, unroll=UNH)
    for copy in copies:
        copy.wait()
    number_q = q_in.shape[1]
    same = lax.broadcasted_iota(jnp.int32, (number_q, number_q), 0) == lax.broadcasted_iota(
        jnp.int32, (number_q, number_q), 1
    )
    q = [
        jnp.sum(jnp.where(same, spread(q_in[c : c + 1, :], number_q), 0.0), axis=1, keepdims=True)
        for c in range(3)
    ]
    lift = slab_ref[0].astype(f32) * slab_depth
    number = lax.broadcasted_iota(jnp.int32, (1, atoms), 1)
    struct_ref[...] = jnp.zeros_like(struct_ref)
    for f in range(frames):
        x, y, z = (pos_ref[c, f : f + 1, :] for c in range(3))
        phases = q[0] * x + q[1] * y + q[2] * (z + lift)
        lengths = jnp.where(spec_ref[f : f + 1, :] == 1, 1.0, hydrogen_length)
        living = (number < count_in[:, f : f + 1]).astype(f32)
        live_ref[f : f + 1, :] = living
        lengths = living * lengths
        cos_part = jnp.sum(lengths * jnp.cos(phases), axis=1, keepdims=True)
        sin_part = jnp.sum(lengths * jnp.sin(phases), axis=1, keepdims=True)
        struct_ref[2 + f : 3 + f, :] = as_row(cos_part)
        struct_ref[4 + f : 5 + f, :] = as_row(sin_part)
    w2_ref[...] = transposed(wr2_in[...])
    wup_ref[...] = transposed(wup_in[...])
    wout_ref[...] = column(wout_in[...])
    for k in range(2):
        scalar_ref[k : k + 1, :] = jnp.broadcast_to(uref_in[:, k : k + 1], (1, LANES))
        scalar_ref[2 + k : 3 + k, :] = temp_ref[...]
        scalar_ref[4 + k : 5 + k, :] = jnp.broadcast_to(eshift_in[:, k : k + 1], (1, LANES))
    scalar_ref[6:8, :] = jnp.zeros((2, LANES), f32)


def second_kernel(
    rows_each,
    live_ref,
    spec_ref,
    scalar_ref,
    nb_ref,
    geo_ref,
    hid_ref,
    feat_ref,
    msg_ref,
    below_ref,
    above_ref,
    w2_ref,
    wup_ref,
    wout_ref,
    struct_ref,
    energy_ref,
    chunk_ref,
    acc_ref,
    pair_ref,
):
    frames, batches, _, atoms = nb_ref.shape
    slots = batches * 8
    hidden = w2_ref.shape[1]
    chunks = chunk_ref.shape[0]
    wout = jnp.concatenate([wout_ref[...]] * 2, axis=1)
    shift = [jnp.concatenate([scalar_ref[4 + k : 5 + k, :]] * 2, axis=1) for k in range(2)]
    scale = slots**-0.5
    extra = [None] * EXTRA
    for f in range(frames):
        halo = jnp.concatenate([below_ref[f], above_ref[f]], axis=1)
        pair_ref[...] = jnp.concatenate([msg_ref[f], halo], axis=0)
        acc_ref[...] = jnp.zeros_like(acc_ref)

        def step(i, carry):
            target = lax.broadcasted_iota(jnp.int32, (2 * LANES, atoms), 0).astype(bf16)
            filters, found = [], []
            for j in range(8):
                want = (nb_ref[f, i, j : j + 1, :] & (2 * LANES - 1)).astype(f32).astype(bf16)
                hot = jnp.where(target == want, jnp.asarray(1, bf16), jnp.asarray(0, bf16))
                found.append(mm(pair_ref[...], hot))
                filters.append(mm(w2_ref[...], hid_ref[f, i, j * hidden : (j + 1) * hidden, :]))
            for half in range(atoms // LANES):
                cols = slice(half * LANES, (half + 1) * LANES)
                own = [spread(nb_ref[f, i, j : j + 1, cols], WIDTH) < 2 * LANES for j in range(8)]
                offset = [[geo_ref[f, c, i, j : j + 1, cols] for c in range(3)] for j in range(8)]
                for part in range(0, LANES, WIDTH):
                    rows = slice(part, part + WIDTH)
                    lower = slice(LANES + part, LANES + part + WIDTH)
                    total = [acc_ref[k, rows, cols] for k in range(4)]
                    for j in range(8):
                        there = jnp.where(own[j], found[j][rows, cols], found[j][lower, cols])
                        total[0] = total[0] + filters[j][rows, cols] * there
                        vec = filters[j][lower, cols] * there
                        for c in range(3):
                            total[c + 1] = total[c + 1] + offset[j][c] * vec
                    for k in range(4):
                        acc_ref[k, rows, cols] = total[k]
            return carry

        lax.fori_loop(0, batches, step, 0, unroll=UN2)

        scalar = scale * acc_ref[0]
        squared = None
        for c in range(3):
            vec = (scale * vector_scale) * acc_ref[c + 1]
            squared = vec * vec if squared is None else squared + vec * vec
        mixed = jnp.concatenate([scalar, squared], axis=0).astype(bf16)
        update = mm(wup_ref[...], mixed)
        gate = sigmoid(update)
        features = feat_ref[f] + update * gate
        living = live_ref[f : f + 1, :]
        slope = (living * wout * (gate * (1.0 + update * (1.0 - gate)))).astype(bf16)
        kind = spec_ref[f : f + 1, :]
        readout = jnp.sum(features * wout, axis=0, keepdims=True)
        energy = living * (readout + jnp.where(kind == 1, shift[1], shift[0]))
        energy_ref[f : f + 1, :] = energy
        grad = lax.dot_general(mixed, slope, (((1,), (1,)), ((), ())), preferred_element_type=f32)
        chunk_ref[:, f * rows_each : (f + 1) * rows_each, :] = grad.reshape(
            chunks, rows_each, LANES
        )
        extra[f] = as_row(jnp.sum(living * features, axis=1, keepdims=True))
        extra[2 + f] = struct_ref[2 + f : 3 + f, :]
        extra[4 + f] = struct_ref[4 + f : 5 + f, :]
        extra[6 + f] = jnp.broadcast_to(jnp.sum(energy, axis=1, keepdims=True), (1, LANES))
    block = jnp.concatenate(extra, axis=0)
    chunk_ref[:, frames * rows_each :, :] = jnp.broadcast_to(block[None], (chunks, EXTRA, LANES))


def total_kernel(scalar_ref, in_ref, out_ref):
    rows = in_ref.shape[1]
    total = in_ref[0]
    for s in range(1, in_ref.shape[0]):
        total = total + in_ref[s]
    for d in range(out_ref.shape[0]):
        out_ref[d] = total
    for f in range(2):
        row = total[rows - 2 + f : rows - 1 + f]
        log_weight = -scalar_ref[2 + f : 3 + f, :] * (row - scalar_ref[f : f + 1, :])
        for d in range(out_ref.shape[0]):
            out_ref[d, rows - 2 + f : rows - 1 + f, :] = log_weight


def final_kernel(
    rows_each,
    atoms_all,
    scalar_ref,
    in_ref,
    target_ref,
    chunk_ref,
    mean_ref,
    out_ref,
):
    devices = in_ref.shape[0]
    q = target_ref.shape[1]
    base = 2 * rows_each

    def gather(at):
        return jnp.concatenate([in_ref[d, base + at : base + at + 2, :] for d in range(devices)], 0)

    cos_tot, sin_tot, log_weight = gather(2), gather(4), gather(6)
    structure = ((cos_tot * cos_tot + sin_tot * sin_tot) / atoms_all)[:, :q]
    scaled = jnp.exp(log_weight - jnp.max(log_weight, axis=0, keepdims=True))
    weights = scaled / jnp.sum(scaled, axis=0, keepdims=True)
    mean = jnp.sum(weights[:, :q] * structure, axis=0, keepdims=True)
    slope_sq = (mean - target_ref[...]) / target_var
    observed = jnp.sum(structure * slope_sq, axis=1, keepdims=True)
    average = jnp.sum(mean * slope_sq, axis=1, keepdims=True)
    factor = -scalar_ref[2:3, :] * weights * (observed - average)
    mean_ref[...] = mean
    out_ref[...] = jnp.sum(factor * gather(0), axis=0, keepdims=True)
    grad = jnp.zeros((rows_each, LANES), f32)
    for d in range(devices):
        for f in range(2):
            k = 2 * d + f
            grad = grad + factor[k : k + 1] * in_ref[d, f * rows_each : (f + 1) * rows_each, :]
    for s in range(chunk_ref.shape[0]):
        chunk_ref[s] = grad


VM = pl.BlockSpec(memory_space=pltpu.VMEM)
SM = pl.BlockSpec(memory_space=pltpu.SMEM)
HB = pl.BlockSpec(memory_space=pltpu.HBM)


def call(kernel, name, ins, outs, scratch, *operands):
    return pl.pallas_call(
        kernel,
        name=name,
        out_shape=outs,
        in_specs=ins,
        out_specs=jax.tree.map(lambda _: VM, outs),
        scratch_shapes=scratch,
        compiler_params=pltpu.CompilerParams(vmem_limit_bytes=VMEM_BYTES),
    )(*operands)


def in_hbm(value):
    return pltpu.with_memory_space_constraint(value, pltpu.HBM)


def array(shape, dtype=f32):
    return jax.ShapeDtypeStruct(shape, dtype)


def per_device(
    positions,
    species,
    atom_count,
    halo_index,
    neighbours,
    embedding,
    w_msg,
    w_rad1,
    w_rad2,
    w_up,
    w_out,
    e_shift,
    u_reference,
    inverse_temp,
    q_vectors,
    s_target,
):
    frames, _, atoms = positions.shape
    slots = neighbours.shape[1]
    halo = halo_index.shape[2]
    hidden = w_rad1.shape[2]
    channels = w_msg.shape[1]
    neighbours = neighbours.reshape(frames, slots // 8, 8, atoms)
    positions = positions.transpose(1, 0, 2)
    slab_devs = lax.axis_size("slab")
    frame_devs = lax.axis_size("frame")
    rows_each = 2 * channels // slab_devs
    chunk_rows = frames * rows_each + EXTRA
    up = [(i, (i + 1) % slab_devs) for i in range(slab_devs)]
    down = [(j, i) for i, j in up]

    basis = w_rad1.shape[1]
    rows = array((4 * frames, halo))
    leave_down, leave_up, positions, species, halo_index = call(
        pack_kernel,
        "halo_rows",
        [HB] * 3,
        (
            rows,
            rows,
            array(positions.shape),
            array(species.shape, jnp.int32),
            array(halo_index.shape, jnp.int32),
        ),
        [pltpu.SemaphoreType.DMA((3,))],
        *map(in_hbm, (positions, species, halo_index)),
    )
    below = lax.ppermute(leave_up, "slab", up)
    above = lax.ppermute(leave_down, "slab", down)
    q = s_target.shape[0]
    staged = (embedding, w_msg, w_rad1)
    halves = (array(w_rad2.shape[1:], bf16), array(w_up.shape[1:], bf16))
    neighbours, w1, w2, wup, wmsg, kinds, temp = call(
        stage_kernel,
        "staged_inputs",
        [SM] + [HB] * 6,
        (
            array(neighbours.shape, jnp.int32),
            array((2, GROUP * hidden, GROUP * basis), bf16),
            array((2 * channels, hidden), bf16),
            array((channels, 2 * channels), bf16),
            array((channels, channels), bf16),
            array((4, channels, LANES)),
            array((1, LANES)),
        ),
        [pltpu.VMEM(w.shape, w.dtype) for w in (*staged, *halves)]
        + [pltpu.SemaphoreType.DMA((6,))],
        inverse_temp,
        *map(in_hbm, (neighbours, *staged, w_rad2, w_up)),
    )
    halo_rows = array((frames, channels, halo), bf16)
    geometry, features, message, msg_down, msg_up = call(
        first_kernel,
        "first_layer",
        [VM] * 11,
        (
            array((frames, 4, slots // 8, 8, atoms)),
            array((frames, channels, atoms)),
            array((frames, channels, atoms), bf16),
            halo_rows,
            halo_rows,
        ),
        [pltpu.VMEM((7, slots // 8, 8, atoms), f32), pltpu.VMEM((8, hidden, atoms), f32)],
        positions,
        species,
        below,
        above,
        neighbours,
        halo_index,
        w1,
        w2,
        wup,
        wmsg,
        kinds,
    )
    msg_below = lax.ppermute(msg_up, "slab", up)
    msg_above = lax.ppermute(msg_down, "slab", down)
    small = (
        u_reference.reshape(1, frames),
        e_shift.reshape(1, 2),
        atom_count.reshape(1, frames),
        q_vectors,
    )
    wout_row = w_out.reshape(1, channels)
    radial_hidden, w2, wup, wout, structure, living, scalars, target = call(
        hidden_kernel,
        "radial_hidden",
        [SM] + [VM] * 5 + [HB] * 8,
        (
            array((frames, slots // 8, 8 * hidden, atoms), bf16),
            array((2 * channels, hidden), bf16),
            array((channels, 2 * channels), bf16),
            array((channels, LANES)),
            array((EXTRA, LANES)),
            array((frames, atoms)),
            array((8, LANES)),
            array((1, q)),
        ),
        [pltpu.VMEM(w.shape, w.dtype) for w in (*small, *halves, wout_row)]
        + [pltpu.SemaphoreType.DMA((8,))],
        lax.axis_index("slab").reshape(1),
        geometry,
        w1,
        temp,
        positions,
        species,
        *map(in_hbm, (s_target.reshape(1, q), *small, w_rad2, w_up, wout_row)),
    )
    atom_energy, chunks = call(
        functools.partial(second_kernel, rows_each),
        "second_layer",
        [VM] * 14,
        (array((frames, atoms)), array((slab_devs, chunk_rows, LANES))),
        [
            pltpu.VMEM((4, channels, atoms), f32),
            pltpu.VMEM((2 * channels, 2 * LANES), bf16),
        ],
        living,
        species,
        scalars,
        neighbours,
        geometry,
        radial_hidden,
        features,
        message,
        msg_below,
        msg_above,
        w2,
        wup,
        wout,
        structure,
    )
    chunks = lax.all_to_all(chunks, "slab", 0, 0, tiled=True)
    totals = call(
        total_kernel,
        "slab_totals",
        [VM, VM],
        array((frame_devs, chunk_rows, LANES)),
        [],
        scalars,
        chunks,
    )
    totals = lax.all_to_all(totals, "frame", 0, 0, tiled=True)
    grad_rows, mean_structure, grad_out = call(
        functools.partial(final_kernel, rows_each, atoms * slab_devs),
        "reweighted",
        [VM] * 3,
        (array((slab_devs, rows_each, LANES)), array((1, q)), array((1, channels))),
        [],
        scalars,
        totals,
        target,
    )
    grad_up = lax.all_to_all(grad_rows, "slab", 0, 0, tiled=True)
    return (
        atom_energy,
        mean_structure.reshape(q),
        grad_up.reshape(2 * channels, channels),
        grad_out.reshape(channels),
    )


def solution(mesh):
    in_specs = (
        P("frame", None, "slab"),
        P("frame", "slab"),
        P("frame", "slab"),
        P("frame", None, "slab"),
        P("frame", None, "slab"),
        P(),
        P(),
        P(),
        P(),
        P(),
        P(),
        P(),
        P("frame"),
        P(),
        P(),
        P(),
    )
    out_specs = (P("frame", "slab"), P(), P(), P())
    return jax.shard_map(
        per_device, mesh=mesh, in_specs=in_specs, out_specs=out_specs, check_vma=False
    )
```

```python
import functools

import jax
import jax.numpy as jnp
from jax import lax
from jax.experimental import pallas as pl
from jax.experimental.pallas import tpu as pltpu
from jax.sharding import PartitionSpec as P

slab_depth = 6.0
vector_scale = 0.2
target_var = 0.01
hydrogen_length = -0.64
LANES = 128
GROUP = 4
EXTRA = 8
EMPTY = 1.0e4
UN1 = 6
UNH = 3
UN2 = 3
WIDTH = 32
VMEM_BYTES = 48 * 1024 * 1024

f32 = jnp.float32
bf16 = jnp.bfloat16


def lane_gather(table, index):
    numbers = lax.GatherDimensionNumbers(
        offset_dims=(),
        collapsed_slice_dims=(1,),
        start_index_map=(1,),
        operand_batching_dims=(0,),
        start_indices_batching_dims=(0,),
    )
    return lax.gather(
        table,
        index[..., None],
        numbers,
        slice_sizes=(1, 1),
        mode=lax.GatherScatterMode.PROMISE_IN_BOUNDS,
    )


def spread(row, rows):
    return jnp.broadcast_to(row, (rows, row.shape[1]))


def column(row):
    return spread(row, LANES).T


def as_row(col):
    wide = jnp.broadcast_to(col, (col.shape[0], LANES))
    if col.shape[0] < LANES:
        wide = jnp.concatenate([wide, jnp.zeros((LANES - col.shape[0], LANES), f32)], axis=0)
    return wide.T[0:1]


def sigmoid(values):
    return 0.5 * (1.0 + jnp.tanh(0.5 * values))


def silu(values):
    half = 0.5 * values
    return half + half * jnp.tanh(half)


def silu_of_twice(half):
    return half + half * jnp.tanh(half)


def mm(a, b):
    return jnp.dot(a, b, preferred_element_type=f32)


def rad1_blocks(w_rad1):
    basis, hidden = w_rad1.shape
    w = 0.5 * w_rad1.astype(f32)
    wide = jnp.concatenate([w] * GROUP, axis=1)
    tall = jnp.concatenate([wide] * GROUP, axis=0)
    row = lax.broadcasted_iota(jnp.int32, tall.shape, 0) // basis
    col = lax.broadcasted_iota(jnp.int32, tall.shape, 1) // hidden
    tall = jnp.where(row == col, tall, 0.0)
    tall = jnp.concatenate([tall, jnp.zeros((LANES - GROUP * basis, GROUP * hidden), f32)], axis=0)
    return tall.T[:, : GROUP * basis].astype(bf16)


def transposed(w):
    return w.astype(f32).T.astype(bf16)


def fetch_all(sems, pairs):
    copies = [pltpu.make_async_copy(src, dst, sems.at[i]) for i, (src, dst) in enumerate(pairs)]
    for copy in copies:
        copy.start()
    return copies


def pack_kernel(pos_hbm, spec_hbm, halo_hbm, down_ref, up_ref, pos_ref, spec_ref, halo_ref, sems):
    pairs = ((pos_hbm, pos_ref), (spec_hbm, spec_ref), (halo_hbm, halo_ref))
    for copy in fetch_all(sems, pairs):
        copy.wait()
    frames = spec_ref.shape[0]
    for f in range(frames):
        rows = [pos_ref[c, f : f + 1, :] for c in range(3)]
        rows.append(spec_ref[f : f + 1, :].astype(f32))
        for side, out in ((0, down_ref), (1, up_ref)):
            index = halo_ref[f, side : side + 1, :]
            lane = spread(index & (LANES - 1), 8)
            high = spread(index, 8) >= LANES
            for c, row in enumerate(rows):
                low_g = lane_gather(spread(row[:, :LANES], 8), lane)
                high_g = lane_gather(spread(row[:, LANES:], 8), lane)
                out[4 * f + c : 4 * f + c + 1, :] = jnp.where(high, high_g, low_g)[0:1]


def stage_kernel(
    beta_ref,
    nb_hbm,
    emb_hbm,
    wmsg_hbm,
    wr1_hbm,
    wr2_hbm,
    wup_hbm,
    nb_ref,
    w1_ref,
    w2_ref,
    wup_ref,
    wmsg_ref,
    kind_ref,
    temp_ref,
    emb_in,
    wmsg_in,
    wr1_in,
    wr2_in,
    wup_in,
    sems,
):
    pairs = (
        (nb_hbm, nb_ref),
        (wr1_hbm, wr1_in),
        (wr2_hbm.at[0], wr2_in),
        (wup_hbm.at[0], wup_in),
        (wmsg_hbm, wmsg_in),
        (emb_hbm, emb_in),
    )
    copies = fetch_all(sems, pairs)
    temp_ref[...] = jnp.full((1, LANES), beta_ref[0], f32)
    for copy in copies:
        copy.wait()
    for layer in range(2):
        w1_ref[layer] = rad1_blocks(wr1_in[layer])
    w2_ref[...] = transposed(wr2_in[...])
    wup_ref[...] = transposed(wup_in[...])
    wmsg_ref[...] = transposed(wmsg_in[1])
    emb = emb_in[...]
    table = mm(emb, wmsg_in[0]).astype(bf16).astype(f32)
    for k in range(2):
        kind_ref[k] = column(emb[k : k + 1].astype(f32))
        kind_ref[2 + k] = column(table[k : k + 1])


def basis_rows(dist_ref, f, i, first, atoms):
    center = lax.broadcasted_iota(jnp.int32, (8, atoms), 0).astype(f32)
    parts = []
    for j in range(first, first + GROUP):
        off = spread(dist_ref[f, 3, i, j : j + 1, :], 8) - center
        parts.append(jnp.exp(-(off * off)))
    return jnp.concatenate(parts, axis=0).astype(bf16)


def first_kernel(
    pos_ref,
    spec_ref,
    below_ref,
    above_ref,
    nb_ref,
    halo_ref,
    w1_ref,
    w2_ref,
    wup_ref,
    wmsg_ref,
    kind_ref,
    geo_ref,
    feat_ref,
    msg_ref,
    down_ref,
    up_ref,
    wgt_ref,
    acc_ref,
):
    _, frames, atoms = pos_ref.shape
    batches = nb_ref.shape[1]
    slots = batches * 8
    hidden = w2_ref.shape[1]
    w2s = jnp.concatenate([w2_ref[:LANES, :]] * 2, axis=1)
    w2v = jnp.concatenate([w2_ref[LANES:, :]] * 2, axis=1)
    scale = slots**-0.5
    for f in range(frames):
        for half in range(atoms // LANES):
            cols = slice(half * LANES, (half + 1) * LANES)
            for s in range(batches):
                index = nb_ref[f, s, :, cols]
                lane = index & (LANES - 1)
                block = index >> 7

                def fetch(own_row, halo_row):
                    parts = [
                        own_row[:, :LANES],
                        own_row[:, LANES:],
                        below_ref[halo_row : halo_row + 1, :],
                        above_ref[halo_row : halo_row + 1, :],
                    ]
                    return parts

                squares = None
                offsets = []
                for c in range(3):
                    own_row = pos_ref[c, f : f + 1, :]
                    parts = fetch(own_row, 4 * f + c)
                    if c == 2:
                        parts[2] = parts[2] - slab_depth
                        parts[3] = parts[3] + slab_depth
                    got = [lane_gather(spread(p, 8), lane) for p in parts]
                    there = jnp.where(
                        block == 0,
                        got[0],
                        jnp.where(block == 1, got[1], jnp.where(block == 2, got[2], got[3])),
                    )
                    offset = there - own_row[:, cols]
                    offsets.append(offset)
                    geo_ref[f, c, s, :, cols] = offset
                    squares = offset * offset if squares is None else squares + offset * offset
                geo_ref[f, 3, s, :, cols] = jnp.where(index >= 0, jnp.sqrt(squares), EMPTY)
                parts = fetch(spec_ref[f : f + 1, :].astype(f32), 4 * f + 3)
                got = [lane_gather(spread(p, 8), lane) for p in parts]
                kind = jnp.where(
                    block == 0,
                    got[0],
                    jnp.where(block == 1, got[1], jnp.where(block == 2, got[2], got[3])),
                )
                wgt_ref[0, s, :, cols] = kind
                for c in range(3):
                    wgt_ref[2 * c + 1, s, :, cols] = offsets[c] * (1.0 - kind)
                    wgt_ref[2 * c + 2, s, :, cols] = offsets[c] * kind
        acc_ref[...] = jnp.zeros_like(acc_ref)

        def step(i, carry):
            acts = []
            for first in range(0, 8, GROUP):
                pre = mm(w1_ref[0], basis_rows(geo_ref, f, i, first, atoms))
                acts.append(silu_of_twice(pre).astype(bf16).astype(f32))
            for half in range(atoms // LANES):
                cols = slice(half * LANES, (half + 1) * LANES)
                for part in range(0, hidden, 32):
                    hid = []
                    for j in range(8):
                        at = (j % GROUP) * hidden + part
                        hid.append(acts[j // GROUP][at : at + 32, cols])
                    total = hid[0]
                    for j in range(1, 8):
                        total = total + hid[j]
                    acc_ref[0, part : part + 32, cols] += total
                    for k in range(7):
                        total = acc_ref[k + 1, part : part + 32, cols]
                        for j in range(8):
                            total = total + wgt_ref[k, i, j : j + 1, cols] * hid[j]
                        acc_ref[k + 1, part : part + 32, cols] = total
            return carry

        lax.fori_loop(0, batches, step, 0, unroll=UN1)

        acc_ref[0] = acc_ref[0] - acc_ref[1]

        def project(k, w):
            total = acc_ref[k]
            high = total.astype(bf16)
            low = (total - high.astype(f32)).astype(bf16)
            return mm(w, jnp.concatenate([high, low], axis=0))

        cols0 = jnp.concatenate([kind_ref[2]] * 2, axis=1)
        cols1 = jnp.concatenate([kind_ref[3]] * 2, axis=1)
        scalar = scale * (cols0 * project(0, w2s) + cols1 * project(1, w2s))
        squared = None
        for c in range(3):
            vec = (scale * vector_scale) * (
                cols0 * project(2 * c + 2, w2v) + cols1 * project(2 * c + 3, w2v)
            )
            squared = vec * vec if squared is None else squared + vec * vec
        mixed = jnp.concatenate([scalar, squared], axis=0).astype(bf16)
        update = mm(wup_ref[...], mixed)
        e0 = jnp.concatenate([kind_ref[0]] * 2, axis=1)
        e1 = jnp.concatenate([kind_ref[1]] * 2, axis=1)
        features = jnp.where(spec_ref[f : f + 1, :] == 1, e1, e0) + silu(update)
        feat_ref[f] = features
        message = mm(wmsg_ref[...], features.astype(bf16)).astype(bf16)
        msg_ref[f] = message
        for side, out in ((0, down_ref), (1, up_ref)):
            index = spread(halo_ref[f, side : side + 1, :], LANES)
            lane = (index & (LANES - 1)).astype(jnp.int16)
            high = (index >> 7).astype(jnp.int16) > 0
            low_g = lane_gather(message[:, :LANES], lane)
            high_g = lane_gather(message[:, LANES:], lane)
            out[f] = jnp.where(high, high_g, low_g)


def hidden_kernel(
    slab_ref,
    geo_ref,
    w1_ref,
    temp_ref,
    pos_ref,
    spec_ref,
    target_hbm,
    uref_hbm,
    eshift_hbm,
    count_hbm,
    q_hbm,
    wr2_hbm,
    wup_hbm,
    wout_hbm,
    out_ref,
    w2_ref,
    wup_ref,
    wout_ref,
    struct_ref,
    live_ref,
    scalar_ref,
    target_ref,
    uref_in,
    eshift_in,
    count_in,
    q_in,
    wr2_in,
    wup_in,
    wout_in,
    sems,
):
    pairs = (
        (target_hbm, target_ref),
        (uref_hbm, uref_in),
        (eshift_hbm, eshift_in),
        (count_hbm, count_in),
        (q_hbm, q_in),
        (wr2_hbm.at[1], wr2_in),
        (wup_hbm.at[1], wup_in),
        (wout_hbm, wout_in),
    )
    copies = fetch_all(sems, pairs)
    _, frames, atoms = pos_ref.shape
    batches = geo_ref.shape[2]
    hidden = wr2_in.shape[0]
    for f in range(frames):

        def step(i, carry):
            for first in range(0, 8, GROUP):
                act = silu_of_twice(mm(w1_ref[1], basis_rows(geo_ref, f, i, first, atoms)))
                out_ref[f, i, first * hidden : (first + GROUP) * hidden, :] = act.astype(bf16)
            return carry

        lax.fori_loop(0, batches, step, 0, unroll=UNH)
    for copy in copies:
        copy.wait()
    number_q = q_in.shape[1]
    same = lax.broadcasted_iota(jnp.int32, (number_q, number_q), 0) == lax.broadcasted_iota(
        jnp.int32, (number_q, number_q), 1
    )
    q = [
        jnp.sum(jnp.where(same, spread(q_in[c : c + 1, :], number_q), 0.0), axis=1, keepdims=True)
        for c in range(3)
    ]
    lift = slab_ref[0].astype(f32) * slab_depth
    number = lax.broadcasted_iota(jnp.int32, (1, atoms), 1)
    struct_ref[...] = jnp.zeros_like(struct_ref)
    for f in range(frames):
        x, y, z = (pos_ref[c, f : f + 1, :] for c in range(3))
        phases = q[0] * x + q[1] * y + q[2] * (z + lift)
        lengths = jnp.where(spec_ref[f : f + 1, :] == 1, 1.0, hydrogen_length)
        living = (number < count_in[:, f : f + 1]).astype(f32)
        live_ref[f : f + 1, :] = living
        lengths = living * lengths
        cos_part = jnp.sum(lengths * jnp.cos(phases), axis=1, keepdims=True)
        sin_part = jnp.sum(lengths * jnp.sin(phases), axis=1, keepdims=True)
        struct_ref[2 + f : 3 + f, :] = as_row(cos_part)
        struct_ref[4 + f : 5 + f, :] = as_row(sin_part)
    w2_ref[...] = transposed(wr2_in[...])
    wup_ref[...] = transposed(wup_in[...])
    wout_ref[...] = column(wout_in[...])
    for k in range(2):
        scalar_ref[k : k + 1, :] = jnp.broadcast_to(uref_in[:, k : k + 1], (1, LANES))
        scalar_ref[2 + k : 3 + k, :] = temp_ref[...]
        scalar_ref[4 + k : 5 + k, :] = jnp.broadcast_to(eshift_in[:, k : k + 1], (1, LANES))
    scalar_ref[6:8, :] = jnp.zeros((2, LANES), f32)


def second_kernel(
    rows_each,
    live_ref,
    spec_ref,
    scalar_ref,
    nb_ref,
    geo_ref,
    hid_ref,
    feat_ref,
    msg_ref,
    above_ref,
    below_ref,
    w2_ref,
    wup_ref,
    wout_ref,
    struct_ref,
    energy_ref,
    chunk_ref,
    acc_ref,
    pair_ref,
):
    frames, batches, _, atoms = nb_ref.shape
    slots = batches * 8
    hidden = w2_ref.shape[1]
    chunks = chunk_ref.shape[0]
    wout = jnp.concatenate([wout_ref[...]] * 2, axis=1)
    shift = [jnp.concatenate([scalar_ref[4 + k : 5 + k, :]] * 2, axis=1) for k in range(2)]
    scale = slots**-0.5
    extra = [None] * EXTRA
    for f in range(frames):
        halo = jnp.concatenate([below_ref[f], above_ref[f]], axis=1)
        pair_ref[...] = jnp.concatenate([msg_ref[f], halo], axis=0)
        acc_ref[...] = jnp.zeros_like(acc_ref)

        def step(i, carry):
            target = lax.broadcasted_iota(jnp.int32, (2 * LANES, atoms), 0).astype(bf16)
            filters, found = [], []
            for j in range(8):
                want = (nb_ref[f, i, j : j + 1, :] & (2 * LANES - 1)).astype(f32).astype(bf16)
                hot = jnp.where(target == want, jnp.asarray(1, bf16), jnp.asarray(0, bf16))
                found.append(mm(pair_ref[...], hot))
                filters.append(mm(w2_ref[...], hid_ref[f, i, j * hidden : (j + 1) * hidden, :]))
            for half in range(atoms // LANES):
                cols = slice(half * LANES, (half + 1) * LANES)
                own = [spread(nb_ref[f, i, j : j + 1, cols], WIDTH) < 2 * LANES for j in range(8)]
                offset = [[geo_ref[f, c, i, j : j + 1, cols] for c in range(3)] for j in range(8)]
                for part in range(0, LANES, WIDTH):
                    rows = slice(part, part + WIDTH)
                    lower = slice(LANES + part, LANES + part + WIDTH)
                    total = [acc_ref[k, rows, cols] for k in range(4)]
                    for j in range(8):
                        there = jnp.where(own[j], found[j][rows, cols], found[j][lower, cols])
                        total[0] = total[0] + filters[j][rows, cols] * there
                        vec = filters[j][lower, cols] * there
                        for c in range(3):
                            total[c + 1] = total[c + 1] + offset[j][c] * vec
                    for k in range(4):
                        acc_ref[k, rows, cols] = total[k]
            return carry

        lax.fori_loop(0, batches, step, 0, unroll=UN2)

        scalar = scale * acc_ref[0]
        squared = None
        for c in range(3):
            vec = (scale * vector_scale) * acc_ref[c + 1]
            squared = vec * vec if squared is None else squared + vec * vec
        mixed = jnp.concatenate([scalar, squared], axis=0).astype(bf16)
        update = mm(wup_ref[...], mixed)
        gate = sigmoid(update)
        features = feat_ref[f] + update * gate
        living = live_ref[f : f + 1, :]
        slope = (living * wout * (gate * (1.0 + update * (1.0 - gate)))).astype(bf16)
        kind = spec_ref[f : f + 1, :]
        readout = jnp.sum(features * wout, axis=0, keepdims=True)
        energy = living * (readout + jnp.where(kind == 1, shift[1], shift[0]))
        energy_ref[f : f + 1, :] = energy
        grad = lax.dot_general(mixed, slope, (((1,), (1,)), ((), ())), preferred_element_type=f32)
        chunk_ref[:, f * rows_each : (f + 1) * rows_each, :] = grad.reshape(
            chunks, rows_each, LANES
        )
        extra[f] = as_row(jnp.sum(living * features, axis=1, keepdims=True))
        extra[2 + f] = struct_ref[2 + f : 3 + f, :]
        extra[4 + f] = struct_ref[4 + f : 5 + f, :]
        extra[6 + f] = jnp.broadcast_to(jnp.sum(energy, axis=1, keepdims=True), (1, LANES))
    block = jnp.concatenate(extra, axis=0)
    chunk_ref[:, frames * rows_each :, :] = jnp.broadcast_to(block[None], (chunks, EXTRA, LANES))


def total_kernel(scalar_ref, in_ref, out_ref):
    rows = in_ref.shape[1]
    total = in_ref[0]
    for s in range(1, in_ref.shape[0]):
        total = total + in_ref[s]
    for d in range(out_ref.shape[0]):
        out_ref[d] = total
    for f in range(2):
        row = total[rows - 2 + f : rows - 1 + f]
        log_weight = -scalar_ref[2 + f : 3 + f, :] * (row - scalar_ref[f : f + 1, :])
        for d in range(out_ref.shape[0]):
            out_ref[d, rows - 2 + f : rows - 1 + f, :] = log_weight


def final_kernel(
    rows_each,
    atoms_all,
    scalar_ref,
    in_ref,
    target_ref,
    chunk_ref,
    mean_ref,
    out_ref,
):
    devices = in_ref.shape[0]
    q = target_ref.shape[1]
    base = 2 * rows_each

    def gather(at):
        return jnp.concatenate([in_ref[d, base + at : base + at + 2, :] for d in range(devices)], 0)

    cos_tot, sin_tot, log_weight = gather(2), gather(4), gather(6)
    structure = ((cos_tot * cos_tot + sin_tot * sin_tot) / atoms_all)[:, :q]
    scaled = jnp.exp(log_weight - jnp.max(log_weight, axis=0, keepdims=True))
    weights = scaled / jnp.sum(scaled, axis=0, keepdims=True)
    mean = jnp.sum(weights[:, :q] * structure, axis=0, keepdims=True)
    slope_sq = (mean - target_ref[...]) / target_var
    observed = jnp.sum(structure * slope_sq, axis=1, keepdims=True)
    average = jnp.sum(mean * slope_sq, axis=1, keepdims=True)
    factor = -scalar_ref[2:3, :] * weights * (observed - average)
    mean_ref[...] = mean
    out_ref[...] = jnp.sum(factor * gather(0), axis=0, keepdims=True)
    grad = jnp.zeros((rows_each, LANES), f32)
    for d in range(devices):
        for f in range(2):
            k = 2 * d + f
            grad = grad + factor[k : k + 1] * in_ref[d, f * rows_each : (f + 1) * rows_each, :]
    for s in range(chunk_ref.shape[0]):
        chunk_ref[s] = grad


VM = pl.BlockSpec(memory_space=pltpu.VMEM)
SM = pl.BlockSpec(memory_space=pltpu.SMEM)
HB = pl.BlockSpec(memory_space=pltpu.HBM)


def call(kernel, name, ins, outs, scratch, *operands):
    return pl.pallas_call(
        kernel,
        name=name,
        out_shape=outs,
        in_specs=ins,
        out_specs=jax.tree.map(lambda _: VM, outs),
        scratch_shapes=scratch,
        compiler_params=pltpu.CompilerParams(vmem_limit_bytes=VMEM_BYTES),
    )(*operands)


def in_hbm(value):
    return pltpu.with_memory_space_constraint(value, pltpu.HBM)


def array(shape, dtype=f32):
    return jax.ShapeDtypeStruct(shape, dtype)


def per_device(
    positions,
    species,
    atom_count,
    halo_index,
    neighbours,
    embedding,
    w_msg,
    w_rad1,
    w_rad2,
    w_up,
    w_out,
    e_shift,
    u_reference,
    inverse_temp,
    q_vectors,
    s_target,
):
    frames, _, atoms = positions.shape
    slots = neighbours.shape[1]
    halo = halo_index.shape[2]
    hidden = w_rad1.shape[2]
    channels = w_msg.shape[1]
    neighbours = neighbours.reshape(frames, slots // 8, 8, atoms)
    positions = positions.transpose(1, 0, 2)
    slab_devs = lax.axis_size("slab")
    frame_devs = lax.axis_size("frame")
    rows_each = 2 * channels // slab_devs
    chunk_rows = frames * rows_each + EXTRA
    up = [(i, (i + 1) % slab_devs) for i in range(slab_devs)]
    down = [(j, i) for i, j in up]

    basis = w_rad1.shape[1]
    rows = array((4 * frames, halo))
    leave_down, leave_up, positions, species, halo_index = call(
        pack_kernel,
        "halo_rows",
        [HB] * 3,
        (
            rows,
            rows,
            array(positions.shape),
            array(species.shape, jnp.int32),
            array(halo_index.shape, jnp.int32),
        ),
        [pltpu.SemaphoreType.DMA((3,))],
        *map(in_hbm, (positions, species, halo_index)),
    )
    below = lax.ppermute(leave_up, "slab", up)
    above = lax.ppermute(leave_down, "slab", down)
    q = s_target.shape[0]
    staged = (embedding, w_msg, w_rad1)
    halves = (array(w_rad2.shape[1:], bf16), array(w_up.shape[1:], bf16))
    neighbours, w1, w2, wup, wmsg, kinds, temp = call(
        stage_kernel,
        "staged_inputs",
        [SM] + [HB] * 6,
        (
            array(neighbours.shape, jnp.int32),
            array((2, GROUP * hidden, GROUP * basis), bf16),
            array((2 * channels, hidden), bf16),
            array((channels, 2 * channels), bf16),
            array((channels, channels), bf16),
            array((4, channels, LANES)),
            array((1, LANES)),
        ),
        [pltpu.VMEM(w.shape, w.dtype) for w in (*staged, *halves)]
        + [pltpu.SemaphoreType.DMA((6,))],
        inverse_temp,
        *map(in_hbm, (neighbours, *staged, w_rad2, w_up)),
    )
    halo_rows = array((frames, channels, halo), bf16)
    geometry, features, message, msg_down, msg_up = call(
        first_kernel,
        "first_layer",
        [VM] * 11,
        (
            array((frames, 4, slots // 8, 8, atoms)),
            array((frames, channels, atoms)),
            array((frames, channels, atoms), bf16),
            halo_rows,
            halo_rows,
        ),
        [pltpu.VMEM((7, slots // 8, 8, atoms), f32), pltpu.VMEM((8, hidden, atoms), f32)],
        positions,
        species,
        below,
        above,
        neighbours,
        halo_index,
        w1,
        w2,
        wup,
        wmsg,
        kinds,
    )
    msg_above = lax.ppermute(msg_down, "slab", down)
    msg_below = lax.ppermute(msg_up, "slab", up)
    small = (
        u_reference.reshape(1, frames),
        e_shift.reshape(1, 2),
        atom_count.reshape(1, frames),
        q_vectors,
    )
    wout_row = w_out.reshape(1, channels)
    radial_hidden, w2, wup, wout, structure, living, scalars, target = call(
        hidden_kernel,
        "radial_hidden",
        [SM] + [VM] * 5 + [HB] * 8,
        (
            array((frames, slots // 8, 8 * hidden, atoms), bf16),
            array((2 * channels, hidden), bf16),
            array((channels, 2 * channels), bf16),
            array((channels, LANES)),
            array((EXTRA, LANES)),
            array((frames, atoms)),
            array((8, LANES)),
            array((1, q)),
        ),
        [pltpu.VMEM(w.shape, w.dtype) for w in (*small, *halves, wout_row)]
        + [pltpu.SemaphoreType.DMA((8,))],
        lax.axis_index("slab").reshape(1),
        geometry,
        w1,
        temp,
        positions,
        species,
        *map(in_hbm, (s_target.reshape(1, q), *small, w_rad2, w_up, wout_row)),
    )
    atom_energy, chunks = call(
        functools.partial(second_kernel, rows_each),
        "second_layer",
        [VM] * 14,
        (array((frames, atoms)), array((slab_devs, chunk_rows, LANES))),
        [
            pltpu.VMEM((4, channels, atoms), f32),
            pltpu.VMEM((2 * channels, 2 * LANES), bf16),
        ],
        living,
        species,
        scalars,
        neighbours,
        geometry,
        radial_hidden,
        features,
        message,
        msg_above,
        msg_below,
        w2,
        wup,
        wout,
        structure,
    )
    chunks = lax.all_to_all(chunks, "slab", 0, 0, tiled=True)
    totals = call(
        total_kernel,
        "slab_totals",
        [VM, VM],
        array((frame_devs, chunk_rows, LANES)),
        [],
        scalars,
        chunks,
    )
    totals = lax.all_to_all(totals, "frame", 0, 0, tiled=True)
    grad_rows, mean_structure, grad_out = call(
        functools.partial(final_kernel, rows_each, atoms * slab_devs),
        "reweighted",
        [VM] * 3,
        (array((slab_devs, rows_each, LANES)), array((1, q)), array((1, channels))),
        [],
        scalars,
        totals,
        target,
    )
    grad_up = lax.all_to_all(grad_rows, "slab", 0, 0, tiled=True)
    return (
        atom_energy,
        mean_structure.reshape(q),
        grad_up.reshape(2 * channels, channels),
        grad_out.reshape(channels),
    )


def solution(mesh):
    in_specs = (
        P("frame", None, "slab"),
        P("frame", "slab"),
        P("frame", "slab"),
        P("frame", None, "slab"),
        P("frame", None, "slab"),
        P(),
        P(),
        P(),
        P(),
        P(),
        P(),
        P(),
        P("frame"),
        P(),
        P(),
        P(),
    )
    out_specs = (P("frame", "slab"), P(), P(), P())
    return jax.shard_map(
        per_device, mesh=mesh, in_specs=in_specs, out_specs=out_specs, check_vma=False
    )
```
